32 devices in a mesh: dp: 8 (over z, y), expert: 4 (over x, core).
Axes of the slice: x: 2, y: 2, z: 4, core: 2. Of those that a mesh axis runs over, the one named last changes fastest.
Arguments:
- tokens: bfloat16 [1024, 4096], P('dp', 'expert'), may hold values from -24 to 24
- expert_ids: int32 [1024, 8], P('dp'), may hold values from 0 to 63, all different within a row; in each aligned block of 128 rows (0 to 127, 128 to 255, ...) at most 20 rows name the same one
- route_weights: float32 [1024, 8], P('dp'), may hold values from 0.05 to 1
- gate_weight: bfloat16 [64, 1536, 4096], P('dp', 'expert'), may hold values from -0.09375 to 0.09375
- up_weight: bfloat16 [64, 1536, 4096], P('dp', 'expert'), may hold values from -0.09375 to 0.09375
- down_weight: bfloat16 [64, 1536, 4096], P('dp', None, 'expert'), may hold values from -0.15625 to 0.15625
Outputs:
- quant_out: bfloat16 [1024, 4096], P('dp', 'expert')
- float_out: float32 [1024, 4096], P('dp', 'expert')
The draws below stay inside these ranges and needn't reach their ends.
Inputs may be any that keep to these rules, and one draw needn't show every extreme that they name: `expert_ids`: each row names 8 different experts; every expert is named by some row; within the 128 rows of one index of dp no expert is named more than 20 times, and in every draw some expert is named exactly 20 times in some such block.
All inputs are finite; a program needn't handle non-finite values. Where the reference program divides by a largest or mean magnitude, that divisor is 1e-20 or more.
Results may differ from the reference program's by a relative error of at most 0.011.
Values may be sent and summed in bfloat16 or wider, within the bound.
No kernel may reach another device: no remote copies, remote signals or barrier semaphores. Data moves between devices by JAX's collectives and lax.ppermute only.
A program may use at most 192 MiB of HBM per device.

```python
import math
from functools import partial
import jax
import jax.numpy as jnp
import numpy as np
from jax import lax

D = 4096
FF = 1536
TOPK = 8
EXPERTS = 64
TOK_DEV = 128
CAP = 20
TOKENS = 1024
N_DP = 8


def draw_tokens(key, part):
    key_scale, key_body = jax.random.split(jax.random.fold_in(key, 17), 2)
    channel_scale = jnp.exp(jax.random.uniform(key_scale, (1, D), jnp.float32, math.log(0.05), math.log(4.0)))
    values = jnp.clip(jax.random.normal(key_body, (TOKENS, D), jnp.float32), -6.0, 6.0) * channel_scale
    return values.astype(jnp.bfloat16)


def block_scale(rng, shape, pieces, smallest, largest):
    factor_of, own = 1.0, jax.random.fold_in(rng, 6)
    for dim, shards_of in pieces:
        steps = jnp.exp(jax.random.uniform(jax.random.fold_in(own, dim), (shards_of,), jnp.float32, smallest / len(pieces), largest / len(pieces)))
        factor_of = factor_of * jnp.repeat(steps, shape[dim] // shards_of).reshape([-1 if axis == dim else 1 for axis in range(len(shape))])
    return factor_of


def shared_out(stream_key, own, number, rows, amount, top, most, slope):
    ranking = jax.random.permutation(stream_key, amount)
    crowded, ordinary = portions_of(amount, rows * top, most, slope, True), portions_of(amount, rows * top, most, slope, False)
    places = jnp.arange(amount)

    def named(lengths, turn):
        used = int((lengths > 0).sum())
        fixed = max(1, used // 4)
        passed = fixed + (places - fixed + turn * (used - fixed)) % max(1, amount - fixed)
        return jnp.zeros((amount,), jnp.int32).at[ranking[jnp.where(places < fixed, places, passed)]].set(jnp.asarray(lengths, jnp.int32))

    lengths = jnp.where(number % 4 == 0, named(crowded, number // 4), named(ordinary, number - number // 4 - 1))
    mixed = jax.random.permutation(jax.random.fold_in(own, 3), amount)
    source_of, sink = mixed[0:amount // 2 * 2:2], mixed[1:amount // 2 * 2:2]
    room = jnp.minimum(lengths[source_of] - 1, most - lengths[sink]) // 2
    room = jnp.where((source_of == ranking[0]) | (sink == ranking[0]) | (lengths[sink] == 0), 0, jnp.maximum(room, 0))
    passed = jax.random.randint(jax.random.fold_in(own, 4), (amount // 2,), 0, 1 << 20) % (room + 1)
    lengths = lengths.at[source_of].add(-passed).at[sink].add(passed)
    labels = jnp.searchsorted(jnp.cumsum(lengths), jnp.arange(rows * top), side="right").astype(jnp.int32)
    grid = labels.reshape(top, rows).T
    grid = grid[jax.random.permutation(jax.random.fold_in(own, 1), rows)]
    turn = jax.random.randint(jax.random.fold_in(own, 2), (rows, 1), 0, top)
    return jnp.take_along_axis(grid, (jnp.arange(top)[None, :] + turn) % top, axis=1)


def portions_of(number_of, total, most, slope, full):
    portions = [(1 << 20) // math.isqrt(rank ** slope) + 1 for rank in range(1, number_of + 1)]
    largest = most if full else min(most, max(-(-total // number_of), total * portions[0] // sum(portions)))
    least = 1 if total - largest >= number_of - 1 else 0
    counts, surplus = [largest] + [least] * (number_of - 1), total - largest - least * (number_of - 1)
    while surplus > 0:
        movable = [i for i in range(1, number_of) if counts[i] < largest] or [i for i in range(1, number_of) if counts[i] < most]
        mass, remaining = sum([portions[i] for i in movable]), surplus
        for i in movable:
            addition = min(most - counts[i], max(1, remaining * portions[i] // mass), surplus)
            counts[i] = counts[i] + addition
            surplus = surplus - addition
    return np.array(counts)


def centred(stream_key, extent, spread, bound, cuts=(), kind=jnp.bfloat16):
    array = spread * jax.random.normal(stream_key, extent, jnp.float32)
    if cuts:
        array = array * block_scale(stream_key, extent, cuts, -0.22, 0.18)
    return jnp.clip(array, -bound, bound).astype(kind)


def setup_inputs(seed: int = 0) -> dict:
    streams_of = jax.random.split(jax.random.key(seed), 7)
    tokens = draw_tokens(jax.random.fold_in(streams_of[6], 71), 0)
    expert_ids_keys = jax.random.split(jax.random.fold_in(streams_of[1], 1), TOKENS // TOK_DEV)
    expert_ids_turns = jax.random.permutation(jax.random.fold_in(streams_of[1], 3), TOKENS // TOK_DEV)
    expert_ids = jax.vmap(lambda own, number: shared_out(jax.random.fold_in(streams_of[1], 2), own, number, TOK_DEV, EXPERTS, TOPK, CAP, 2))(expert_ids_keys, expert_ids_turns).reshape((TOKENS, TOPK))
    route_weights = jnp.clip(jnp.exp(math.log(1.0) - 2.9957323 * jax.random.uniform(streams_of[2], (TOKENS, TOPK), jnp.float32) ** block_scale(streams_of[2], (TOKENS, TOPK), ((0, 8),), -0.2, 0.2)), 0.05, 1.0)
    gate_weight = centred(streams_of[3], (EXPERTS, FF, D), D ** -0.5, 0.09375, ((0, 8), (1, 4)))
    up_weight = centred(streams_of[4], (EXPERTS, FF, D), D ** -0.5, 0.09375, ((0, 8), (1, 4)))
    down_weight = centred(streams_of[5], (EXPERTS, FF, D), FF ** -0.5, 0.15625, ((0, 8), (2, 4)))
    return dict(tokens=tokens, expert_ids=expert_ids, route_weights=route_weights, gate_weight=gate_weight, up_weight=up_weight, down_weight=down_weight)


TWO_PI = 6.283185307179586

def soft_level(values):
    return values - jnp.sin(TWO_PI * values) / TWO_PI

def fake_quant(values, reduce_axis, levels):
    peak_abs = lax.optimization_barrier(jnp.max(jnp.abs(values), axis=reduce_axis, keepdims=True)) + 1e-06
    return peak_abs / levels * soft_level(levels * values / peak_abs)

def slot_layout(expert_ids):
    source_ids = expert_ids.reshape(N_DP, TOK_DEV * TOPK)
    hit_mask = (source_ids[:, :, None] == jnp.arange(EXPERTS, dtype=jnp.int32)[None, None, :]).astype(jnp.int32)
    before = jnp.cumsum(hit_mask, axis=1) - hit_mask
    slot_index = lax.optimization_barrier(jnp.sum(before * hit_mask, axis=2)).astype(jnp.int32)
    source = jnp.arange(N_DP, dtype=jnp.int32)[:, None]
    position = source * (TOK_DEV * TOPK) + jnp.arange(TOK_DEV * TOPK, dtype=jnp.int32)[None, :]
    token_index = (position // TOPK).astype(jnp.int32)
    target = (source_ids * (N_DP * CAP) + source * CAP + slot_index).astype(jnp.int32)
    slot_table = jnp.full((EXPERTS * N_DP * CAP,), -1, jnp.int32).at[target.reshape(-1)].set(token_index.reshape(-1))
    return (target.reshape(TOKENS, TOPK), slot_table.reshape(EXPERTS, N_DP * CAP))

def expert_pass(tokens, operands):
    token_index, w_gate, w_up, w_down = operands
    present = token_index >= 0
    picked = jnp.take(tokens, jnp.maximum(token_index, 0), axis=0)
    rows = jnp.where(present[:, None], picked, jnp.zeros_like(picked))
    gate_float = jnp.dot(rows, w_gate.T, preferred_element_type=jnp.float32)
    up_float = jnp.dot(rows, w_up.T, preferred_element_type=jnp.float32)
    hidden_float = (jax.nn.silu(gate_float) * up_float).astype(jnp.bfloat16)
    out_float = jnp.dot(hidden_float, w_down, preferred_element_type=jnp.float32).astype(jnp.bfloat16)
    rows_wide = rows.astype(jnp.float32)
    act_peak = jnp.maximum(lax.optimization_barrier(jnp.max(jnp.abs(rows_wide), axis=0)), 1.0)
    weight_peak = jnp.maximum(lax.optimization_barrier(jnp.max(jnp.abs(w_gate.astype(jnp.float32)), axis=0)), lax.optimization_barrier(jnp.max(jnp.abs(w_up.astype(jnp.float32)), axis=0))) + 1e-06
    smooth = jnp.sqrt(act_peak / weight_peak)
    rows_quant = fake_quant(rows_wide / smooth[None, :], 1, 7.0).astype(jnp.bfloat16)
    gate_quant_w = fake_quant(w_gate.astype(jnp.float32) * smooth[None, :], 1, 7.0).astype(jnp.bfloat16)
    up_quant_w = fake_quant(w_up.astype(jnp.float32) * smooth[None, :], 1, 7.0).astype(jnp.bfloat16)
    gate_quant = jnp.dot(rows_quant, gate_quant_w.T, preferred_element_type=jnp.float32)
    up_quant = jnp.dot(rows_quant, up_quant_w.T, preferred_element_type=jnp.float32)
    hidden_quant = (jax.nn.silu(gate_quant) * up_quant).astype(jnp.bfloat16)
    hidden_quant = lax.optimization_barrier(hidden_quant)
    hidden_levels = fake_quant(hidden_quant.astype(jnp.float32), 1, 7.0).astype(jnp.bfloat16)
    down_quant_w = fake_quant(w_down.astype(jnp.float32), 0, 7.0).astype(jnp.bfloat16)
    out_quant = jnp.dot(hidden_levels, down_quant_w, preferred_element_type=jnp.float32).astype(jnp.bfloat16)
    return (out_quant, out_float)

def reference(tokens, expert_ids, route_weights, gate_weight, up_weight, down_weight):
    target, slot_table = slot_layout(expert_ids)
    out_quant, out_float = lax.map(partial(expert_pass, tokens), (slot_table, gate_weight, up_weight, down_weight))
    flat_quant = out_quant.reshape(EXPERTS * N_DP * CAP, D)
    flat_float = out_float.reshape(EXPERTS * N_DP * CAP, D)
    shares = route_weights / lax.optimization_barrier(jnp.sum(route_weights, axis=1, keepdims=True))

    def accumulate(carry, column):
        acc_quant, acc_float = carry
        index_col, share_col = column
        acc_quant = acc_quant + share_col[:, None] * jnp.take(flat_quant, index_col, axis=0).astype(jnp.float32)
        acc_float = acc_float + share_col[:, None] * jnp.take(flat_float, index_col, axis=0).astype(jnp.float32)
        return ((acc_quant, acc_float), None)
    start = (jnp.zeros((TOKENS, D), jnp.float32), jnp.zeros((TOKENS, D), jnp.float32))
    (acc_quant, acc_float), _ = lax.scan(accumulate, start, (target.T, shares.T))
    return (acc_quant.astype(jnp.bfloat16), acc_float)
```

```python
import functools

import jax
import jax.numpy as jnp
from jax import lax
from jax.experimental import pallas as pl
from jax.experimental.pallas import tpu as pltpu
from jax.sharding import PartitionSpec as P

CAP = 20
UNIT = 4
LEVELS = 7.0
EPS = 1e-06
VMEM = 56 * 1024 * 1024
LANES = 128
SLAB = 16

FRACTION_BF16 = (6.55787162, -12.52307356, 9.17209913)
FRACTION_F32 = (6.57971384, -12.98683711, 12.19123288, -6.56909136, 1.9674894)

bf16 = jnp.bfloat16
f32 = jnp.float32


def fraction(r, coefficients):
    dtype = r.dtype
    square = r * r
    total = jnp.asarray(coefficients[-1], dtype)
    for c in coefficients[-2::-1]:
        total = total * square + jnp.asarray(c, dtype)
    return (r * square) * total


def level_bf16(v):
    n = jnp.round(v)
    r = (v - n).astype(bf16)
    return n.astype(bf16) + fraction(r, FRACTION_BF16)


def level_f32(v):
    n = jnp.round(v)
    return n + fraction(v - n, FRACTION_F32)


def fold_max(x):
    if x.shape[1] % LANES:
        return jnp.max(x, axis=1, keepdims=True)
    out = x[:, :LANES]
    for c in range(LANES, x.shape[1], LANES):
        out = jnp.maximum(out, x[:, c : c + LANES])
    return out


def wide(x, width):
    return jnp.concatenate([x] * (width // LANES), axis=1)


def dot_t(a, b):
    return lax.dot_general(a, b, (((1,), (1,)), ((), ())), preferred_element_type=f32)


def params():
    return pltpu.CompilerParams(vmem_limit_bytes=VMEM)


def prep_kernel(local_experts, groups, group_tokens, first_ref, ids_ref, route_ref, hot_ref, share_ref):
    units = groups // UNIT
    unit_rows, unit_tokens = UNIT * CAP, UNIT * group_tokens
    ids = ids_ref[...]
    route = route_ref[...]
    shares = route / jnp.sum(route, axis=0, keepdims=True)
    first = first_ref[0]
    hits, weights = [], []
    for e in range(local_experts):
        hit = ids == first + e
        hits.append(jnp.max(jnp.where(hit, 1.0, 0.0), axis=0, keepdims=True))
        weights.append(jnp.sum(jnp.where(hit, shares, 0.0), axis=0, keepdims=True))
    hit_all = jnp.concatenate(hits, axis=0)
    before = lax.broadcasted_iota(jnp.int32, (group_tokens, group_tokens), 0) < lax.broadcasted_iota(
        jnp.int32, (group_tokens, group_tokens), 1
    )
    before = jnp.where(before, 1.0, 0.0).astype(bf16)
    codes = []
    for g in range(groups):
        part = hit_all[:, g * group_tokens : (g + 1) * group_tokens]
        slot = jnp.dot(part.astype(bf16), before, preferred_element_type=f32)
        codes.append(jnp.where(part > 0.5, slot + float((g % UNIT) * CAP), -1.0))
    row = lax.broadcasted_iota(jnp.int32, (unit_rows, unit_tokens), 0).astype(f32)
    for u in range(units):
        code = jnp.concatenate(codes[u * UNIT : (u + 1) * UNIT], axis=1)
        for e in range(local_experts):
            hot = row == code[e : e + 1, :]
            hot_ref[u, e * unit_rows : (e + 1) * unit_rows, :] = jnp.where(hot, 1.0, 0.0).astype(bf16)
            weight = weights[e][:, u * unit_tokens : (u + 1) * unit_tokens]
            share_ref[e, u * unit_rows : (u + 1) * unit_rows, :] = jnp.sum(
                jnp.where(hot, weight, 0.0), axis=1, keepdims=True
            )


def prep(first, ids_t, route_t, local_experts, groups, group_tokens):
    units = groups // UNIT
    return pl.pallas_call(
        functools.partial(prep_kernel, local_experts, groups, group_tokens),
        out_shape=(
            jax.ShapeDtypeStruct((units, local_experts * UNIT * CAP, UNIT * group_tokens), bf16),
            jax.ShapeDtypeStruct((local_experts, groups * CAP, 1), f32),
        ),
        in_specs=[
            pl.BlockSpec(memory_space=pltpu.SMEM),
            pl.BlockSpec(memory_space=pltpu.VMEM),
            pl.BlockSpec(memory_space=pltpu.VMEM),
        ],
        out_specs=(pl.BlockSpec(memory_space=pltpu.VMEM), pl.BlockSpec(memory_space=pltpu.VMEM)),
        compiler_params=params(),
        name="routing_tables",
    )(first, ids_t, route_t)


def down_quant_kernel(rows, width, down_ref, level_ref, scale_ref):
    step = 8 * SLAB

    def peak(i, carry):
        base = pl.multiple_of(i * step, step)
        for j in range(0, step, SLAB):
            carry = jnp.maximum(carry, jnp.abs(down_ref[0, pl.ds(base + j, SLAB), :]))
        return carry

    top = lax.fori_loop(0, rows // step, peak, jnp.zeros((SLAB, width), bf16))
    top = jnp.max(top.astype(f32), axis=0, keepdims=True) + EPS
    scale_ref[0] = top / LEVELS
    inverse = jnp.broadcast_to(LEVELS / top, (SLAB, width))

    def quantize(i, carry):
        base = pl.multiple_of(i * step, step)
        for j in range(0, step, SLAB):
            value = down_ref[0, pl.ds(base + j, SLAB), :].astype(f32) * inverse
            level_ref[0, pl.ds(base + j, SLAB), :] = level_bf16(value)
        return carry

    lax.fori_loop(0, rows // step, quantize, 0)


def down_quant(down):
    experts, hidden, width = down.shape
    block = 512
    return pl.pallas_call(
        functools.partial(down_quant_kernel, hidden, block),
        grid=(experts, width // block),
        out_shape=(
            jax.ShapeDtypeStruct(down.shape, bf16),
            jax.ShapeDtypeStruct((experts, 1, width), f32),
        ),
        in_specs=[pl.BlockSpec((1, hidden, block), lambda e, c: (e, 0, c))],
        out_specs=(
            pl.BlockSpec((1, hidden, block), lambda e, c: (e, 0, c)),
            pl.BlockSpec((1, 1, block), lambda e, c: (e, 0, c)),
        ),
        compiler_params=params(),
        cost_estimate=pl.CostEstimate(
            flops=down.size * 24, bytes_accessed=down.size * 4, transcendentals=0
        ),
        name="down_levels",
    )(down)


def rows_kernel(local_experts, units, hot_ref, tokens_ref, peak_ref, rows_ref, smooth_ref):
    unit_rows = UNIT * CAP
    group_tokens, width = tokens_ref.shape[2], tokens_ref.shape[3]
    top = [None] * local_experts
    for u in range(units):
        tokens = tokens_ref[u * UNIT : (u + 1) * UNIT, 0].reshape(UNIT * group_tokens, width)
        picked = jnp.dot(hot_ref[u], tokens, preferred_element_type=f32)
        for e in range(local_experts):
            part = picked[e * unit_rows : (e + 1) * unit_rows]
            rows_ref[e, u * unit_rows : (u + 1) * unit_rows, :] = part.astype(bf16)
            most = jnp.max(jnp.abs(part), axis=0, keepdims=True)
            top[e] = most if top[e] is None else jnp.maximum(top[e], most)
    for e in range(local_experts):
        smooth_ref[e] = jnp.sqrt(jnp.maximum(top[e], 1.0) / (peak_ref[e : e + 1, :] + EPS))


def expert_rows(hot, tokens, weight_peak, local_experts, groups):
    shards, group_tokens, share = tokens.shape[1:]
    units = groups // UNIT
    block = 512
    per = share // block
    return pl.pallas_call(
        functools.partial(rows_kernel, local_experts, units),
        grid=(shards * per,),
        out_shape=(
            jax.ShapeDtypeStruct((local_experts, groups * CAP, shards * share), bf16),
            jax.ShapeDtypeStruct((local_experts, 1, shards * share), f32),
        ),
        in_specs=[
            pl.BlockSpec(hot.shape, lambda c: (0, 0, 0)),
            pl.BlockSpec((groups, 1, group_tokens, block), lambda c: (0, c // per, 0, c % per)),
            pl.BlockSpec((local_experts, block), lambda c: (0, c)),
        ],
        out_specs=(
            pl.BlockSpec((local_experts, groups * CAP, block), lambda c: (0, 0, c)),
            pl.BlockSpec((local_experts, 1, block), lambda c: (0, 0, c)),
        ),
        compiler_params=params(),
        name="expert_rows",
    )(hot, tokens, weight_peak)


CHUNK = 512


def hidden_kernel(
    rows_ref, gate_ref, up_ref, smooth_ref, float_ref, quant_ref,
    smooth_s, unsmooth_s, top_s, top_r, inverse_s, inverse_r, scale_r, scale_w, acc, levels, row_levels,
):
    count = rows_ref.shape[1]
    hidden = gate_ref.shape[1]
    depth = gate_ref.shape[2]
    chunks = depth // CHUNK
    weights = ((gate_ref, 0), (up_ref, hidden))

    smooth = smooth_ref[0]
    smooth_s[...] = jnp.broadcast_to(smooth, smooth_s.shape)
    unsmooth_s[...] = jnp.broadcast_to(1.0 / smooth, unsmooth_s.shape)
    top_s[...] = jnp.zeros_like(top_s)
    top_r[...] = jnp.zeros_like(top_r)
    acc[...] = jnp.zeros_like(acc)

    def peaks(i, carry):
        cols = pl.ds(pl.multiple_of(i * CHUNK, CHUNK), CHUNK)
        smooth_c = smooth_s[:, cols]
        unsmooth_c = unsmooth_s[:, cols]
        rows = rows_ref[0, :, cols]
        for ref, base in weights:
            acc[:, base : base + hidden] += dot_t(rows, ref[0, :, cols])
            for f in range(0, hidden, SLAB):
                value = jnp.abs(ref[0, f : f + SLAB, cols]).astype(f32) * smooth_c
                spot = slice(base + f, base + f + SLAB)
                top_s[spot, :] = jnp.maximum(top_s[spot, :], fold_max(value))
        for r in range(0, count, SLAB):
            value = jnp.abs(rows_ref[0, r : r + SLAB, cols]).astype(f32) * unsmooth_c
            top_r[r : r + SLAB, :] = jnp.maximum(top_r[r : r + SLAB, :], fold_max(value))
        return carry

    lax.fori_loop(0, chunks, peaks, 0)

    gate, up = acc[:, :hidden], acc[:, hidden:]
    float_ref[0] = (gate / (1.0 + jnp.exp(-gate)) * up).astype(bf16)

    for r in range(0, count, SLAB):
        top = jnp.max(top_r[r : r + SLAB, :], axis=1, keepdims=True) + EPS
        inverse_r[r : r + SLAB, :] = jnp.broadcast_to(LEVELS / top, (SLAB, LANES))
        scale_r[r : r + SLAB, :] = jnp.broadcast_to(top / LEVELS, (SLAB, LANES))
    eye = lax.broadcasted_iota(jnp.int32, (LANES, LANES), 0) == lax.broadcasted_iota(
        jnp.int32, (LANES, LANES), 1
    )
    for f in range(0, 2 * hidden, LANES):
        top = jnp.max(top_s[f : f + LANES, :], axis=1, keepdims=True) + EPS
        inverse_s[f : f + LANES, :] = jnp.broadcast_to(LEVELS / top, (LANES, LANES))
        scale_w[:, f : f + LANES] = jnp.sum(jnp.where(eye, top / LEVELS, 0.0), axis=0, keepdims=True)
    acc[...] = jnp.zeros_like(acc)

    def quantize(i, slot):
        cols = pl.ds(pl.multiple_of(i * CHUNK, CHUNK), CHUNK)
        smooth_c = smooth_s[:, cols]
        unsmooth_c = unsmooth_s[:, cols]
        for r in range(0, count, SLAB):
            value = rows_ref[0, r : r + SLAB, cols].astype(f32) * unsmooth_c
            value = value * wide(inverse_r[r : r + SLAB, :], CHUNK)
            level = level_f32(value) * wide(scale_r[r : r + SLAB, :], CHUNK)
            row_levels[slot, r : r + SLAB, :] = level.astype(bf16)
        for ref, base in weights:
            for f in range(0, hidden, SLAB):
                value = ref[0, f : f + SLAB, cols].astype(f32) * smooth_c
                value = value * wide(inverse_s[base + f : base + f + SLAB, :], CHUNK)
                levels[slot, base + f : base + f + SLAB, :] = level_bf16(value)

    def multiply(slot):
        acc[...] += dot_t(row_levels[slot], levels[slot])

    quantize(0, 0)

    def pair(i, carry):
        multiply(0)
        quantize(2 * i + 1, 1)
        multiply(1)
        quantize(2 * i + 2, 0)
        return carry

    lax.fori_loop(0, chunks // 2 - 1, pair, 0)
    multiply(0)
    quantize(chunks - 1, 1)
    multiply(1)

    scaled = acc[...] * scale_w[...]
    gate, up = scaled[:, :hidden], scaled[:, hidden:]
    quant_ref[0] = (gate / (1.0 + jnp.exp(-gate)) * up).astype(bf16)


def hidden_units(rows, gate, up, smooth, first, amount):
    count, depth = rows.shape[1:]
    hidden = gate.shape[1]

    def spec(*tail):
        return pl.BlockSpec((1,) + tail, lambda e: (first + e,) + (0,) * len(tail))

    out = jax.ShapeDtypeStruct((amount, count, hidden), bf16)
    out_spec = pl.BlockSpec((1, count, hidden), lambda e: (e, 0, 0))
    flops = 2 * 2 * amount * count * depth * 2 * hidden
    return pl.pallas_call(
        hidden_kernel,
        grid=(amount,),
        out_shape=(out, out),
        in_specs=[spec(count, depth), spec(hidden, depth), spec(hidden, depth), spec(1, depth)],
        out_specs=(out_spec, out_spec),
        scratch_shapes=[
            pltpu.VMEM((SLAB, depth), f32),
            pltpu.VMEM((SLAB, depth), f32),
            pltpu.VMEM((2 * hidden, LANES), f32),
            pltpu.VMEM((count, LANES), f32),
            pltpu.VMEM((2 * hidden, LANES), f32),
            pltpu.VMEM((count, LANES), f32),
            pltpu.VMEM((count, LANES), f32),
            pltpu.VMEM((1, 2 * hidden), f32),
            pltpu.VMEM((count, 2 * hidden), f32),
            pltpu.VMEM((2, 2 * hidden, CHUNK), bf16),
            pltpu.VMEM((2, count, CHUNK), bf16),
        ],
        compiler_params=params(),
        cost_estimate=pl.CostEstimate(
            flops=flops * 3, bytes_accessed=amount * 2 * hidden * depth * 2, transcendentals=0
        ),
        name="hidden_units",
    )(rows, gate, up, smooth)


def combine_kernel(
    units, hot_ref, share_ref, hf_ref, hq_ref, down_ref, level_ref, scale_ref, quant_ref, float_ref,
    wide_f, wide_q, keep_q, keep_f,
):
    block, e = pl.program_id(0), pl.program_id(1)
    shards, count, part = hf_ref.shape[0], hf_ref.shape[2], hf_ref.shape[3]
    unit_rows = UNIT * CAP

    @pl.when(block == 0)
    def _():
        for r in range(0, count, SLAB):
            spot = slice(r, r + SLAB)
            top = None
            for s in range(shards):
                value = fold_max(jnp.abs(hq_ref[s, 0, spot, :]).astype(f32))
                top = value if top is None else jnp.maximum(top, value)
                wide_f[e, spot, s * part : (s + 1) * part] = hf_ref[s, 0, spot, :]
            top = jnp.max(top, axis=1, keepdims=True) + EPS
            inverse, scale = LEVELS / top, top / LEVELS
            for s in range(shards):
                value = hq_ref[s, 0, spot, :].astype(f32) * inverse
                wide_q[e, spot, s * part : (s + 1) * part] = (level_f32(value) * scale).astype(bf16)

    share = share_ref[0]
    out_q = jnp.dot(wide_q[e], level_ref[0], preferred_element_type=f32) * scale_ref[0] * share
    out_f = jnp.dot(wide_f[e], down_ref[0], preferred_element_type=f32) * share
    at = pl.ds(pl.multiple_of(e * unit_rows, SLAB), unit_rows)
    for u in range(units):
        spot = slice(u * unit_rows, (u + 1) * unit_rows)
        keep_q[u, at, :] = out_q[spot].astype(bf16)
        keep_f[u, at, :] = out_f[spot].astype(bf16)

    @pl.when(e == pl.num_programs(1) - 1)
    def _():
        tokens = hot_ref.shape[1]
        for u in range(units):
            spot = slice(u * tokens, (u + 1) * tokens)
            hot = hot_ref[u]
            quant_ref[spot, :] = jnp.dot(hot, keep_q[u], preferred_element_type=f32).astype(bf16)
            float_ref[spot, :] = jnp.dot(hot, keep_f[u], preferred_element_type=f32).astype(bf16)


def combine(hot_t, share, hf, hq, down, level, scale):
    units, unit_tokens, hot_rows = hot_t.shape
    shards, experts, count, part = hf.shape
    hidden, width = down.shape[1:]
    block = 512
    out = jax.ShapeDtypeStruct((units * unit_tokens, width), bf16)
    out_spec = pl.BlockSpec((units * unit_tokens, block), lambda c, e: (0, c))
    once = lambda c, e: (0, jnp.where(c == 0, e, experts - 1), 0, 0)
    weight_spec = pl.BlockSpec((1, hidden, block), lambda c, e: (e, 0, c))
    return pl.pallas_call(
        functools.partial(combine_kernel, units),
        grid=(width // block, experts),
        out_shape=(out, out),
        in_specs=[
            pl.BlockSpec(hot_t.shape, lambda c, e: (0, 0, 0)),
            pl.BlockSpec((1, count, 1), lambda c, e: (e, 0, 0)),
            pl.BlockSpec((shards, 1, count, part), once),
            pl.BlockSpec((shards, 1, count, part), once),
            weight_spec,
            weight_spec,
            pl.BlockSpec((1, 1, block), lambda c, e: (e, 0, c)),
        ],
        out_specs=(out_spec, out_spec),
        scratch_shapes=[
            pltpu.VMEM((experts, count, hidden), bf16),
            pltpu.VMEM((experts, count, hidden), bf16),
            pltpu.VMEM((units, hot_rows, block), bf16),
            pltpu.VMEM((units, hot_rows, block), bf16),
        ],
        compiler_params=params(),
        cost_estimate=pl.CostEstimate(
            flops=4 * experts * count * hidden * width, bytes_accessed=down.size * 4, transcendentals=0
        ),
        name="down_and_combine",
    )(hot_t, share, hf, hq, down, level, scale)


def on_device(tokens, expert_ids, route_weights, gate_weight, up_weight, down_weight):
    groups = lax.axis_size("dp")
    group_tokens = tokens.shape[0]
    experts = gate_weight.shape[0]

    ids = lax.all_gather(expert_ids, "dp", axis=0, tiled=True).T
    route = lax.all_gather(route_weights, "dp", axis=0, tiled=True).T
    all_tokens = lax.all_gather(tokens, ("dp", "expert"), axis=0)
    all_tokens = all_tokens.reshape((groups, -1) + tokens.shape)

    local_peak = jnp.maximum(
        jnp.max(jnp.abs(gate_weight), axis=1), jnp.max(jnp.abs(up_weight), axis=1)
    )
    weight_peak = lax.pmax(local_peak, "expert").astype(f32)
    levels, scale = down_quant(down_weight)

    first = (lax.axis_index("dp") * experts).astype(jnp.int32).reshape(1)
    hot, share = prep(first, ids, route, experts, groups, group_tokens)
    hot_t = jnp.swapaxes(hot, 1, 2)
    rows, smooth = expert_rows(hot, all_tokens, weight_peak, experts, groups)

    parts = 2
    amount = experts // parts
    hf, hq = [], []
    for p in range(parts):
        one_f, one_q = hidden_units(rows, gate_weight, up_weight, smooth, p * amount, amount)
        hf.append(lax.all_gather(one_f, "expert", axis=0))
        hq.append(lax.all_gather(one_q, "expert", axis=0))
    hf = jnp.concatenate(hf, axis=1)
    hq = jnp.concatenate(hq, axis=1)
    part_q, part_f = combine(hot_t, share, hf, hq, down_weight, levels, scale)
    out_q = lax.psum_scatter(part_q, "dp", scatter_dimension=0, tiled=True)
    out_f = lax.psum_scatter(part_f, "dp", scatter_dimension=0, tiled=True)
    return out_q, out_f.astype(f32)


def solution(mesh):
    in_specs = (
        P("dp", "expert"),
        P("dp", None),
        P("dp", None),
        P("dp", "expert", None),
        P("dp", "expert", None),
        P("dp", None, "expert"),
    )
    out_specs = (P("dp", "expert"), P("dp", "expert"))
    return jax.shard_map(
        on_device, mesh=mesh, in_specs=in_specs, out_specs=out_specs, check_vma=False
    )
```

```python
import functools

import jax
import jax.numpy as jnp
from jax import lax
from jax.experimental import pallas as pl
from jax.experimental.pallas import tpu as pltpu
from jax.sharding import PartitionSpec as P

CAP = 20
UNIT = 4
LEVELS = 7.0
EPS = 1e-06
VMEM = 56 * 1024 * 1024
LANES = 128
SLAB = 16

FRACTION_BF16 = (6.55787162, -12.52307356, 9.17209913)

bf16 = jnp.bfloat16
f32 = jnp.float32


def fraction(r, coefficients):
    dtype = r.dtype
    square = r * r
    total = jnp.asarray(coefficients[-1], dtype)
    for c in coefficients[-2::-1]:
        total = total * square + jnp.asarray(c, dtype)
    return (r * square) * total


def level_bf16(v):
    n = jnp.round(v)
    r = (v - n).astype(bf16)
    return n.astype(bf16) + fraction(r, FRACTION_BF16)


def level_mixed(v):
    n = jnp.round(v)
    return n + fraction((v - n).astype(bf16), FRACTION_BF16).astype(f32)


def fold_max(x):
    if x.shape[1] % LANES:
        return jnp.max(x, axis=1, keepdims=True)
    out = x[:, :LANES]
    for c in range(LANES, x.shape[1], LANES):
        out = jnp.maximum(out, x[:, c : c + LANES])
    return out


def wide(x, width):
    return jnp.concatenate([x] * (width // LANES), axis=1)


def dot_t(a, b):
    return lax.dot_general(a, b, (((1,), (1,)), ((), ())), preferred_element_type=f32)


def params():
    return pltpu.CompilerParams(vmem_limit_bytes=VMEM)


def prep_kernel(local_experts, groups, choices, first_ref, route_ref, hot_ref, share_ref):
    units = groups // UNIT
    group_tokens = route_ref.shape[1]
    unit_rows, unit_tokens = UNIT * CAP, UNIT * group_tokens
    first = first_ref[0].astype(f32)
    before = lax.broadcasted_iota(jnp.int32, (group_tokens, group_tokens), 0) < lax.broadcasted_iota(
        jnp.int32, (group_tokens, group_tokens), 1
    )
    before = jnp.where(before, 1.0, 0.0).astype(bf16)
    codes, weights = [], []
    for g in range(groups):
        base = 2 * choices * g
        ids = route_ref[base : base + choices, :]
        route = route_ref[base + choices : base + 2 * choices, :]
        shares = route / jnp.sum(route, axis=0, keepdims=True)
        hits, mine = [], []
        for e in range(local_experts):
            hit = ids == first + float(e)
            hits.append(jnp.max(jnp.where(hit, 1.0, 0.0), axis=0, keepdims=True))
            mine.append(jnp.sum(jnp.where(hit, shares, 0.0), axis=0, keepdims=True))
        part = jnp.concatenate(hits, axis=0)
        weights.append(jnp.concatenate(mine, axis=0))
        slot = jnp.dot(part.astype(bf16), before, preferred_element_type=f32)
        codes.append(jnp.where(part > 0.5, slot + float((g % UNIT) * CAP), -1.0))
    row = lax.broadcasted_iota(jnp.int32, (unit_rows, unit_tokens), 0).astype(f32)
    for u in range(units):
        code = jnp.concatenate(codes[u * UNIT : (u + 1) * UNIT], axis=1)
        weight = jnp.concatenate(weights[u * UNIT : (u + 1) * UNIT], axis=1)
        for e in range(local_experts):
            hot = row == code[e : e + 1, :]
            hot_ref[u, e * unit_rows : (e + 1) * unit_rows, :] = jnp.where(hot, 1.0, 0.0).astype(bf16)
            share_ref[e, u * unit_rows : (u + 1) * unit_rows, :] = jnp.sum(
                jnp.where(hot, weight[e : e + 1, :], 0.0), axis=1, keepdims=True
            )


def prep(first, route, local_experts, groups, choices):
    units = groups // UNIT
    return pl.pallas_call(
        functools.partial(prep_kernel, local_experts, groups, choices),
        out_shape=(
            jax.ShapeDtypeStruct((units, local_experts * UNIT * CAP, UNIT * route.shape[1]), bf16),
            jax.ShapeDtypeStruct((local_experts, groups * CAP, 1), f32),
        ),
        in_specs=[
            pl.BlockSpec(memory_space=pltpu.SMEM),
            pl.BlockSpec(memory_space=pltpu.VMEM),
        ],
        out_specs=(pl.BlockSpec(memory_space=pltpu.VMEM), pl.BlockSpec(memory_space=pltpu.VMEM)),
        compiler_params=params(),
        name="routing_tables",
    )(first, route)


def down_quant_kernel(rows, width, down_ref, level_ref, scale_ref):
    step = 8 * SLAB

    def peak(i, carry):
        base = pl.multiple_of(i * step, step)
        for j in range(0, step, SLAB):
            carry = jnp.maximum(carry, jnp.abs(down_ref[0, pl.ds(base + j, SLAB), :]))
        return carry

    top = lax.fori_loop(0, rows // step, peak, jnp.zeros((SLAB, width), bf16))
    top = jnp.max(top.astype(f32), axis=0, keepdims=True) + EPS
    scale_ref[0] = top / LEVELS
    inverse = jnp.broadcast_to(LEVELS / top, (SLAB, width))

    def quantize(i, carry):
        base = pl.multiple_of(i * step, step)
        for j in range(0, step, SLAB):
            value = down_ref[0, pl.ds(base + j, SLAB), :].astype(f32) * inverse
            level_ref[0, pl.ds(base + j, SLAB), :] = level_bf16(value)
        return carry

    lax.fori_loop(0, rows // step, quantize, 0)


def down_quant(down):
    experts, hidden, width = down.shape
    block = 512
    return pl.pallas_call(
        functools.partial(down_quant_kernel, hidden, block),
        grid=(experts, width // block),
        out_shape=(
            jax.ShapeDtypeStruct(down.shape, bf16),
            jax.ShapeDtypeStruct((experts, 1, width), f32),
        ),
        in_specs=[pl.BlockSpec((1, hidden, block), lambda e, c: (e, 0, c))],
        out_specs=(
            pl.BlockSpec((1, hidden, block), lambda e, c: (e, 0, c)),
            pl.BlockSpec((1, 1, block), lambda e, c: (e, 0, c)),
        ),
        compiler_params=params(),
        cost_estimate=pl.CostEstimate(
            flops=down.size * 24, bytes_accessed=down.size * 4, transcendentals=0
        ),
        name="down_levels",
    )(down)


def rows_kernel(local_experts, units, hot_ref, tokens_ref, peak_ref, rows_ref, smooth_ref):
    unit_rows = UNIT * CAP
    group_tokens, width = tokens_ref.shape[2], tokens_ref.shape[3]
    top = [None] * local_experts
    for u in range(units):
        tokens = tokens_ref[u * UNIT : (u + 1) * UNIT, 0].reshape(UNIT * group_tokens, width)
        picked = jnp.dot(hot_ref[u], tokens, preferred_element_type=f32)
        for e in range(local_experts):
            part = picked[e * unit_rows : (e + 1) * unit_rows]
            rows_ref[e, u * unit_rows : (u + 1) * unit_rows, :] = part.astype(bf16)
            most = jnp.max(jnp.abs(part), axis=0, keepdims=True)
            top[e] = most if top[e] is None else jnp.maximum(top[e], most)
    for e in range(local_experts):
        smooth_ref[e] = jnp.sqrt(jnp.maximum(top[e], 1.0) / (peak_ref[e : e + 1, :] + EPS))


def expert_rows(hot, tokens, weight_peak, local_experts, groups):
    shards, group_tokens, share = tokens.shape[1:]
    units = groups // UNIT
    block = 512
    per = share // block
    return pl.pallas_call(
        functools.partial(rows_kernel, local_experts, units),
        grid=(shards * per,),
        out_shape=(
            jax.ShapeDtypeStruct((local_experts, groups * CAP, shards * share), bf16),
            jax.ShapeDtypeStruct((local_experts, 1, shards * share), f32),
        ),
        in_specs=[
            pl.BlockSpec(hot.shape, lambda c: (0, 0, 0)),
            pl.BlockSpec((groups, 1, group_tokens, block), lambda c: (0, c // per, 0, c % per)),
            pl.BlockSpec((local_experts, block), lambda c: (0, c)),
        ],
        out_specs=(
            pl.BlockSpec((local_experts, groups * CAP, block), lambda c: (0, 0, c)),
            pl.BlockSpec((local_experts, 1, block), lambda c: (0, 0, c)),
        ),
        compiler_params=params(),
        name="expert_rows",
    )(hot, tokens, weight_peak)


CHUNK = 512


def silu_product(gate, up):
    return (gate / (1.0 + jnp.exp(-gate)) * up).astype(bf16)


def float_kernel(
    rows_ref, gate_ref, up_ref, smooth_ref,
    hidden_ref, inverse_w, scale_w, inverse_r, scale_r,
    smooth_s, unsmooth_s, top_s, top_r, acc,
):
    count = rows_ref.shape[1]
    hidden = gate_ref.shape[1]
    chunks = gate_ref.shape[2] // CHUNK
    weights = ((gate_ref, 0), (up_ref, hidden))

    smooth = smooth_ref[0]
    smooth_s[...] = jnp.broadcast_to(smooth, smooth_s.shape)
    unsmooth_s[...] = jnp.broadcast_to(1.0 / smooth, unsmooth_s.shape)
    top_s[...] = jnp.zeros_like(top_s)
    top_r[...] = jnp.zeros_like(top_r)
    acc[...] = jnp.zeros_like(acc)

    def peaks(i, carry):
        cols = pl.ds(pl.multiple_of(i * CHUNK, CHUNK), CHUNK)
        smooth_c = smooth_s[:, cols]
        unsmooth_c = unsmooth_s[:, cols]
        rows = rows_ref[0, :, cols]
        for ref, base in weights:
            acc[:, base : base + hidden] += dot_t(rows, ref[0, :, cols])
            for f in range(0, hidden, SLAB):
                value = jnp.abs(ref[0, f : f + SLAB, cols]).astype(f32) * smooth_c
                spot = slice(base + f, base + f + SLAB)
                top_s[spot, :] = jnp.maximum(top_s[spot, :], fold_max(value))
        for r in range(0, count, SLAB):
            value = jnp.abs(rows_ref[0, r : r + SLAB, cols]).astype(f32) * unsmooth_c
            top_r[r : r + SLAB, :] = jnp.maximum(top_r[r : r + SLAB, :], fold_max(value))
        return carry

    lax.fori_loop(0, chunks, peaks, 0)
    hidden_ref[0] = silu_product(acc[:, :hidden], acc[:, hidden:])

    for r in range(0, count, SLAB):
        top = jnp.max(top_r[r : r + SLAB, :], axis=1, keepdims=True) + EPS
        inverse_r[0, r : r + SLAB, :] = jnp.broadcast_to(LEVELS / top, (SLAB, LANES))
        scale_r[0, r : r + SLAB, :] = jnp.broadcast_to(top / LEVELS, (SLAB, LANES))
    eye = lax.broadcasted_iota(jnp.int32, (LANES, LANES), 0) == lax.broadcasted_iota(
        jnp.int32, (LANES, LANES), 1
    )
    for f in range(0, 2 * hidden, LANES):
        top = jnp.max(top_s[f : f + LANES, :], axis=1, keepdims=True) + EPS
        inverse_w[0, f : f + LANES, :] = jnp.broadcast_to(LEVELS / top, (LANES, LANES))
        scale_w[0, :, f : f + LANES] = jnp.sum(
            jnp.where(eye, top / LEVELS, 0.0), axis=0, keepdims=True
        )


def float_hidden(rows, gate, up, smooth):
    experts, count, depth = rows.shape
    hidden = gate.shape[1]

    def spec(*tail):
        return pl.BlockSpec((1,) + tail, lambda e: (e,) + (0,) * len(tail))

    tails = ((count, hidden), (2 * hidden, LANES), (1, 2 * hidden), (count, LANES), (count, LANES))
    kinds = (bf16, f32, f32, f32, f32)
    return pl.pallas_call(
        float_kernel,
        grid=(experts,),
        out_shape=tuple(jax.ShapeDtypeStruct((experts,) + s, k) for s, k in zip(tails, kinds)),
        in_specs=[spec(count, depth), spec(hidden, depth), spec(hidden, depth), spec(1, depth)],
        out_specs=tuple(spec(*s) for s in tails),
        scratch_shapes=[
            pltpu.VMEM((SLAB, depth), f32),
            pltpu.VMEM((SLAB, depth), f32),
            pltpu.VMEM((2 * hidden, LANES), f32),
            pltpu.VMEM((count, LANES), f32),
            pltpu.VMEM((count, 2 * hidden), f32),
        ],
        compiler_params=params(),
        cost_estimate=pl.CostEstimate(
            flops=4 * experts * count * depth * hidden * 2,
            bytes_accessed=experts * 2 * hidden * depth * 2,
            transcendentals=0,
        ),
        name="float_hidden",
    )(rows, gate, up, smooth)


def quant_kernel(
    rows_ref, gate_ref, up_ref, smooth_ref, inverse_w, scale_w, inverse_r, scale_r, hidden_ref,
    smooth_s, unsmooth_s, acc, levels, row_levels,
):
    count = rows_ref.shape[1]
    hidden = gate_ref.shape[1]
    chunks = gate_ref.shape[2] // CHUNK
    weights = ((gate_ref, 0), (up_ref, hidden))

    smooth = smooth_ref[0]
    smooth_s[...] = jnp.broadcast_to(smooth, smooth_s.shape)
    unsmooth_s[...] = jnp.broadcast_to(1.0 / smooth, unsmooth_s.shape)
    acc[...] = jnp.zeros_like(acc)

    def quantize(i, slot):
        cols = pl.ds(pl.multiple_of(i * CHUNK, CHUNK), CHUNK)
        smooth_c = smooth_s[:, cols]
        unsmooth_c = unsmooth_s[:, cols]
        for r in range(0, count, SLAB):
            value = rows_ref[0, r : r + SLAB, cols].astype(f32) * unsmooth_c
            value = value * wide(inverse_r[0, r : r + SLAB, :], CHUNK)
            level = level_mixed(value) * wide(scale_r[0, r : r + SLAB, :], CHUNK)
            row_levels[slot, r : r + SLAB, :] = level.astype(bf16)
        for ref, base in weights:
            for f in range(0, hidden, SLAB):
                value = ref[0, f : f + SLAB, cols].astype(f32) * smooth_c
                value = value * wide(inverse_w[0, base + f : base + f + SLAB, :], CHUNK)
                levels[slot, base + f : base + f + SLAB, :] = level_bf16(value)

    def multiply(slot):
        acc[...] += dot_t(row_levels[slot], levels[slot])

    quantize(0, 0)

    def pair(i, carry):
        multiply(0)
        quantize(2 * i + 1, 1)
        multiply(1)
        quantize(2 * i + 2, 0)
        return carry

    lax.fori_loop(0, chunks // 2 - 1, pair, 0)
    multiply(0)
    quantize(chunks - 1, 1)
    multiply(1)

    scaled = acc[...] * scale_w[0]
    hidden_ref[0] = silu_product(scaled[:, :hidden], scaled[:, hidden:])


def quant_hidden(rows, gate, up, smooth, scales, first, amount):
    count, depth = rows.shape[1:]
    hidden = gate.shape[1]

    def spec(*tail):
        return pl.BlockSpec((1,) + tail, lambda e: (first + e,) + (0,) * len(tail))

    return pl.pallas_call(
        quant_kernel,
        grid=(amount,),
        out_shape=jax.ShapeDtypeStruct((amount, count, hidden), bf16),
        in_specs=[spec(*a.shape[1:]) for a in (rows, gate, up, smooth) + scales],
        out_specs=pl.BlockSpec((1, count, hidden), lambda e: (e, 0, 0)),
        scratch_shapes=[
            pltpu.VMEM((SLAB, depth), f32),
            pltpu.VMEM((SLAB, depth), f32),
            pltpu.VMEM((count, 2 * hidden), f32),
            pltpu.VMEM((2, 2 * hidden, CHUNK), bf16),
            pltpu.VMEM((2, count, CHUNK), bf16),
        ],
        compiler_params=params(),
        cost_estimate=pl.CostEstimate(
            flops=8 * amount * count * depth * hidden * 2,
            bytes_accessed=amount * 2 * hidden * depth * 2,
            transcendentals=0,
        ),
        name="quant_hidden",
    )(rows, gate, up, smooth, *scales)


def combine_kernel(amounts, quantized, hot_ref, share_ref, *refs):
    parts = len(amounts)
    hidden_refs, down_ref, scale_ref = refs[:parts], refs[parts], refs[parts + 1]
    out_ref, wide_s, keep_s = refs[parts + 2 :]
    block, e = pl.program_id(0), pl.program_id(1)
    shards, _, count, part = hidden_refs[0].shape
    unit_rows = UNIT * CAP
    units = hot_ref.shape[0]
    first = 0
    for ref, amount in zip(hidden_refs, amounts):

        @pl.when((block == 0) & (e >= first) & (e < first + amount))
        def _(ref=ref):
            for r in range(0, count, SLAB):
                spot = slice(r, r + SLAB)
                if not quantized:
                    for s in range(shards):
                        wide_s[e, spot, s * part : (s + 1) * part] = ref[s, 0, spot, :]
                    continue
                top = None
                for s in range(shards):
                    value = fold_max(jnp.abs(ref[s, 0, spot, :]).astype(f32))
                    top = value if top is None else jnp.maximum(top, value)
                top = jnp.max(top, axis=1, keepdims=True) + EPS
                inverse, scale = LEVELS / top, top / LEVELS
                for s in range(shards):
                    value = level_mixed(ref[s, 0, spot, :].astype(f32) * inverse) * scale
                    wide_s[e, spot, s * part : (s + 1) * part] = value.astype(bf16)

        first += amount

    out = jnp.dot(wide_s[e], down_ref[0], preferred_element_type=f32) * scale_ref[0] * share_ref[0]
    at = pl.ds(pl.multiple_of(e * unit_rows, SLAB), unit_rows)
    for u in range(units):
        keep_s[u, at, :] = out[u * unit_rows : (u + 1) * unit_rows].astype(bf16)

    @pl.when(e == pl.num_programs(1) - 1)
    def _():
        tokens = hot_ref.shape[1]
        for u in range(units):
            out_ref[u * tokens : (u + 1) * tokens, :] = jnp.dot(
                hot_ref[u], keep_s[u], preferred_element_type=f32
            ).astype(bf16)


def combine(hot_t, share, hidden_parts, down, scale, quantized):
    units, unit_tokens, hot_rows = hot_t.shape
    shards, _, count, part = hidden_parts[0].shape
    experts, hidden, width = down.shape
    block = 512
    amounts = tuple(h.shape[1] for h in hidden_parts)
    hidden_specs, first = [], 0
    for amount in amounts:

        def once(c, e, first=first, amount=amount):
            return (0, jnp.where(c == 0, jnp.clip(e - first, 0, amount - 1), amount - 1), 0, 0)

        hidden_specs.append(pl.BlockSpec((shards, 1, count, part), once))
        first += amount
    return pl.pallas_call(
        functools.partial(combine_kernel, amounts, quantized),
        grid=(width // block, experts),
        out_shape=jax.ShapeDtypeStruct((units * unit_tokens, width), bf16),
        in_specs=[
            pl.BlockSpec(hot_t.shape, lambda c, e: (0, 0, 0)),
            pl.BlockSpec((1, count, 1), lambda c, e: (e, 0, 0)),
            *hidden_specs,
            pl.BlockSpec((1, hidden, block), lambda c, e: (e, 0, c)),
            pl.BlockSpec((1, 1, block), lambda c, e: (e, 0, c)),
        ],
        out_specs=pl.BlockSpec((units * unit_tokens, block), lambda c, e: (0, c)),
        scratch_shapes=[
            pltpu.VMEM((experts, count, hidden), bf16),
            pltpu.VMEM((units, hot_rows, block), bf16),
        ],
        compiler_params=params(),
        cost_estimate=pl.CostEstimate(
            flops=2 * experts * count * hidden * width, bytes_accessed=down.size * 2, transcendentals=0
        ),
        name="combine_quant" if quantized else "combine_float",
    )(hot_t, share, *hidden_parts, down, scale)


def to_tokens(part, groups):
    width = part.shape[1]
    back = lax.all_to_all(part.reshape(groups, -1, width), "dp", split_axis=0, concat_axis=0)
    return jnp.sum(back.astype(f32), axis=0)


def on_device(tokens, expert_ids, route_weights, gate_weight, up_weight, down_weight):
    groups = lax.axis_size("dp")
    experts = gate_weight.shape[0]
    choices = expert_ids.shape[1]

    payload = jnp.concatenate([expert_ids.T.astype(f32), route_weights.T], axis=0)
    route = lax.all_gather(payload, "dp", axis=0, tiled=True)
    all_tokens = lax.all_gather(tokens, ("dp", "expert"), axis=0)
    all_tokens = all_tokens.reshape((groups, -1) + tokens.shape)

    local_peak = jnp.maximum(
        jnp.max(jnp.abs(gate_weight), axis=1), jnp.max(jnp.abs(up_weight), axis=1)
    )
    weight_peak = lax.pmax(local_peak, "expert").astype(f32)
    levels, level_scale = down_quant(down_weight)

    first = (lax.axis_index("dp") * experts).astype(jnp.int32).reshape(1)
    hot, share = prep(first, route, experts, groups, choices)
    hot_t = jnp.swapaxes(hot, 1, 2)
    hot, levels = lax.optimization_barrier((hot, levels))
    rows, smooth = expert_rows(hot, all_tokens, weight_peak, experts, groups)

    hf, *scales = float_hidden(rows, gate_weight, up_weight, smooth)
    scales = tuple(scales)
    wide_f = lax.all_gather(hf, "expert", axis=0)

    half = experts // 2
    hq = quant_hidden(rows, gate_weight, up_weight, smooth, scales, 0, half)
    wide_q = [lax.all_gather(hq, "expert", axis=0)]
    ones = jnp.ones_like(level_scale)
    hq, wide_f = lax.optimization_barrier((hq, wide_f))
    part_f = combine(hot_t, share, [wide_f], down_weight, ones, False)
    out_f = to_tokens(part_f, groups)
    rows, part_f = lax.optimization_barrier((rows, part_f))
    hq = quant_hidden(rows, gate_weight, up_weight, smooth, scales, half, experts - half)
    wide_q.append(lax.all_gather(hq, "expert", axis=0))
    part_q = combine(hot_t, share, wide_q, levels, level_scale, True)
    out_q = to_tokens(part_q, groups)
    return out_q.astype(bf16), out_f


def solution(mesh):
    in_specs = (
        P("dp", "expert"),
        P("dp", None),
        P("dp", None),
        P("dp", "expert", None),
        P("dp", "expert", None),
        P("dp", None, "expert"),
    )
    out_specs = (P("dp", "expert"), P("dp", "expert"))
    return jax.shard_map(
        on_device, mesh=mesh, in_specs=in_specs, out_specs=out_specs, check_vma=False
    )
```

```python
import functools

import jax
import jax.numpy as jnp
from jax import lax
from jax.experimental import pallas as pl
from jax.experimental.pallas import tpu as pltpu
from jax.sharding import PartitionSpec as P

CAP = 20
UNIT = 4
LEVELS = 7.0
EPS = 1e-06
VMEM = 56 * 1024 * 1024
LANES = 128
SLAB = 16
CHUNK = 512
BRIEF = pl.CostEstimate(flops=1, bytes_accessed=1, transcendentals=0)

FRACTION_BF16 = (6.55787162, -12.52307356, 9.17209913)

bf16 = jnp.bfloat16
f32 = jnp.float32


def fraction(r, coefficients):
    dtype = r.dtype
    square = r * r
    total = jnp.asarray(coefficients[-1], dtype)
    for c in coefficients[-2::-1]:
        total = total * square + jnp.asarray(c, dtype)
    return (r * square) * total


def level_bf16(v):
    n = jnp.round(v)
    r = (v - n).astype(bf16)
    return n.astype(bf16) + fraction(r, FRACTION_BF16)


def level_mixed(v):
    n = jnp.round(v)
    return n + fraction((v - n).astype(bf16), FRACTION_BF16).astype(f32)


def fold_max(x):
    if x.shape[1] % LANES:
        return jnp.max(x, axis=1, keepdims=True)
    out = x[:, :LANES]
    for c in range(LANES, x.shape[1], LANES):
        out = jnp.maximum(out, x[:, c : c + LANES])
    return out


def wide(x, width):
    return jnp.concatenate([x] * (width // LANES), axis=1)


def dot_t(a, b):
    return lax.dot_general(a, b, (((1,), (1,)), ((), ())), preferred_element_type=f32)


def flipped(x):
    high, broad = -x.shape[0] % LANES, -x.shape[1] % LANES
    return jnp.pad(x, ((0, high), (0, broad))).T[: x.shape[1], : x.shape[0]]


def params():
    return pltpu.CompilerParams(vmem_limit_bytes=VMEM)


def prep_kernel(local_experts, groups, choices, first_ref, route_ref, hot_ref, share_ref):
    units = groups // UNIT
    group_tokens = route_ref.shape[1]
    unit_rows, unit_tokens = UNIT * CAP, UNIT * group_tokens
    first = first_ref[0].astype(f32)
    before = lax.broadcasted_iota(jnp.int32, (group_tokens, group_tokens), 0) < lax.broadcasted_iota(
        jnp.int32, (group_tokens, group_tokens), 1
    )
    before = jnp.where(before, 1.0, 0.0).astype(bf16)
    codes, weights = [], []
    for g in range(groups):
        base = 2 * choices * g
        ids = route_ref[base : base + choices, :]
        route = route_ref[base + choices : base + 2 * choices, :]
        shares = route / jnp.sum(route, axis=0, keepdims=True)
        hits, mine = [], []
        for e in range(local_experts):
            hit = ids == first + float(e)
            hits.append(jnp.max(jnp.where(hit, 1.0, 0.0), axis=0, keepdims=True))
            mine.append(jnp.sum(jnp.where(hit, shares, 0.0), axis=0, keepdims=True))
        part = jnp.concatenate(hits, axis=0)
        weights.append(jnp.concatenate(mine, axis=0))
        slot = jnp.dot(part.astype(bf16), before, preferred_element_type=f32)
        codes.append(jnp.where(part > 0.5, slot + float((g % UNIT) * CAP), -1.0))
    row = lax.broadcasted_iota(jnp.int32, (unit_rows, unit_tokens), 0).astype(f32)
    for u in range(units):
        code = jnp.concatenate(codes[u * UNIT : (u + 1) * UNIT], axis=1)
        weight = jnp.concatenate(weights[u * UNIT : (u + 1) * UNIT], axis=1)
        for e in range(local_experts):
            hot = row == code[e : e + 1, :]
            hot_ref[u, e * unit_rows : (e + 1) * unit_rows, :] = jnp.where(hot, 1.0, 0.0).astype(bf16)
            share_ref[e, u * unit_rows : (u + 1) * unit_rows, :] = jnp.sum(
                jnp.where(hot, weight[e : e + 1, :], 0.0), axis=1, keepdims=True
            )


def prep(first, route, local_experts, groups, choices):
    units = groups // UNIT
    return pl.pallas_call(
        functools.partial(prep_kernel, local_experts, groups, choices),
        out_shape=(
            jax.ShapeDtypeStruct((units, local_experts * UNIT * CAP, UNIT * route.shape[1]), bf16),
            jax.ShapeDtypeStruct((local_experts, groups * CAP, 1), f32),
        ),
        in_specs=[
            pl.BlockSpec(memory_space=pltpu.SMEM),
            pl.BlockSpec(memory_space=pltpu.VMEM),
        ],
        out_specs=(pl.BlockSpec(memory_space=pltpu.VMEM), pl.BlockSpec(memory_space=pltpu.VMEM)),
        compiler_params=params(),
        name="routing_tables",
    )(first, route)


def channel_peak_kernel(gate_ref, up_ref, peak_ref):
    hidden, depth = gate_ref.shape[1:]

    def one(i, carry):
        cols = pl.ds(pl.multiple_of(i * CHUNK, CHUNK), CHUNK)
        top = None
        for ref in (gate_ref, up_ref):
            for f in range(0, hidden, SLAB):
                value = jnp.abs(ref[0, f : f + SLAB, cols])
                top = value if top is None else jnp.maximum(top, value)
        peak_ref[0, :, cols] = jnp.max(top.astype(f32), axis=0, keepdims=True)
        return carry

    lax.fori_loop(0, depth // CHUNK, one, 0)


def channel_peak(gate, up):
    experts, hidden, depth = gate.shape
    spec = pl.BlockSpec((1, hidden, depth), lambda e: (e, 0, 0))
    return pl.pallas_call(
        channel_peak_kernel,
        grid=(experts,),
        out_shape=jax.ShapeDtypeStruct((experts, 1, depth), f32),
        in_specs=[spec, spec],
        out_specs=pl.BlockSpec((1, 1, depth), lambda e: (e, 0, 0)),
        compiler_params=params(),
        cost_estimate=BRIEF,
        name="channel_peak",
    )(gate, up)


def down_quant_kernel(rows, width, down_ref, level_ref, scale_ref):
    step = 8 * SLAB

    def peak(i, carry):
        base = pl.multiple_of(i * step, step)
        for j in range(0, step, SLAB):
            carry = jnp.maximum(carry, jnp.abs(down_ref[0, pl.ds(base + j, SLAB), :]))
        return carry

    top = lax.fori_loop(0, rows // step, peak, jnp.zeros((SLAB, width), bf16))
    top = jnp.max(top.astype(f32), axis=0, keepdims=True) + EPS
    scale_ref[0] = top / LEVELS
    inverse = jnp.broadcast_to(LEVELS / top, (SLAB, width))

    def quantize(i, carry):
        base = pl.multiple_of(i * step, step)
        for j in range(0, step, SLAB):
            value = down_ref[0, pl.ds(base + j, SLAB), :].astype(f32) * inverse
            level_ref[0, pl.ds(base + j, SLAB), :] = level_bf16(value)
        return carry

    lax.fori_loop(0, rows // step, quantize, 0)


def down_quant(down):
    experts, hidden, width = down.shape
    block = 512
    return pl.pallas_call(
        functools.partial(down_quant_kernel, hidden, block),
        grid=(experts, width // block),
        out_shape=(
            jax.ShapeDtypeStruct(down.shape, bf16),
            jax.ShapeDtypeStruct((experts, 1, width), f32),
        ),
        in_specs=[pl.BlockSpec((1, hidden, block), lambda e, c: (e, 0, c))],
        out_specs=(
            pl.BlockSpec((1, hidden, block), lambda e, c: (e, 0, c)),
            pl.BlockSpec((1, 1, block), lambda e, c: (e, 0, c)),
        ),
        compiler_params=params(),
        cost_estimate=BRIEF,
        name="down_levels",
    )(down)


def rows_kernel(local_experts, units, hot_ref, tokens_ref, peak_ref, rows_ref, smooth_ref):
    unit_rows = UNIT * CAP
    group_tokens, width = tokens_ref.shape[2], tokens_ref.shape[3]
    top = [None] * local_experts
    for u in range(units):
        tokens = tokens_ref[u * UNIT : (u + 1) * UNIT, 0].reshape(UNIT * group_tokens, width)
        picked = jnp.dot(hot_ref[u], tokens, preferred_element_type=f32)
        for e in range(local_experts):
            part = picked[e * unit_rows : (e + 1) * unit_rows]
            rows_ref[e, u * unit_rows : (u + 1) * unit_rows, :] = part.astype(bf16)
            most = jnp.max(jnp.abs(part), axis=0, keepdims=True)
            top[e] = most if top[e] is None else jnp.maximum(top[e], most)
    for e in range(local_experts):
        smooth_ref[e] = jnp.sqrt(jnp.maximum(top[e], 1.0) / (peak_ref[e : e + 1, :] + EPS))


def expert_rows(hot, tokens, weight_peak, local_experts, groups):
    shards, group_tokens, share = tokens.shape[1:]
    units = groups // UNIT
    block = 512
    per = share // block
    return pl.pallas_call(
        functools.partial(rows_kernel, local_experts, units),
        grid=(shards * per,),
        out_shape=(
            jax.ShapeDtypeStruct((local_experts, groups * CAP, shards * share), bf16),
            jax.ShapeDtypeStruct((local_experts, 1, shards * share), f32),
        ),
        in_specs=[
            pl.BlockSpec(hot.shape, lambda c: (0, 0, 0)),
            pl.BlockSpec((groups, 1, group_tokens, block), lambda c: (0, c // per, 0, c % per)),
            pl.BlockSpec((local_experts, block), lambda c: (0, c)),
        ],
        out_specs=(
            pl.BlockSpec((local_experts, groups * CAP, block), lambda c: (0, 0, c)),
            pl.BlockSpec((local_experts, 1, block), lambda c: (0, 0, c)),
        ),
        compiler_params=params(),
        name="expert_rows",
    )(hot, tokens, weight_peak)


def silu_product(both):
    half = both.shape[0] // 2
    gate, up = both[:half], both[half:]
    return flipped(gate / (1.0 + jnp.exp(-gate)) * up).astype(bf16)


def float_kernel(
    rows_ref, gate_ref, up_ref, smooth_ref,
    hidden_ref, inverse_w, scale_w, inverse_r, scale_r,
    smooth_s, unsmooth_s, top_s, top_r, acc,
):
    count = rows_ref.shape[1]
    hidden = gate_ref.shape[1]
    chunks = gate_ref.shape[2] // CHUNK
    weights = ((gate_ref, 0), (up_ref, hidden))

    smooth = smooth_ref[0]
    smooth_s[...] = jnp.broadcast_to(smooth, smooth_s.shape)
    unsmooth_s[...] = jnp.broadcast_to(1.0 / smooth, unsmooth_s.shape)
    top_s[...] = jnp.zeros_like(top_s)
    top_r[...] = jnp.zeros_like(top_r)
    acc[...] = jnp.zeros_like(acc)

    def peaks(i, carry):
        cols = pl.ds(pl.multiple_of(i * CHUNK, CHUNK), CHUNK)
        smooth_c = smooth_s[:, cols]
        unsmooth_c = unsmooth_s[:, cols]
        rows = rows_ref[0, :, cols]
        for ref, base in weights:
            acc[base : base + hidden, :] += dot_t(ref[0, :, cols], rows)
            for f in range(0, hidden, SLAB):
                value = jnp.abs(ref[0, f : f + SLAB, cols]).astype(f32) * smooth_c
                spot = slice(base + f, base + f + SLAB)
                top_s[spot, :] = jnp.maximum(top_s[spot, :], fold_max(value))
        for r in range(0, count, SLAB):
            value = jnp.abs(rows_ref[0, r : r + SLAB, cols]).astype(f32) * unsmooth_c
            top_r[r : r + SLAB, :] = jnp.maximum(top_r[r : r + SLAB, :], fold_max(value))
        return carry

    lax.fori_loop(0, chunks, peaks, 0)
    hidden_ref[0] = silu_product(acc[...])

    for r in range(0, count, SLAB):
        top = jnp.max(top_r[r : r + SLAB, :], axis=1, keepdims=True) + EPS
        inverse_r[0, r : r + SLAB, :] = jnp.broadcast_to(LEVELS / top, (SLAB, LANES))
        scale_r[0, r : r + SLAB, :] = jnp.broadcast_to(top / LEVELS, (SLAB, LANES))
    for f in range(0, 2 * hidden, LANES):
        top = jnp.max(top_s[f : f + LANES, :], axis=1, keepdims=True) + EPS
        inverse_w[0, f : f + LANES, :] = jnp.broadcast_to(LEVELS / top, (LANES, LANES))
        scale_w[0, f : f + LANES, :] = jnp.broadcast_to(top / LEVELS, (LANES, LANES))


def float_hidden(rows, gate, up, smooth):
    experts, count, depth = rows.shape
    hidden = gate.shape[1]

    def spec(*tail):
        return pl.BlockSpec((1,) + tail, lambda e: (e,) + (0,) * len(tail))

    tails = ((count, hidden), (2 * hidden, LANES), (2 * hidden, LANES), (count, LANES), (count, LANES))
    kinds = (bf16, f32, f32, f32, f32)
    return pl.pallas_call(
        float_kernel,
        grid=(experts,),
        out_shape=tuple(jax.ShapeDtypeStruct((experts,) + s, k) for s, k in zip(tails, kinds)),
        in_specs=[spec(count, depth), spec(hidden, depth), spec(hidden, depth), spec(1, depth)],
        out_specs=tuple(spec(*s) for s in tails),
        scratch_shapes=[
            pltpu.VMEM((SLAB, depth), f32),
            pltpu.VMEM((SLAB, depth), f32),
            pltpu.VMEM((2 * hidden, LANES), f32),
            pltpu.VMEM((count, LANES), f32),
            pltpu.VMEM((2 * hidden, count), f32),
        ],
        compiler_params=params(),
        cost_estimate=pl.CostEstimate(
            flops=4 * experts * count * depth * hidden * 2,
            bytes_accessed=experts * 2 * hidden * depth * 2,
            transcendentals=0,
        ),
        name="float_hidden",
    )(rows, gate, up, smooth)


def quant_kernel(
    rows_ref, gate_ref, up_ref, smooth_ref, inverse_w, scale_w, inverse_r, scale_r, hidden_ref,
    smooth_s, unsmooth_s, acc, levels, row_levels,
):
    count = rows_ref.shape[1]
    hidden = gate_ref.shape[1]
    chunks = gate_ref.shape[2] // CHUNK
    weights = ((gate_ref, 0), (up_ref, hidden))

    smooth = smooth_ref[0]
    smooth_s[...] = jnp.broadcast_to(smooth, smooth_s.shape)
    unsmooth_s[...] = jnp.broadcast_to(1.0 / smooth, unsmooth_s.shape)
    acc[...] = jnp.zeros_like(acc)

    def quantize(i, slot):
        cols = pl.ds(pl.multiple_of(i * CHUNK, CHUNK), CHUNK)
        smooth_c = smooth_s[:, cols]
        unsmooth_c = unsmooth_s[:, cols]
        for r in range(0, count, SLAB):
            value = rows_ref[0, r : r + SLAB, cols].astype(f32) * unsmooth_c
            value = value * wide(inverse_r[0, r : r + SLAB, :], CHUNK)
            level = level_mixed(value) * wide(scale_r[0, r : r + SLAB, :], CHUNK)
            row_levels[slot, r : r + SLAB, :] = level.astype(bf16)
        for ref, base in weights:
            for f in range(0, hidden, SLAB):
                value = ref[0, f : f + SLAB, cols].astype(f32) * smooth_c
                value = value * wide(inverse_w[0, base + f : base + f + SLAB, :], CHUNK)
                levels[slot, base + f : base + f + SLAB, :] = level_bf16(value)

    def multiply(slot):
        acc[...] += dot_t(levels[slot], row_levels[slot])

    quantize(0, 0)

    def pair(i, carry):
        multiply(0)
        quantize(2 * i + 1, 1)
        multiply(1)
        quantize(2 * i + 2, 0)
        return carry

    lax.fori_loop(0, chunks // 2 - 1, pair, 0)
    multiply(0)
    quantize(chunks - 1, 1)
    multiply(1)

    hidden_ref[0] = silu_product(acc[...] * scale_w[0][:, :1])


def quant_hidden(rows, gate, up, smooth, scales, first, amount):
    count, depth = rows.shape[1:]
    hidden = gate.shape[1]

    def spec(*tail):
        return pl.BlockSpec((1,) + tail, lambda e: (first + e,) + (0,) * len(tail))

    return pl.pallas_call(
        quant_kernel,
        grid=(amount,),
        out_shape=jax.ShapeDtypeStruct((amount, count, hidden), bf16),
        in_specs=[spec(*a.shape[1:]) for a in (rows, gate, up, smooth) + scales],
        out_specs=pl.BlockSpec((1, count, hidden), lambda e: (e, 0, 0)),
        scratch_shapes=[
            pltpu.VMEM((SLAB, depth), f32),
            pltpu.VMEM((SLAB, depth), f32),
            pltpu.VMEM((2 * hidden, count), f32),
            pltpu.VMEM((2, 2 * hidden, CHUNK), bf16),
            pltpu.VMEM((2, count, CHUNK), bf16),
        ],
        compiler_params=params(),
        cost_estimate=pl.CostEstimate(
            flops=8 * amount * count * depth * hidden * 2,
            bytes_accessed=amount * 2 * hidden * depth * 2,
            transcendentals=0,
        ),
        name="quant_hidden",
    )(rows, gate, up, smooth, *scales)


def combine_kernel(amounts, quantized, hot_ref, share_ref, *refs):
    parts = len(amounts)
    hidden_refs, down_ref, scale_ref = refs[:parts], refs[parts], refs[parts + 1]
    out_ref, wide_s, keep_s = refs[parts + 2 :]
    block, e = pl.program_id(0), pl.program_id(1)
    shards, _, count, part = hidden_refs[0].shape
    unit_rows = UNIT * CAP
    units = hot_ref.shape[0]
    first = 0
    for ref, amount in zip(hidden_refs, amounts):

        @pl.when((block == 0) & (e >= first) & (e < first + amount))
        def _(ref=ref):
            for r in range(0, count, SLAB):
                spot = slice(r, r + SLAB)
                if not quantized:
                    for s in range(shards):
                        wide_s[e, spot, s * part : (s + 1) * part] = ref[s, 0, spot, :]
                    continue
                top = None
                for s in range(shards):
                    value = fold_max(jnp.abs(ref[s, 0, spot, :]).astype(f32))
                    top = value if top is None else jnp.maximum(top, value)
                top = jnp.max(top, axis=1, keepdims=True) + EPS
                inverse, scale = LEVELS / top, top / LEVELS
                for s in range(shards):
                    value = level_mixed(ref[s, 0, spot, :].astype(f32) * inverse) * scale
                    wide_s[e, spot, s * part : (s + 1) * part] = value.astype(bf16)

        first += amount

    out = jnp.dot(wide_s[e], down_ref[0], preferred_element_type=f32) * scale_ref[0] * share_ref[0]
    at = pl.ds(pl.multiple_of(e * unit_rows, SLAB), unit_rows)
    for u in range(units):
        keep_s[u, at, :] = out[u * unit_rows : (u + 1) * unit_rows].astype(bf16)

    @pl.when(e == pl.num_programs(1) - 1)
    def _():
        tokens = hot_ref.shape[1]
        for u in range(units):
            out_ref[u * tokens : (u + 1) * tokens, :] = jnp.dot(
                hot_ref[u], keep_s[u], preferred_element_type=f32
            ).astype(bf16)


def combine(hot_t, share, hidden_parts, down, scale, quantized, at, pieces):
    units, unit_tokens, hot_rows = hot_t.shape
    shards, _, count, part = hidden_parts[0].shape
    experts, hidden, width = down.shape
    block = width // pieces
    amounts = tuple(h.shape[1] for h in hidden_parts)
    hidden_specs, first = [], 0
    for amount in amounts:

        def once(c, e, first=first, amount=amount):
            return (0, jnp.where(c == 0, jnp.clip(e - first, 0, amount - 1), amount - 1), 0, 0)

        hidden_specs.append(pl.BlockSpec((shards, 1, count, part), once))
        first += amount
    return pl.pallas_call(
        functools.partial(combine_kernel, amounts, quantized),
        grid=(1, experts),
        out_shape=jax.ShapeDtypeStruct((units * unit_tokens, block), bf16),
        in_specs=[
            pl.BlockSpec(hot_t.shape, lambda c, e: (0, 0, 0)),
            pl.BlockSpec((1, count, 1), lambda c, e: (e, 0, 0)),
            *hidden_specs,
            pl.BlockSpec((1, hidden, block), lambda c, e: (e, 0, at)),
            pl.BlockSpec((1, 1, block), lambda c, e: (e, 0, at)),
        ],
        out_specs=pl.BlockSpec((units * unit_tokens, block), lambda c, e: (0, 0)),
        scratch_shapes=[
            pltpu.VMEM((experts, count, hidden), bf16),
            pltpu.VMEM((units, hot_rows, block), bf16),
        ],
        compiler_params=params(),
        cost_estimate=pl.CostEstimate(
            flops=2 * experts * count * hidden * width, bytes_accessed=down.size * 2, transcendentals=0
        ),
        name="combine_quant" if quantized else "combine_float",
    )(hot_t, share, *hidden_parts, down, scale)


def to_tokens(part, groups):
    width = part.shape[1]
    back = lax.all_to_all(part.reshape(groups, -1, width), "dp", split_axis=0, concat_axis=0)
    return jnp.sum(back.astype(f32), axis=0)


def from_all(x, axis):
    copies = jnp.broadcast_to(x, (lax.axis_size(axis),) + x.shape)
    return lax.all_to_all(copies, axis, split_axis=0, concat_axis=0)


def on_device(tokens, expert_ids, route_weights, gate_weight, up_weight, down_weight):
    groups = lax.axis_size("dp")
    experts = gate_weight.shape[0]
    choices = expert_ids.shape[1]

    payload = jnp.concatenate([expert_ids.T.astype(f32), route_weights.T], axis=0)
    route = from_all(payload, "dp").reshape(-1, payload.shape[1])
    all_tokens = lax.all_gather(tokens, ("dp", "expert"), axis=0)
    all_tokens = all_tokens.reshape((groups, -1) + tokens.shape)

    local_peak = channel_peak(gate_weight, up_weight)
    weight_peak = from_all(local_peak.reshape(experts, -1).astype(bf16), "expert")
    weight_peak = jnp.max(weight_peak, axis=0).astype(f32)
    down_weight, local_peak = lax.optimization_barrier((down_weight, local_peak))
    levels, level_scale = down_quant(down_weight)

    first = (lax.axis_index("dp") * experts).astype(jnp.int32).reshape(1)
    hot, share = prep(first, route, experts, groups, choices)
    hot_t = jnp.swapaxes(hot, 1, 2)
    hot, levels = lax.optimization_barrier((hot, levels))
    rows, smooth = expert_rows(hot, all_tokens, weight_peak, experts, groups)

    hf, *scales = float_hidden(rows, gate_weight, up_weight, smooth)
    scales = tuple(scales)
    wide_f = lax.all_gather(hf, "expert", axis=0)

    amounts = [experts // 2, experts // 4, experts - experts // 2 - experts // 4]
    wide_q, start, out_f = [], 0, None
    for p, amount in enumerate(a for a in amounts if a):
        hq = quant_hidden(rows, gate_weight, up_weight, smooth, scales, start, amount)
        start += amount
        wide_q.append(lax.all_gather(hq, "expert", axis=0))
        if p == 0:
            hq, wide_f = lax.optimization_barrier((hq, wide_f))
            part_f = combine(
                hot_t, share, [wide_f], down_weight, jnp.ones_like(level_scale), False, 0, 1
            )
            out_f = to_tokens(part_f, groups)
            rows, part_f = lax.optimization_barrier((rows, part_f))
    out_q = []
    for at in range(2):
        part_q = combine(hot_t, share, wide_q, levels, level_scale, True, at, 2)
        out_q.append(to_tokens(part_q, groups).astype(bf16))
        wide_q[0], part_q = lax.optimization_barrier((wide_q[0], part_q))
    return jnp.concatenate(out_q, axis=1), out_f


def solution(mesh):
    in_specs = (
        P("dp", "expert"),
        P("dp", None),
        P("dp", None),
        P("dp", "expert", None),
        P("dp", "expert", None),
        P("dp", None, "expert"),
    )
    out_specs = (P("dp", "expert"), P("dp", "expert"))
    return jax.shard_map(
        on_device, mesh=mesh, in_specs=in_specs, out_specs=out_specs, check_vma=False
    )
```

```python
import functools

import jax
import jax.numpy as jnp
from jax import lax
from jax.experimental import pallas as pl
from jax.experimental.pallas import tpu as pltpu
from jax.sharding import PartitionSpec as P

CAP = 20
UNIT = 4
LEVELS = 7.0
EPS = 1e-06
VMEM = 56 * 1024 * 1024
LANES = 128
SLAB = 16
CHUNK = 512
BRIEF = pl.CostEstimate(flops=1, bytes_accessed=1, transcendentals=0)

FRACTION_BF16 = (6.55787162, -12.52307356, 9.17209913)

bf16 = jnp.bfloat16
f32 = jnp.float32


def fraction(r, coefficients):
    dtype = r.dtype
    square = r * r
    total = jnp.asarray(coefficients[-1], dtype)
    for c in coefficients[-2::-1]:
        total = total * square + jnp.asarray(c, dtype)
    return (r * square) * total


def level_bf16(v):
    n = jnp.round(v)
    r = (v - n).astype(bf16)
    return n.astype(bf16) + fraction(r, FRACTION_BF16)


def level_mixed(v):
    n = jnp.round(v)
    return n + fraction((v - n).astype(bf16), FRACTION_BF16).astype(f32)


def fold_max(x):
    if x.shape[1] % LANES:
        return jnp.max(x, axis=1, keepdims=True)
    out = x[:, :LANES]
    for c in range(LANES, x.shape[1], LANES):
        out = jnp.maximum(out, x[:, c : c + LANES])
    return out


def wide(x, width):
    return jnp.concatenate([x] * (width // LANES), axis=1)


def dot_t(a, b):
    return lax.dot_general(a, b, (((1,), (1,)), ((), ())), preferred_element_type=f32)


def flipped(x):
    high, broad = -x.shape[0] % LANES, -x.shape[1] % LANES
    return jnp.pad(x, ((0, high), (0, broad))).T[: x.shape[1], : x.shape[0]]


def params():
    return pltpu.CompilerParams(vmem_limit_bytes=VMEM)


def prep_kernel(local_experts, groups, choices, first_ref, route_ref, hot_ref, share_ref):
    units = groups // UNIT
    group_tokens = route_ref.shape[1]
    unit_rows, unit_tokens = UNIT * CAP, UNIT * group_tokens
    first = first_ref[0].astype(f32)
    before = lax.broadcasted_iota(jnp.int32, (group_tokens, group_tokens), 0) < lax.broadcasted_iota(
        jnp.int32, (group_tokens, group_tokens), 1
    )
    before = jnp.where(before, 1.0, 0.0).astype(bf16)
    codes, weights = [], []
    for g in range(groups):
        base = 2 * choices * g
        ids = route_ref[base : base + choices, :]
        route = route_ref[base + choices : base + 2 * choices, :]
        shares = route / jnp.sum(route, axis=0, keepdims=True)
        hits, mine = [], []
        for e in range(local_experts):
            hit = ids == first + float(e)
            hits.append(jnp.max(jnp.where(hit, 1.0, 0.0), axis=0, keepdims=True))
            mine.append(jnp.sum(jnp.where(hit, shares, 0.0), axis=0, keepdims=True))
        part = jnp.concatenate(hits, axis=0)
        weights.append(jnp.concatenate(mine, axis=0))
        slot = jnp.dot(part.astype(bf16), before, preferred_element_type=f32)
        codes.append(jnp.where(part > 0.5, slot + float((g % UNIT) * CAP), -1.0))
    row = lax.broadcasted_iota(jnp.int32, (unit_rows, unit_tokens), 0).astype(f32)
    for u in range(units):
        code = jnp.concatenate(codes[u * UNIT : (u + 1) * UNIT], axis=1)
        weight = jnp.concatenate(weights[u * UNIT : (u + 1) * UNIT], axis=1)
        for e in range(local_experts):
            hot = row == code[e : e + 1, :]
            hot_ref[u, e * unit_rows : (e + 1) * unit_rows, :] = jnp.where(hot, 1.0, 0.0).astype(bf16)
            share_ref[e, u * unit_rows : (u + 1) * unit_rows, :] = jnp.sum(
                jnp.where(hot, weight[e : e + 1, :], 0.0), axis=1, keepdims=True
            )


def prep(first, route, local_experts, groups, choices):
    units = groups // UNIT
    return pl.pallas_call(
        functools.partial(prep_kernel, local_experts, groups, choices),
        out_shape=(
            jax.ShapeDtypeStruct((units, local_experts * UNIT * CAP, UNIT * route.shape[1]), bf16),
            jax.ShapeDtypeStruct((local_experts, groups * CAP, 1), f32),
        ),
        in_specs=[
            pl.BlockSpec(memory_space=pltpu.SMEM),
            pl.BlockSpec(memory_space=pltpu.VMEM),
        ],
        out_specs=(pl.BlockSpec(memory_space=pltpu.VMEM), pl.BlockSpec(memory_space=pltpu.VMEM)),
        compiler_params=params(),
        name="routing_tables",
    )(first, route)


def channel_peak_kernel(gate_ref, up_ref, peak_ref):
    hidden, depth = gate_ref.shape[1:]

    def one(i, carry):
        cols = pl.ds(pl.multiple_of(i * CHUNK, CHUNK), CHUNK)
        top = None
        for ref in (gate_ref, up_ref):
            for f in range(0, hidden, SLAB):
                value = jnp.abs(ref[0, f : f + SLAB, cols])
                top = value if top is None else jnp.maximum(top, value)
        peak_ref[0, :, cols] = jnp.max(top.astype(f32), axis=0, keepdims=True)
        return carry

    lax.fori_loop(0, depth // CHUNK, one, 0)


def channel_peak(gate, up):
    experts, hidden, depth = gate.shape
    spec = pl.BlockSpec((1, hidden, depth), lambda e: (e, 0, 0))
    return pl.pallas_call(
        channel_peak_kernel,
        grid=(experts,),
        out_shape=jax.ShapeDtypeStruct((experts, 1, depth), f32),
        in_specs=[spec, spec],
        out_specs=pl.BlockSpec((1, 1, depth), lambda e: (e, 0, 0)),
        compiler_params=params(),
        cost_estimate=BRIEF,
        name="channel_peak",
    )(gate, up)


def down_quant_kernel(rows, width, down_ref, level_ref, scale_ref):
    step = 8 * SLAB

    def peak(i, carry):
        base = pl.multiple_of(i * step, step)
        for j in range(0, step, SLAB):
            carry = jnp.maximum(carry, jnp.abs(down_ref[0, pl.ds(base + j, SLAB), :]))
        return carry

    top = lax.fori_loop(0, rows // step, peak, jnp.zeros((SLAB, width), bf16))
    top = jnp.max(top.astype(f32), axis=0, keepdims=True) + EPS
    scale_ref[0] = top / LEVELS
    inverse = jnp.broadcast_to(LEVELS / top, (SLAB, width))

    def quantize(i, carry):
        base = pl.multiple_of(i * step, step)
        for j in range(0, step, SLAB):
            value = down_ref[0, pl.ds(base + j, SLAB), :].astype(f32) * inverse
            level_ref[0, pl.ds(base + j, SLAB), :] = level_bf16(value)
        return carry

    lax.fori_loop(0, rows // step, quantize, 0)


def down_quant(down):
    experts, hidden, width = down.shape
    block = 512
    return pl.pallas_call(
        functools.partial(down_quant_kernel, hidden, block),
        grid=(experts, width // block),
        out_shape=(
            jax.ShapeDtypeStruct(down.shape, bf16),
            jax.ShapeDtypeStruct((experts, 1, width), f32),
        ),
        in_specs=[pl.BlockSpec((1, hidden, block), lambda e, c: (e, 0, c))],
        out_specs=(
            pl.BlockSpec((1, hidden, block), lambda e, c: (e, 0, c)),
            pl.BlockSpec((1, 1, block), lambda e, c: (e, 0, c)),
        ),
        compiler_params=params(),
        cost_estimate=BRIEF,
        name="down_levels",
    )(down)


def rows_kernel(local_experts, units, hot_ref, tokens_ref, peak_ref, rows_ref, smooth_ref):
    unit_rows = UNIT * CAP
    group_tokens, width = tokens_ref.shape[2], tokens_ref.shape[3]
    top = [None] * local_experts
    for u in range(units):
        tokens = tokens_ref[u * UNIT : (u + 1) * UNIT, 0].reshape(UNIT * group_tokens, width)
        picked = jnp.dot(hot_ref[u], tokens, preferred_element_type=f32)
        for e in range(local_experts):
            part = picked[e * unit_rows : (e + 1) * unit_rows]
            rows_ref[e, u * unit_rows : (u + 1) * unit_rows, :] = part.astype(bf16)
            most = jnp.max(jnp.abs(part), axis=0, keepdims=True)
            top[e] = most if top[e] is None else jnp.maximum(top[e], most)
    for e in range(local_experts):
        smooth_ref[e] = jnp.sqrt(jnp.maximum(top[e], 1.0) / (peak_ref[e : e + 1, :] + EPS))


def expert_rows(hot, tokens, weight_peak, local_experts, groups):
    shards, group_tokens, share = tokens.shape[1:]
    units = groups // UNIT
    block = 512
    per = share // block
    return pl.pallas_call(
        functools.partial(rows_kernel, local_experts, units),
        grid=(shards * per,),
        out_shape=(
            jax.ShapeDtypeStruct((local_experts, groups * CAP, shards * share), bf16),
            jax.ShapeDtypeStruct((local_experts, 1, shards * share), f32),
        ),
        in_specs=[
            pl.BlockSpec(hot.shape, lambda c: (0, 0, 0)),
            pl.BlockSpec((groups, 1, group_tokens, block), lambda c: (0, c // per, 0, c % per)),
            pl.BlockSpec((local_experts, block), lambda c: (0, c)),
        ],
        out_specs=(
            pl.BlockSpec((local_experts, groups * CAP, block), lambda c: (0, 0, c)),
            pl.BlockSpec((local_experts, 1, block), lambda c: (0, 0, c)),
        ),
        compiler_params=params(),
        name="expert_rows",
    )(hot, tokens, weight_peak)


def silu_product(both):
    half = both.shape[0] // 2
    gate, up = both[:half], both[half:]
    return flipped(gate / (1.0 + jnp.exp(-gate)) * up).astype(bf16)


def float_kernel(
    rows_ref, gate_ref, up_ref, smooth_ref,
    hidden_ref, inverse_w, scale_w, inverse_r, scale_r,
    smooth_s, unsmooth_s, top_s, top_r, acc,
):
    count = rows_ref.shape[1]
    hidden = gate_ref.shape[1]
    chunks = gate_ref.shape[2] // CHUNK
    weights = ((gate_ref, 0), (up_ref, hidden))

    smooth = smooth_ref[0]
    smooth_s[...] = jnp.broadcast_to(smooth, smooth_s.shape)
    unsmooth_s[...] = jnp.broadcast_to(1.0 / smooth, unsmooth_s.shape)
    top_s[...] = jnp.zeros_like(top_s)
    top_r[...] = jnp.zeros_like(top_r)
    acc[...] = jnp.zeros_like(acc)

    def peaks(i, carry):
        cols = pl.ds(pl.multiple_of(i * CHUNK, CHUNK), CHUNK)
        smooth_c = smooth_s[:, cols]
        unsmooth_c = unsmooth_s[:, cols]
        rows = rows_ref[0, :, cols]
        for ref, base in weights:
            acc[base : base + hidden, :] += dot_t(ref[0, :, cols], rows)
            for f in range(0, hidden, SLAB):
                value = jnp.abs(ref[0, f : f + SLAB, cols]).astype(f32) * smooth_c
                spot = slice(base + f, base + f + SLAB)
                top_s[spot, :] = jnp.maximum(top_s[spot, :], fold_max(value))
        for r in range(0, count, SLAB):
            value = jnp.abs(rows_ref[0, r : r + SLAB, cols]).astype(f32) * unsmooth_c
            top_r[r : r + SLAB, :] = jnp.maximum(top_r[r : r + SLAB, :], fold_max(value))
        return carry

    lax.fori_loop(0, chunks, peaks, 0)
    hidden_ref[0] = silu_product(acc[...])

    for r in range(0, count, SLAB):
        top = jnp.max(top_r[r : r + SLAB, :], axis=1, keepdims=True) + EPS
        inverse_r[0, r : r + SLAB, :] = jnp.broadcast_to(LEVELS / top, (SLAB, LANES))
        scale_r[0, r : r + SLAB, :] = jnp.broadcast_to(top / LEVELS, (SLAB, LANES))
    for f in range(0, 2 * hidden, LANES):
        top = jnp.max(top_s[f : f + LANES, :], axis=1, keepdims=True) + EPS
        inverse_w[0, f : f + LANES, :] = jnp.broadcast_to(LEVELS / top, (LANES, LANES))
        scale_w[0, f : f + LANES, :] = jnp.broadcast_to(top / LEVELS, (LANES, LANES))


def float_hidden(rows, gate, up, smooth):
    experts, count, depth = rows.shape
    hidden = gate.shape[1]

    def spec(*tail):
        return pl.BlockSpec((1,) + tail, lambda e: (e,) + (0,) * len(tail))

    tails = ((count, hidden), (2 * hidden, LANES), (2 * hidden, LANES), (count, LANES), (count, LANES))
    kinds = (bf16, f32, f32, f32, f32)
    return pl.pallas_call(
        float_kernel,
        grid=(experts,),
        out_shape=tuple(jax.ShapeDtypeStruct((experts,) + s, k) for s, k in zip(tails, kinds)),
        in_specs=[spec(count, depth), spec(hidden, depth), spec(hidden, depth), spec(1, depth)],
        out_specs=tuple(spec(*s) for s in tails),
        scratch_shapes=[
            pltpu.VMEM((SLAB, depth), f32),
            pltpu.VMEM((SLAB, depth), f32),
            pltpu.VMEM((2 * hidden, LANES), f32),
            pltpu.VMEM((count, LANES), f32),
            pltpu.VMEM((2 * hidden, count), f32),
        ],
        compiler_params=params(),
        cost_estimate=BRIEF,
        name="float_hidden",
    )(rows, gate, up, smooth)


def quant_kernel(
    rows_ref, gate_ref, up_ref, smooth_ref, inverse_w, scale_w, inverse_r, scale_r, hidden_ref,
    smooth_s, unsmooth_s, acc, levels, row_levels,
):
    count = rows_ref.shape[1]
    hidden = gate_ref.shape[1]
    chunks = gate_ref.shape[2] // CHUNK
    weights = ((gate_ref, 0), (up_ref, hidden))

    smooth = smooth_ref[0]
    smooth_s[...] = jnp.broadcast_to(smooth, smooth_s.shape)
    unsmooth_s[...] = jnp.broadcast_to(1.0 / smooth, unsmooth_s.shape)
    acc[...] = jnp.zeros_like(acc)

    def quantize(i, slot):
        cols = pl.ds(pl.multiple_of(i * CHUNK, CHUNK), CHUNK)
        smooth_c = smooth_s[:, cols]
        unsmooth_c = unsmooth_s[:, cols]
        for r in range(0, count, SLAB):
            value = rows_ref[0, r : r + SLAB, cols].astype(f32) * unsmooth_c
            value = value * wide(inverse_r[0, r : r + SLAB, :], CHUNK)
            level = level_mixed(value) * wide(scale_r[0, r : r + SLAB, :], CHUNK)
            row_levels[slot, r : r + SLAB, :] = level.astype(bf16)
        for ref, base in weights:
            for f in range(0, hidden, SLAB):
                value = ref[0, f : f + SLAB, cols].astype(f32) * smooth_c
                value = value * wide(inverse_w[0, base + f : base + f + SLAB, :], CHUNK)
                levels[slot, base + f : base + f + SLAB, :] = level_bf16(value)

    def multiply(slot):
        acc[...] += dot_t(levels[slot], row_levels[slot])

    quantize(0, 0)

    def pair(i, carry):
        multiply(0)
        quantize(2 * i + 1, 1)
        multiply(1)
        quantize(2 * i + 2, 0)
        return carry

    lax.fori_loop(0, chunks // 2 - 1, pair, 0)
    multiply(0)
    quantize(chunks - 1, 1)
    multiply(1)

    hidden_ref[0] = silu_product(acc[...] * scale_w[0][:, :1])


def quant_hidden(rows, gate, up, smooth, scales, first, amount):
    count, depth = rows.shape[1:]
    hidden = gate.shape[1]

    def spec(*tail):
        return pl.BlockSpec((1,) + tail, lambda e: (first + e,) + (0,) * len(tail))

    return pl.pallas_call(
        quant_kernel,
        grid=(amount,),
        out_shape=jax.ShapeDtypeStruct((amount, count, hidden), bf16),
        in_specs=[spec(*a.shape[1:]) for a in (rows, gate, up, smooth) + scales],
        out_specs=pl.BlockSpec((1, count, hidden), lambda e: (e, 0, 0)),
        scratch_shapes=[
            pltpu.VMEM((SLAB, depth), f32),
            pltpu.VMEM((SLAB, depth), f32),
            pltpu.VMEM((2 * hidden, count), f32),
            pltpu.VMEM((2, 2 * hidden, CHUNK), bf16),
            pltpu.VMEM((2, count, CHUNK), bf16),
        ],
        compiler_params=params(),
        cost_estimate=BRIEF,
        name="quant_hidden",
    )(rows, gate, up, smooth, *scales)


def combine_kernel(amounts, quantized, hot_ref, share_ref, *refs):
    parts = len(amounts)
    hidden_refs, down_ref, scale_ref = refs[:parts], refs[parts], refs[parts + 1]
    out_ref, wide_s, keep_s = refs[parts + 2 :]
    block, e = pl.program_id(0), pl.program_id(1)
    shards, _, count, part = hidden_refs[0].shape
    unit_rows = UNIT * CAP
    units = hot_ref.shape[0]
    first = 0
    for ref, amount in zip(hidden_refs, amounts):

        @pl.when((block == 0) & (e >= first) & (e < first + amount))
        def _(ref=ref):
            for r in range(0, count, SLAB):
                spot = slice(r, r + SLAB)
                if not quantized:
                    for s in range(shards):
                        wide_s[e, spot, s * part : (s + 1) * part] = ref[s, 0, spot, :]
                    continue
                top = None
                for s in range(shards):
                    value = fold_max(jnp.abs(ref[s, 0, spot, :]).astype(f32))
                    top = value if top is None else jnp.maximum(top, value)
                top = jnp.max(top, axis=1, keepdims=True) + EPS
                inverse, scale = LEVELS / top, top / LEVELS
                for s in range(shards):
                    value = level_mixed(ref[s, 0, spot, :].astype(f32) * inverse) * scale
                    wide_s[e, spot, s * part : (s + 1) * part] = value.astype(bf16)

        first += amount

    out = jnp.dot(wide_s[e], down_ref[0], preferred_element_type=f32) * scale_ref[0] * share_ref[0]
    at = pl.ds(pl.multiple_of(e * unit_rows, SLAB), unit_rows)
    for u in range(units):
        keep_s[u, at, :] = out[u * unit_rows : (u + 1) * unit_rows].astype(bf16)

    @pl.when(e == pl.num_programs(1) - 1)
    def _():
        tokens = hot_ref.shape[1]
        for u in range(units):
            out_ref[u * tokens : (u + 1) * tokens, :] = jnp.dot(
                hot_ref[u], keep_s[u], preferred_element_type=f32
            ).astype(bf16)


def combine(hot_t, share, hidden_parts, down, scale, quantized, at, pieces):
    units, unit_tokens, hot_rows = hot_t.shape
    shards, _, count, part = hidden_parts[0].shape
    experts, hidden, width = down.shape
    block = width // pieces
    amounts = tuple(h.shape[1] for h in hidden_parts)
    hidden_specs, first = [], 0
    for amount in amounts:

        def once(c, e, first=first, amount=amount):
            return (0, jnp.where(c == 0, jnp.clip(e - first, 0, amount - 1), amount - 1), 0, 0)

        hidden_specs.append(pl.BlockSpec((shards, 1, count, part), once))
        first += amount
    return pl.pallas_call(
        functools.partial(combine_kernel, amounts, quantized),
        grid=(1, experts),
        out_shape=jax.ShapeDtypeStruct((units * unit_tokens, block), bf16),
        in_specs=[
            pl.BlockSpec(hot_t.shape, lambda c, e: (0, 0, 0)),
            pl.BlockSpec((1, count, 1), lambda c, e: (e, 0, 0)),
            *hidden_specs,
            pl.BlockSpec((1, hidden, block), lambda c, e: (e, 0, at)),
            pl.BlockSpec((1, 1, block), lambda c, e: (e, 0, at)),
        ],
        out_specs=pl.BlockSpec((units * unit_tokens, block), lambda c, e: (0, 0)),
        scratch_shapes=[
            pltpu.VMEM((experts, count, hidden), bf16),
            pltpu.VMEM((units, hot_rows, block), bf16),
        ],
        compiler_params=params(),
        cost_estimate=BRIEF,
        name="combine_quant" if quantized else "combine_float",
    )(hot_t, share, *hidden_parts, down, scale)


def to_tokens(part, groups):
    width = part.shape[1]
    me = lax.axis_index("dp")
    pairs, low = groups // 2, me & 1
    part = part.reshape(pairs, 2, -1, width)
    kept = lax.dynamic_index_in_dim(part, low, 1, keepdims=False)
    sent = lax.dynamic_index_in_dim(part, 1 - low, 1, keepdims=False)
    came = lax.ppermute(sent, "dp", [(i, i ^ 1) for i in range(groups)])
    both = (kept.astype(f32) + came.astype(f32)).astype(bf16)
    high = me >> 1
    total = lax.dynamic_index_in_dim(both, high, 0, keepdims=False).astype(f32)
    for k in range(1, pairs):
        block = lax.dynamic_index_in_dim(both, lax.rem(high + k, pairs), 0, keepdims=False)
        came = lax.ppermute(block, "dp", [(i, (i + 2 * k) % groups) for i in range(groups)])
        total = total + came.astype(f32)
    return total


def from_all(x, axis):
    copies = jnp.broadcast_to(x, (lax.axis_size(axis),) + x.shape)
    return lax.all_to_all(copies, axis, split_axis=0, concat_axis=0)


def on_device(tokens, expert_ids, route_weights, gate_weight, up_weight, down_weight):
    groups = lax.axis_size("dp")
    experts = gate_weight.shape[0]
    choices = expert_ids.shape[1]

    payload = jnp.concatenate([expert_ids.T.astype(f32), route_weights.T], axis=0)
    route = from_all(payload, "dp").reshape(-1, payload.shape[1])
    all_tokens = lax.all_gather(tokens, ("dp", "expert"), axis=0)
    all_tokens = all_tokens.reshape((groups, -1) + tokens.shape)

    local_peak = channel_peak(gate_weight, up_weight)
    weight_peak = from_all(local_peak.reshape(experts, -1).astype(bf16), "expert")
    weight_peak = jnp.max(weight_peak, axis=0).astype(f32)
    down_weight, local_peak = lax.optimization_barrier((down_weight, local_peak))
    levels, level_scale = down_quant(down_weight)

    first = (lax.axis_index("dp") * experts).astype(jnp.int32).reshape(1)
    hot, share = prep(first, route, experts, groups, choices)
    hot_t = jnp.swapaxes(hot, 1, 2)
    hot, levels = lax.optimization_barrier((hot, levels))
    rows, smooth = expert_rows(hot, all_tokens, weight_peak, experts, groups)

    hf, *scales = float_hidden(rows, gate_weight, up_weight, smooth)
    scales = tuple(scales)
    wide_f = lax.all_gather(hf, "expert", axis=0)

    amounts = [experts // 2, experts - experts // 2]
    wide_q, start, out_f = [], 0, None
    for p, amount in enumerate(a for a in amounts if a):
        hq = quant_hidden(rows, gate_weight, up_weight, smooth, scales, start, amount)
        start += amount
        wide_q.append(lax.all_gather(hq, "expert", axis=0))
        if p == 0:
            hq, wide_f = lax.optimization_barrier((hq, wide_f))
            part_f = combine(
                hot_t, share, [wide_f], down_weight, jnp.ones_like(level_scale), False, 0, 1
            )
            out_f = to_tokens(part_f, groups)
            rows, part_f = lax.optimization_barrier((rows, part_f))
    out_q = []
    for at in range(2):
        part_q = combine(hot_t, share, wide_q, levels, level_scale, True, at, 2)
        out_q.append(to_tokens(part_q, groups).astype(bf16))
        wide_q[0], part_q = lax.optimization_barrier((wide_q[0], part_q))
    return jnp.concatenate(out_q, axis=1), out_f


def solution(mesh):
    in_specs = (
        P("dp", "expert"),
        P("dp", None),
        P("dp", None),
        P("dp", "expert", None),
        P("dp", "expert", None),
        P("dp", None, "expert"),
    )
    out_specs = (P("dp", "expert"), P("dp", "expert"))
    return jax.shard_map(
        on_device, mesh=mesh, in_specs=in_specs, out_specs=out_specs, check_vma=False
    )
```

```python
import functools

import jax
import jax.numpy as jnp
from jax import lax
from jax.experimental import pallas as pl
from jax.experimental.pallas import tpu as pltpu
from jax.sharding import PartitionSpec as P

CAP = 20
UNIT = 4
LEVELS = 7.0
EPS = 1e-06
VMEM = 56 * 1024 * 1024
LANES = 128
SLAB = 16
CHUNK = 1024
BRIEF = pl.CostEstimate(flops=1, bytes_accessed=1, transcendentals=0)

FRACTION_BF16 = (6.55787162, -12.52307356, 9.17209913)

bf16 = jnp.bfloat16
f32 = jnp.float32


def fraction(r, coefficients):
    dtype = r.dtype
    square = r * r
    total = jnp.asarray(coefficients[-1], dtype)
    for c in coefficients[-2::-1]:
        total = total * square + jnp.asarray(c, dtype)
    return (r * square) * total


def level_bf16(v):
    n = jnp.round(v)
    r = (v - n).astype(bf16)
    return n.astype(bf16) + fraction(r, FRACTION_BF16)


def level_mixed(v):
    n = jnp.round(v)
    return n + fraction((v - n).astype(bf16), FRACTION_BF16).astype(f32)


def fold_max(x):
    if x.shape[1] % LANES:
        return jnp.max(x, axis=1, keepdims=True)
    out = x[:, :LANES]
    for c in range(LANES, x.shape[1], LANES):
        out = jnp.maximum(out, x[:, c : c + LANES])
    return out


def wide(x, width):
    return jnp.concatenate([x] * (width // LANES), axis=1)


def dot_t(a, b):
    return lax.dot_general(a, b, (((1,), (1,)), ((), ())), preferred_element_type=f32)


def flipped(x):
    high, broad = -x.shape[0] % LANES, -x.shape[1] % LANES
    return jnp.pad(x, ((0, high), (0, broad))).T[: x.shape[1], : x.shape[0]]


def params():
    return pltpu.CompilerParams(vmem_limit_bytes=VMEM)


def prep_kernel(local_experts, groups, choices, first_ref, route_ref, hot_ref, share_ref):
    units = groups // UNIT
    group_tokens = route_ref.shape[1]
    unit_rows, unit_tokens = UNIT * CAP, UNIT * group_tokens
    first = first_ref[0].astype(f32)
    before = lax.broadcasted_iota(jnp.int32, (group_tokens, group_tokens), 0) < lax.broadcasted_iota(
        jnp.int32, (group_tokens, group_tokens), 1
    )
    before = jnp.where(before, 1.0, 0.0).astype(bf16)
    codes, weights = [], []
    for g in range(groups):
        base = 2 * choices * g
        ids = route_ref[base : base + choices, :]
        route = route_ref[base + choices : base + 2 * choices, :]
        shares = route / jnp.sum(route, axis=0, keepdims=True)
        hits, mine = [], []
        for e in range(local_experts):
            hit = ids == first + float(e)
            hits.append(jnp.max(jnp.where(hit, 1.0, 0.0), axis=0, keepdims=True))
            mine.append(jnp.sum(jnp.where(hit, shares, 0.0), axis=0, keepdims=True))
        part = jnp.concatenate(hits, axis=0)
        weights.append(jnp.concatenate(mine, axis=0))
        slot = jnp.dot(part.astype(bf16), before, preferred_element_type=f32)
        codes.append(jnp.where(part > 0.5, slot + float((g % UNIT) * CAP), -1.0))
    row = lax.broadcasted_iota(jnp.int32, (unit_rows, unit_tokens), 0).astype(f32)
    for u in range(units):
        code = jnp.concatenate(codes[u * UNIT : (u + 1) * UNIT], axis=1)
        weight = jnp.concatenate(weights[u * UNIT : (u + 1) * UNIT], axis=1)
        for e in range(local_experts):
            hot = row == code[e : e + 1, :]
            hot_ref[u, e * unit_rows : (e + 1) * unit_rows, :] = jnp.where(hot, 1.0, 0.0).astype(bf16)
            share_ref[e, u * unit_rows : (u + 1) * unit_rows, :] = jnp.sum(
                jnp.where(hot, weight[e : e + 1, :], 0.0), axis=1, keepdims=True
            )


def prep(first, route, local_experts, groups, choices):
    units = groups // UNIT
    return pl.pallas_call(
        functools.partial(prep_kernel, local_experts, groups, choices),
        out_shape=(
            jax.ShapeDtypeStruct((units, local_experts * UNIT * CAP, UNIT * route.shape[1]), bf16),
            jax.ShapeDtypeStruct((local_experts, groups * CAP, 1), f32),
        ),
        in_specs=[
            pl.BlockSpec(memory_space=pltpu.SMEM),
            pl.BlockSpec(memory_space=pltpu.VMEM),
        ],
        out_specs=(pl.BlockSpec(memory_space=pltpu.VMEM), pl.BlockSpec(memory_space=pltpu.VMEM)),
        compiler_params=params(),
        name="routing_tables",
    )(first, route)


def channel_peak_kernel(gate_ref, up_ref, peak_ref):
    hidden, depth = gate_ref.shape[1:]

    def one(i, carry):
        cols = pl.ds(pl.multiple_of(i * CHUNK, CHUNK), CHUNK)
        top = None
        for ref in (gate_ref, up_ref):
            for f in range(0, hidden, SLAB):
                value = jnp.abs(ref[0, f : f + SLAB, cols])
                top = value if top is None else jnp.maximum(top, value)
        peak_ref[0, :, cols] = jnp.max(top.astype(f32), axis=0, keepdims=True)
        return carry

    lax.fori_loop(0, depth // CHUNK, one, 0)


def channel_peak(gate, up):
    experts, hidden, depth = gate.shape
    spec = pl.BlockSpec((1, hidden, depth), lambda e: (e, 0, 0))
    return pl.pallas_call(
        channel_peak_kernel,
        grid=(experts,),
        out_shape=jax.ShapeDtypeStruct((experts, 1, depth), f32),
        in_specs=[spec, spec],
        out_specs=pl.BlockSpec((1, 1, depth), lambda e: (e, 0, 0)),
        compiler_params=params(),
        cost_estimate=BRIEF,
        name="channel_peak",
    )(gate, up)


def down_quant_kernel(rows, width, down_ref, level_ref, scale_ref):
    step = 8 * SLAB

    def peak(i, carry):
        base = pl.multiple_of(i * step, step)
        for j in range(0, step, SLAB):
            carry = jnp.maximum(carry, jnp.abs(down_ref[0, pl.ds(base + j, SLAB), :]))
        return carry

    top = lax.fori_loop(0, rows // step, peak, jnp.zeros((SLAB, width), bf16))
    top = jnp.max(top.astype(f32), axis=0, keepdims=True) + EPS
    scale_ref[0] = top / LEVELS
    inverse = jnp.broadcast_to(LEVELS / top, (SLAB, width))

    def quantize(i, carry):
        base = pl.multiple_of(i * step, step)
        for j in range(0, step, SLAB):
            value = down_ref[0, pl.ds(base + j, SLAB), :].astype(f32) * inverse
            level_ref[0, pl.ds(base + j, SLAB), :] = level_bf16(value)
        return carry

    lax.fori_loop(0, rows // step, quantize, 0)


def down_quant(down):
    experts, hidden, width = down.shape
    block = 512
    return pl.pallas_call(
        functools.partial(down_quant_kernel, hidden, block),
        grid=(experts, width // block),
        out_shape=(
            jax.ShapeDtypeStruct(down.shape, bf16),
            jax.ShapeDtypeStruct((experts, 1, width), f32),
        ),
        in_specs=[pl.BlockSpec((1, hidden, block), lambda e, c: (e, 0, c))],
        out_specs=(
            pl.BlockSpec((1, hidden, block), lambda e, c: (e, 0, c)),
            pl.BlockSpec((1, 1, block), lambda e, c: (e, 0, c)),
        ),
        compiler_params=params(),
        cost_estimate=BRIEF,
        name="down_levels",
    )(down)


def rows_kernel(local_experts, units, hot_ref, tokens_ref, peak_ref, rows_ref, smooth_ref):
    unit_rows = UNIT * CAP
    group_tokens, width = tokens_ref.shape[2], tokens_ref.shape[3]
    top = [None] * local_experts
    for u in range(units):
        tokens = tokens_ref[u * UNIT : (u + 1) * UNIT, 0].reshape(UNIT * group_tokens, width)
        picked = jnp.dot(hot_ref[u], tokens, preferred_element_type=f32)
        for e in range(local_experts):
            part = picked[e * unit_rows : (e + 1) * unit_rows]
            rows_ref[e, u * unit_rows : (u + 1) * unit_rows, :] = part.astype(bf16)
            most = jnp.max(jnp.abs(part), axis=0, keepdims=True)
            top[e] = most if top[e] is None else jnp.maximum(top[e], most)
    for e in range(local_experts):
        smooth_ref[e] = jnp.sqrt(jnp.maximum(top[e], 1.0) / (peak_ref[e : e + 1, :] + EPS))


def expert_rows(hot, tokens, weight_peak, local_experts, groups):
    shards, group_tokens, share = tokens.shape[1:]
    units = groups // UNIT
    block = 512
    per = share // block
    return pl.pallas_call(
        functools.partial(rows_kernel, local_experts, units),
        grid=(shards * per,),
        out_shape=(
            jax.ShapeDtypeStruct((local_experts, groups * CAP, shards * share), bf16),
            jax.ShapeDtypeStruct((local_experts, 1, shards * share), f32),
        ),
        in_specs=[
            pl.BlockSpec(hot.shape, lambda c: (0, 0, 0)),
            pl.BlockSpec((groups, 1, group_tokens, block), lambda c: (0, c // per, 0, c % per)),
            pl.BlockSpec((local_experts, block), lambda c: (0, c)),
        ],
        out_specs=(
            pl.BlockSpec((local_experts, groups * CAP, block), lambda c: (0, 0, c)),
            pl.BlockSpec((local_experts, 1, block), lambda c: (0, 0, c)),
        ),
        compiler_params=params(),
        name="expert_rows",
    )(hot, tokens, weight_peak)


def silu_product(both):
    half = both.shape[0] // 2
    gate, up = both[:half], both[half:]
    return flipped(gate / (1.0 + jnp.exp(-gate)) * up).astype(bf16)


def float_kernel(
    rows_ref, gate_ref, up_ref, smooth_ref,
    hidden_ref, inverse_w, scale_w, inverse_r, scale_r,
    smooth_s, unsmooth_s, top_s, top_r, acc,
):
    count = rows_ref.shape[1]
    hidden = gate_ref.shape[1]
    chunks = gate_ref.shape[2] // CHUNK
    weights = ((gate_ref, 0), (up_ref, hidden))

    smooth = smooth_ref[0]
    smooth_s[...] = jnp.broadcast_to(smooth, smooth_s.shape)
    unsmooth_s[...] = jnp.broadcast_to(1.0 / smooth, unsmooth_s.shape)
    top_s[...] = jnp.zeros_like(top_s)
    top_r[...] = jnp.zeros_like(top_r)
    acc[...] = jnp.zeros_like(acc)

    def peaks(i, carry):
        cols = pl.ds(pl.multiple_of(i * CHUNK, CHUNK), CHUNK)
        smooth_c = smooth_s[:, cols]
        unsmooth_c = unsmooth_s[:, cols]
        rows = rows_ref[0, :, cols]
        for ref, base in weights:
            acc[base : base + hidden, :] += dot_t(ref[0, :, cols], rows)
            for f in range(0, hidden, SLAB):
                value = jnp.abs(ref[0, f : f + SLAB, cols]).astype(f32) * smooth_c
                spot = slice(base + f, base + f + SLAB)
                top_s[spot, :] = jnp.maximum(top_s[spot, :], fold_max(value))
        for r in range(0, count, SLAB):
            value = jnp.abs(rows_ref[0, r : r + SLAB, cols]).astype(f32) * unsmooth_c
            top_r[r : r + SLAB, :] = jnp.maximum(top_r[r : r + SLAB, :], fold_max(value))
        return carry

    lax.fori_loop(0, chunks, peaks, 0)
    hidden_ref[0] = silu_product(acc[...])

    for r in range(0, count, SLAB):
        top = jnp.max(top_r[r : r + SLAB, :], axis=1, keepdims=True) + EPS
        inverse_r[0, r : r + SLAB, :] = jnp.broadcast_to(LEVELS / top, (SLAB, LANES))
        scale_r[0, r : r + SLAB, :] = jnp.broadcast_to(top / LEVELS, (SLAB, LANES))
    for f in range(0, 2 * hidden, LANES):
        top = jnp.max(top_s[f : f + LANES, :], axis=1, keepdims=True) + EPS
        inverse_w[0, f : f + LANES, :] = jnp.broadcast_to(LEVELS / top, (LANES, LANES))
        scale_w[0, f : f + LANES, :] = jnp.broadcast_to(top / LEVELS, (LANES, LANES))


def float_hidden(rows, gate, up, smooth):
    experts, count, depth = rows.shape
    hidden = gate.shape[1]

    def spec(*tail):
        return pl.BlockSpec((1,) + tail, lambda e: (e,) + (0,) * len(tail))

    tails = ((count, hidden), (2 * hidden, LANES), (2 * hidden, LANES), (count, LANES), (count, LANES))
    kinds = (bf16, f32, f32, f32, f32)
    return pl.pallas_call(
        float_kernel,
        grid=(experts,),
        out_shape=tuple(jax.ShapeDtypeStruct((experts,) + s, k) for s, k in zip(tails, kinds)),
        in_specs=[spec(count, depth), spec(hidden, depth), spec(hidden, depth), spec(1, depth)],
        out_specs=tuple(spec(*s) for s in tails),
        scratch_shapes=[
            pltpu.VMEM((SLAB, depth), f32),
            pltpu.VMEM((SLAB, depth), f32),
            pltpu.VMEM((2 * hidden, LANES), f32),
            pltpu.VMEM((count, LANES), f32),
            pltpu.VMEM((2 * hidden, count), f32),
        ],
        compiler_params=params(),
        cost_estimate=BRIEF,
        name="float_hidden",
    )(rows, gate, up, smooth)


def quant_kernel(
    rows_ref, gate_ref, up_ref, smooth_ref, inverse_w, scale_w, inverse_r, scale_r, *refs
):
    hidden_ref, smooth_s, unsmooth_s, acc, levels, row_levels = refs[-6:]
    count = rows_ref.shape[1]
    hidden = gate_ref.shape[1]
    chunks = gate_ref.shape[2] // CHUNK
    weights = ((gate_ref, 0), (up_ref, hidden))

    smooth = smooth_ref[0]
    smooth_s[...] = jnp.broadcast_to(smooth, smooth_s.shape)
    unsmooth_s[...] = jnp.broadcast_to(1.0 / smooth, unsmooth_s.shape)
    acc[...] = jnp.zeros_like(acc)

    def quantize(i, slot):
        cols = pl.ds(pl.multiple_of(i * CHUNK, CHUNK), CHUNK)
        smooth_c = smooth_s[:, cols]
        unsmooth_c = unsmooth_s[:, cols]
        for r in range(0, count, SLAB):
            value = rows_ref[0, r : r + SLAB, cols].astype(f32) * unsmooth_c
            value = value * wide(inverse_r[0, r : r + SLAB, :], CHUNK)
            level = level_mixed(value) * wide(scale_r[0, r : r + SLAB, :], CHUNK)
            row_levels[slot, r : r + SLAB, :] = level.astype(bf16)
        for ref, base in weights:
            for f in range(0, hidden, SLAB):
                value = ref[0, f : f + SLAB, cols].astype(f32) * smooth_c
                value = value * wide(inverse_w[0, base + f : base + f + SLAB, :], CHUNK)
                levels[slot, base + f : base + f + SLAB, :] = level_bf16(value)

    def multiply(slot):
        acc[...] += dot_t(levels[slot], row_levels[slot])

    quantize(0, 0)

    def pair(i, carry):
        multiply(0)
        quantize(2 * i + 1, 1)
        multiply(1)
        quantize(2 * i + 2, 0)
        return carry

    lax.fori_loop(0, chunks // 2 - 1, pair, 0)
    multiply(0)
    quantize(chunks - 1, 1)
    multiply(1)

    hidden_ref[0] = silu_product(acc[...] * scale_w[0][:, :1])


def quant_hidden(rows, gate, up, smooth, scales, first, amount, space, at, into=None):
    count, depth = rows.shape[1:]
    hidden = gate.shape[1]
    extra = [] if into is None else [into]

    def spec(*tail):
        return pl.BlockSpec((1,) + tail, lambda e: (first + e,) + (0,) * len(tail))

    return pl.pallas_call(
        quant_kernel,
        grid=(amount,),
        out_shape=jax.ShapeDtypeStruct((space, count, hidden), bf16),
        in_specs=[spec(*a.shape[1:]) for a in (rows, gate, up, smooth) + scales]
        + [pl.BlockSpec(memory_space=pl.ANY)] * len(extra),
        out_specs=pl.BlockSpec((1, count, hidden), lambda e: (at + e, 0, 0)),
        input_output_aliases={8: 0} if extra else {},
        scratch_shapes=[
            pltpu.VMEM((SLAB, depth), f32),
            pltpu.VMEM((SLAB, depth), f32),
            pltpu.VMEM((2 * hidden, count), f32),
            pltpu.VMEM((2, 2 * hidden, CHUNK), bf16),
            pltpu.VMEM((2, count, CHUNK), bf16),
        ],
        compiler_params=params(),
        cost_estimate=BRIEF,
        name="quant_hidden",
    )(rows, gate, up, smooth, *scales, *extra)


def combine_kernel(quantized, skip, last, *refs):
    share_ref, hidden_ref, down_ref, scale_ref = refs[:4]
    e = pl.program_id(0)
    shards, _, count, part = hidden_ref.shape
    unit_rows = UNIT * CAP
    wide_s = refs[-1]
    for r in range(0, count, SLAB):
        spot = slice(r, r + SLAB)
        if not quantized:
            for s in range(shards):
                wide_s[spot, s * part : (s + 1) * part] = hidden_ref[s, 0, spot, :]
            continue
        top = None
        for s in range(shards):
            value = fold_max(jnp.abs(hidden_ref[s, 0, spot, :]).astype(f32))
            top = value if top is None else jnp.maximum(top, value)
        top = jnp.max(top, axis=1, keepdims=True) + EPS
        inverse, scale = LEVELS / top, top / LEVELS
        for s in range(shards):
            value = level_mixed(hidden_ref[s, 0, spot, :].astype(f32) * inverse) * scale
            wide_s[spot, s * part : (s + 1) * part] = value.astype(bf16)

    out = jnp.dot(wide_s[...], down_ref[0], preferred_element_type=f32) * scale_ref[0] * share_ref[0]
    out = out.astype(bf16)
    units = count // unit_rows
    if not last:
        for u in range(units):
            refs[-2][u] = out[u * unit_rows : (u + 1) * unit_rows]
        return
    hot_ref, out_ref, keep_s = refs[4], refs[-3], refs[-2]
    if skip:

        @pl.when(e == 0)
        def _():
            keep_s[:, : skip * unit_rows, :] = refs[5][...]

    at = pl.ds(pl.multiple_of((skip + e) * unit_rows, SLAB), unit_rows)
    for u in range(units):
        keep_s[u, at, :] = out[u * unit_rows : (u + 1) * unit_rows]

    @pl.when(e == pl.num_programs(0) - 1)
    def _():
        tokens = hot_ref.shape[1]
        for u in range(units):
            out_ref[u * tokens : (u + 1) * tokens, :] = jnp.dot(
                hot_ref[u], keep_s[u], preferred_element_type=f32
            ).astype(bf16)


def combine(hot_t, share, hidden, down, scale, quantized, first=0, at=0, pieces=1, last=True, earlier=None):
    units, unit_tokens, hot_rows = hot_t.shape
    shards, amount, count, part = hidden.shape
    units_hidden, width = down.shape[1:]
    block = width // pieces
    unit_rows = UNIT * CAP
    in_specs = [
        pl.BlockSpec((1, count, 1), lambda e: (first + e, 0, 0)),
        pl.BlockSpec((shards, 1, count, part), lambda e: (0, e, 0, 0)),
        pl.BlockSpec((1, units_hidden, block), lambda e: (first + e, 0, at)),
        pl.BlockSpec((1, 1, block), lambda e: (first + e, 0, at)),
    ]
    operands = [share, hidden, down, scale]
    scratch = [pltpu.VMEM((count, units_hidden), bf16)]
    if last:
        operands.append(hot_t)
        in_specs.append(pl.BlockSpec(hot_t.shape, lambda e: (0, 0, 0)))
        scratch = [pltpu.VMEM((units, hot_rows, block), bf16)] + scratch
        out_shape = jax.ShapeDtypeStruct((units * unit_tokens, block), bf16)
        out_spec = pl.BlockSpec((units * unit_tokens, block), lambda e: (0, 0))
        if first:
            operands.append(earlier)
            in_specs.append(pl.BlockSpec((units, first * unit_rows, block), lambda e: (0, 0, at)))
    else:
        out_shape = jax.ShapeDtypeStruct((units, amount * unit_rows, block), bf16)
        out_spec = pl.BlockSpec((units, unit_rows, block), lambda e: (0, e, 0))
    return pl.pallas_call(
        functools.partial(combine_kernel, quantized, first, last),
        grid=(amount,),
        out_shape=out_shape,
        in_specs=in_specs,
        out_specs=out_spec,
        scratch_shapes=scratch,
        compiler_params=params(),
        cost_estimate=BRIEF,
        name="combine_quant" if quantized else "combine_float",
    )(*operands)


def to_pairs(part, groups):
    width = part.shape[1]
    low = lax.axis_index("dp") & 1
    part = part.reshape(groups // 2, 2, -1, width)
    kept = lax.dynamic_index_in_dim(part, low, 1, keepdims=False)
    sent = lax.dynamic_index_in_dim(part, 1 - low, 1, keepdims=False)
    came = lax.ppermute(sent, "dp", [(i, i ^ 1) for i in range(groups)])
    return (kept.astype(f32) + came.astype(f32)).astype(bf16)


def to_tokens(both, groups):
    pairs = groups // 2
    high = lax.axis_index("dp") >> 1
    total = lax.dynamic_index_in_dim(both, high, 0, keepdims=False).astype(f32)
    for k in range(1, pairs):
        block = lax.dynamic_index_in_dim(both, lax.rem(high + k, pairs), 0, keepdims=False)
        came = lax.ppermute(block, "dp", [(i, (i + 2 * k) % groups) for i in range(groups)])
        total = total + came.astype(f32)
    return total


def from_all(x, axis):
    copies = jnp.broadcast_to(x, (lax.axis_size(axis),) + x.shape)
    return lax.all_to_all(copies, axis, split_axis=0, concat_axis=0)


def on_device(tokens, expert_ids, route_weights, gate_weight, up_weight, down_weight):
    groups = lax.axis_size("dp")
    experts = gate_weight.shape[0]
    choices = expert_ids.shape[1]

    payload = jnp.concatenate([expert_ids.T.astype(f32), route_weights.T], axis=0)
    route = from_all(payload, "dp").reshape(-1, payload.shape[1])
    all_tokens = lax.all_gather(tokens, ("dp", "expert"), axis=0)
    all_tokens = all_tokens.reshape((groups, -1) + tokens.shape)

    local_peak = channel_peak(gate_weight, up_weight)
    weight_peak = from_all(local_peak.reshape(experts, -1).astype(bf16), "expert")
    weight_peak = jnp.max(weight_peak, axis=0).astype(f32)
    down_weight, local_peak = lax.optimization_barrier((down_weight, local_peak))
    levels, level_scale = down_quant(down_weight)

    first = (lax.axis_index("dp") * experts).astype(jnp.int32).reshape(1)
    hot, share = prep(first, route, experts, groups, choices)
    hot_t = jnp.swapaxes(hot, 1, 2)
    hot, levels = lax.optimization_barrier((hot, levels))
    rows, smooth = expert_rows(hot, all_tokens, weight_peak, experts, groups)

    hf, *scales = float_hidden(rows, gate_weight, up_weight, smooth)
    scales = tuple(scales)
    wide_f = lax.all_gather(hf, "expert", axis=0)

    half = experts // 2
    more = experts - half
    some = (3 * more) // 4
    operands = (gate_weight, up_weight, smooth, scales)
    hq = quant_hidden(rows, *operands, 0, half, half, 0)
    wide_q = [lax.all_gather(hq, "expert", axis=0)]
    wide_f, hq = lax.optimization_barrier((wide_f, hq))
    part_f = combine(hot_t, share, wide_f, down_weight, jnp.ones_like(level_scale), False)
    both_f = to_pairs(part_f, groups)
    rows, part_f = lax.optimization_barrier((rows, part_f))
    hq = quant_hidden(rows, *operands, half, some, more, 0) if some else None
    rows, both_f = lax.optimization_barrier((rows, both_f))
    out_f = to_tokens(both_f, groups)
    hq = quant_hidden(rows, *operands, half + some, more - some, more, some, hq)
    wide_q.append(lax.all_gather(hq, "expert", axis=0))
    share, hq = lax.optimization_barrier((share, hq))
    earlier = combine(hot_t, share, wide_q[0], levels, level_scale, True, last=False)
    earlier, out_f = lax.optimization_barrier((earlier, out_f))
    out_q = []
    for at in range(2):
        part_q = combine(
            hot_t, share, wide_q[1], levels, level_scale, True, half, at, 2, earlier=earlier
        )
        out_q.append(to_tokens(to_pairs(part_q, groups), groups).astype(bf16))
        earlier, part_q = lax.optimization_barrier((earlier, part_q))
    return jnp.concatenate(out_q, axis=1), out_f


def solution(mesh):
    in_specs = (
        P("dp", "expert"),
        P("dp", None),
        P("dp", None),
        P("dp", "expert", None),
        P("dp", "expert", None),
        P("dp", None, "expert"),
    )
    out_specs = (P("dp", "expert"), P("dp", "expert"))
    return jax.shard_map(
        on_device, mesh=mesh, in_specs=in_specs, out_specs=out_specs, check_vma=False
    )
```

```python
import functools

import jax
import jax.numpy as jnp
from jax import lax
from jax.experimental import pallas as pl
from jax.experimental.pallas import tpu as pltpu
from jax.sharding import PartitionSpec as P

CAP = 20
UNIT = 4
LEVELS = 7.0
EPS = 1e-06
VMEM = 56 * 1024 * 1024
LANES = 128
SLAB = 16
SPACING_ONE = 1.5 * 2.0**23
HALVES = 2
CHUNK = 1024
BRIEF = pl.CostEstimate(flops=1, bytes_accessed=1, transcendentals=0)

FRACTION_BF16 = (6.55787162, -12.52307356, 9.17209913)

bf16 = jnp.bfloat16
f32 = jnp.float32


def fraction(r, coefficients):
    dtype = r.dtype
    square = r * r
    total = jnp.asarray(coefficients[-1], dtype)
    for c in coefficients[-2::-1]:
        total = total * square + jnp.asarray(c, dtype)
    return (r * square) * total


def nearest(v):
    return (v + SPACING_ONE) - SPACING_ONE


def level_bf16(v):
    n = nearest(v)
    r = (v - n).astype(bf16)
    return n.astype(bf16) + fraction(r, FRACTION_BF16)


def level_mixed(v):
    n = nearest(v)
    return n + fraction((v - n).astype(bf16), FRACTION_BF16).astype(f32)


def fold_max(x):
    if x.shape[1] % LANES:
        return jnp.max(x, axis=1, keepdims=True)
    out = x[:, :LANES]
    for c in range(LANES, x.shape[1], LANES):
        out = jnp.maximum(out, x[:, c : c + LANES])
    return out


def wide(x, width):
    return jnp.concatenate([x] * (width // LANES), axis=1)


def dot_t(a, b):
    return lax.dot_general(a, b, (((1,), (1,)), ((), ())), preferred_element_type=f32)


def flipped(x):
    high, broad = -x.shape[0] % LANES, -x.shape[1] % LANES
    return jnp.pad(x, ((0, high), (0, broad))).T[: x.shape[1], : x.shape[0]]


def params():
    return pltpu.CompilerParams(vmem_limit_bytes=VMEM)


def prep_kernel(local_experts, groups, choices, first_ref, route_ref, hot_ref, share_ref):
    units = groups // UNIT
    group_tokens = route_ref.shape[1]
    unit_rows, unit_tokens = UNIT * CAP, UNIT * group_tokens
    first = first_ref[0].astype(f32)
    before = lax.broadcasted_iota(jnp.int32, (group_tokens, group_tokens), 0) < lax.broadcasted_iota(
        jnp.int32, (group_tokens, group_tokens), 1
    )
    before = jnp.where(before, 1.0, 0.0).astype(bf16)
    codes, weights = [], []
    for g in range(groups):
        base = 2 * choices * g
        ids = route_ref[base : base + choices, :]
        route = route_ref[base + choices : base + 2 * choices, :]
        shares = route / jnp.sum(route, axis=0, keepdims=True)
        hits, mine = [], []
        for e in range(local_experts):
            hit = ids == first + float(e)
            hits.append(jnp.max(jnp.where(hit, 1.0, 0.0), axis=0, keepdims=True))
            mine.append(jnp.sum(jnp.where(hit, shares, 0.0), axis=0, keepdims=True))
        part = jnp.concatenate(hits, axis=0)
        weights.append(jnp.concatenate(mine, axis=0))
        slot = jnp.dot(part.astype(bf16), before, preferred_element_type=f32)
        codes.append(jnp.where(part > 0.5, slot + float((g % UNIT) * CAP), -1.0))
    row = lax.broadcasted_iota(jnp.int32, (unit_rows, unit_tokens), 0).astype(f32)
    for u in range(units):
        code = jnp.concatenate(codes[u * UNIT : (u + 1) * UNIT], axis=1)
        weight = jnp.concatenate(weights[u * UNIT : (u + 1) * UNIT], axis=1)
        for e in range(local_experts):
            hot = row == code[e : e + 1, :]
            hot_ref[u, e * unit_rows : (e + 1) * unit_rows, :] = jnp.where(hot, 1.0, 0.0).astype(bf16)
            share_ref[e, u * unit_rows : (u + 1) * unit_rows, :] = jnp.sum(
                jnp.where(hot, weight[e : e + 1, :], 0.0), axis=1, keepdims=True
            )


def prep(first, route, local_experts, groups, choices):
    units = groups // UNIT
    return pl.pallas_call(
        functools.partial(prep_kernel, local_experts, groups, choices),
        out_shape=(
            jax.ShapeDtypeStruct((units, local_experts * UNIT * CAP, UNIT * route.shape[1]), bf16),
            jax.ShapeDtypeStruct((local_experts, groups * CAP, 1), f32),
        ),
        in_specs=[
            pl.BlockSpec(memory_space=pltpu.SMEM),
            pl.BlockSpec(memory_space=pltpu.VMEM),
        ],
        out_specs=(pl.BlockSpec(memory_space=pltpu.VMEM), pl.BlockSpec(memory_space=pltpu.VMEM)),
        compiler_params=params(),
        name="routing_tables",
    )(first, route)


def channel_peak_kernel(gate_ref, up_ref, peak_ref):
    hidden, depth = gate_ref.shape[1:]

    def one(i, carry):
        cols = pl.ds(pl.multiple_of(i * CHUNK, CHUNK), CHUNK)
        top = None
        for ref in (gate_ref, up_ref):
            for f in range(0, hidden, SLAB):
                value = jnp.abs(ref[0, f : f + SLAB, cols])
                top = value if top is None else jnp.maximum(top, value)
        peak_ref[0, :, cols] = jnp.max(top.astype(f32), axis=0, keepdims=True)
        return carry

    lax.fori_loop(0, depth // CHUNK, one, 0)


def channel_peak(gate, up):
    experts, hidden, depth = gate.shape
    spec = pl.BlockSpec((1, hidden, depth), lambda e: (e, 0, 0))
    return pl.pallas_call(
        channel_peak_kernel,
        grid=(experts,),
        out_shape=jax.ShapeDtypeStruct((experts, 1, depth), f32),
        in_specs=[spec, spec],
        out_specs=pl.BlockSpec((1, 1, depth), lambda e: (e, 0, 0)),
        compiler_params=params(),
        cost_estimate=BRIEF,
        name="channel_peak",
    )(gate, up)


def down_quant_kernel(rows, width, down_ref, level_ref, scale_ref):
    step = 8 * SLAB

    def peak(i, carry):
        base = pl.multiple_of(i * step, step)
        for j in range(0, step, SLAB):
            carry = jnp.maximum(carry, jnp.abs(down_ref[0, pl.ds(base + j, SLAB), :]))
        return carry

    top = lax.fori_loop(0, rows // step, peak, jnp.zeros((SLAB, width), bf16))
    top = jnp.max(top.astype(f32), axis=0, keepdims=True) + EPS
    scale_ref[0] = top / LEVELS
    inverse = jnp.broadcast_to(LEVELS / top, (SLAB, width))

    def quantize(i, carry):
        base = pl.multiple_of(i * step, step)
        for j in range(0, step, SLAB):
            value = down_ref[0, pl.ds(base + j, SLAB), :].astype(f32) * inverse
            level_ref[0, pl.ds(base + j, SLAB), :] = level_bf16(value)
        return carry

    lax.fori_loop(0, rows // step, quantize, 0)


def down_quant(down):
    experts, hidden, width = down.shape
    block = 512
    return pl.pallas_call(
        functools.partial(down_quant_kernel, hidden, block),
        grid=(experts, width // block),
        out_shape=(
            jax.ShapeDtypeStruct(down.shape, bf16),
            jax.ShapeDtypeStruct((experts, 1, width), f32),
        ),
        in_specs=[pl.BlockSpec((1, hidden, block), lambda e, c: (e, 0, c))],
        out_specs=(
            pl.BlockSpec((1, hidden, block), lambda e, c: (e, 0, c)),
            pl.BlockSpec((1, 1, block), lambda e, c: (e, 0, c)),
        ),
        compiler_params=params(),
        cost_estimate=BRIEF,
        name="down_levels",
    )(down)


def rows_kernel(local_experts, units, hot_ref, tokens_ref, peak_ref, rows_ref, smooth_ref):
    unit_rows = UNIT * CAP
    group_tokens, width = tokens_ref.shape[2], tokens_ref.shape[3]
    top = [None] * local_experts
    for u in range(units):
        tokens = tokens_ref[u * UNIT : (u + 1) * UNIT, 0].reshape(UNIT * group_tokens, width)
        picked = jnp.dot(hot_ref[u], tokens, preferred_element_type=f32)
        for e in range(local_experts):
            part = picked[e * unit_rows : (e + 1) * unit_rows]
            rows_ref[e, u * unit_rows : (u + 1) * unit_rows, :] = part.astype(bf16)
            most = jnp.max(jnp.abs(part), axis=0, keepdims=True)
            top[e] = most if top[e] is None else jnp.maximum(top[e], most)
    for e in range(local_experts):
        smooth_ref[e] = jnp.sqrt(jnp.maximum(top[e], 1.0) / (peak_ref[e : e + 1, :] + EPS))


def expert_rows(hot, tokens, weight_peak, local_experts, groups, part):
    shards, group_tokens, block = tokens.shape[1:]
    units = groups // UNIT
    return pl.pallas_call(
        functools.partial(rows_kernel, local_experts, units),
        grid=(shards,),
        out_shape=(
            jax.ShapeDtypeStruct((local_experts, groups * CAP, shards * block), bf16),
            jax.ShapeDtypeStruct((local_experts, 1, shards * block), f32),
        ),
        in_specs=[
            pl.BlockSpec(hot.shape, lambda c: (0, 0, 0)),
            pl.BlockSpec((groups, 1, group_tokens, block), lambda c: (0, c, 0, 0)),
            pl.BlockSpec((local_experts, block), lambda c: (0, HALVES * c + part)),
        ],
        out_specs=(
            pl.BlockSpec((local_experts, groups * CAP, block), lambda c: (0, 0, c)),
            pl.BlockSpec((local_experts, 1, block), lambda c: (0, 0, c)),
        ),
        compiler_params=params(),
        cost_estimate=BRIEF,
        name="expert_rows",
    )(hot, tokens, weight_peak)


def silu_product(both):
    half = both.shape[0] // 2
    gate, up = both[:half], both[half:]
    return flipped(gate / (1.0 + jnp.exp(-gate)) * up).astype(bf16)


def float_kernel(shards, part, rows_ref, smooth_ref, *refs):
    gates, ups = refs[:shards], refs[shards : 2 * shards]
    refs = refs[2 * shards :]
    count = rows_ref.shape[1]
    hidden, block = gates[0].shape[1:]
    last = part == HALVES - 1
    if part:
        before, refs = refs[:3], refs[3:]
    if last:
        hidden_ref, inverse_w, scale_w, inverse_r, scale_r, acc, top_s, top_r = refs
    else:
        acc, top_s, top_r = (ref.at[0] for ref in refs)
    for n, ref in enumerate((acc, top_s, top_r)):
        ref[...] = before[n][0] if part else jnp.zeros_like(ref)

    for s in range(shards):
        cols = slice(s * block, (s + 1) * block)
        smooth = smooth_ref[0, :, cols]
        smooth_c = jnp.broadcast_to(smooth, (SLAB, block))
        unsmooth_c = jnp.broadcast_to(1.0 / smooth, (SLAB, block))
        rows = rows_ref[0, :, cols]
        for ref, base in ((gates[s], 0), (ups[s], hidden)):
            acc[base : base + hidden, :] += dot_t(ref[0], rows)
            for f in range(0, hidden, SLAB):
                value = jnp.abs(ref[0, f : f + SLAB, :]).astype(f32) * smooth_c
                spot = slice(base + f, base + f + SLAB)
                top_s[spot, :] = jnp.maximum(top_s[spot, :], fold_max(value))
        for r in range(0, count, SLAB):
            value = jnp.abs(rows_ref[0, r : r + SLAB, cols]).astype(f32) * unsmooth_c
            top_r[r : r + SLAB, :] = jnp.maximum(top_r[r : r + SLAB, :], fold_max(value))
    if not last:
        return

    hidden_ref[0] = silu_product(acc[...])
    for r in range(0, count, SLAB):
        top = jnp.max(top_r[r : r + SLAB, :], axis=1, keepdims=True) + EPS
        inverse_r[0, r : r + SLAB, :] = jnp.broadcast_to(LEVELS / top, (SLAB, LANES))
        scale_r[0, r : r + SLAB, :] = jnp.broadcast_to(top / LEVELS, (SLAB, LANES))
    for f in range(0, 2 * hidden, LANES):
        top = jnp.max(top_s[f : f + LANES, :], axis=1, keepdims=True) + EPS
        inverse_w[0, f : f + LANES, :] = jnp.broadcast_to(LEVELS / top, (LANES, LANES))
        scale_w[0, f : f + LANES, :] = jnp.broadcast_to(top / LEVELS, (LANES, LANES))


def float_hidden(rows, gate, up, smooth, shards, part, before):
    experts, count, depth = rows.shape
    hidden, width = gate.shape[1:]
    block = width // (HALVES * shards)

    def spec(*tail):
        return pl.BlockSpec((1,) + tail, lambda e: (e,) + (0,) * len(tail))

    def piece(s):
        return pl.BlockSpec((1, hidden, block), lambda e: (e, 0, HALVES * s + part))

    pieces = [piece(s) for s in range(shards)]
    carried = ((2 * hidden, count), (2 * hidden, LANES), (count, LANES))
    last = part == HALVES - 1
    if last:
        tails = ((count, hidden), (2 * hidden, LANES), (2 * hidden, LANES), (count, LANES), (count, LANES))
        kinds = (bf16, f32, f32, f32, f32)
    else:
        tails, kinds = carried, (f32,) * 3
    return pl.pallas_call(
        functools.partial(float_kernel, shards, part),
        grid=(experts,),
        out_shape=tuple(jax.ShapeDtypeStruct((experts,) + s, k) for s, k in zip(tails, kinds)),
        in_specs=[spec(count, depth), spec(1, depth)] + pieces + pieces
        + [spec(*s) for s in carried if part],
        out_specs=tuple(spec(*s) for s in tails),
        scratch_shapes=[pltpu.VMEM(s, f32) for s in carried if last],
        compiler_params=params(),
        cost_estimate=BRIEF,
        name="float_hidden",
    )(rows, smooth, *([gate] * shards), *([up] * shards), *before)


def quant_kernel(gate_ref, up_ref, inverse_w, scale_w, inverse_r, scale_r, *refs):
    rows_refs, smooth_refs = refs[:HALVES], refs[HALVES : 2 * HALVES]
    hidden_ref, smooth_s, unsmooth_s, acc, levels, row_levels = refs[-6:]
    count = rows_refs[0].shape[1]
    hidden, depth = gate_ref.shape[1:]
    chunk = levels.shape[2]
    chunks, part = depth // chunk, chunk // HALVES
    weights = ((gate_ref, 0), (up_ref, hidden))

    for c in range(chunks):
        for h in range(HALVES):
            smooth = smooth_refs[h][0, :, c * part : (c + 1) * part]
            spot = slice(c * chunk + h * part, c * chunk + (h + 1) * part)
            smooth_s[:, spot] = jnp.broadcast_to(smooth, (SLAB, part))
            unsmooth_s[:, spot] = jnp.broadcast_to(1.0 / smooth, (SLAB, part))
    acc[...] = jnp.zeros_like(acc)

    def quantize(i, slot):
        for h in range(HALVES):
            spot = slice(h * part, (h + 1) * part)
            cols = pl.ds(pl.multiple_of(i * chunk + h * part, part), part)
            rows_cols = pl.ds(pl.multiple_of(i * part, part), part)
            smooth_c = smooth_s[:, cols]
            unsmooth_c = unsmooth_s[:, cols]
            for r in range(0, count, SLAB):
                value = rows_refs[h][0, r : r + SLAB, rows_cols].astype(f32) * unsmooth_c
                value = value * wide(inverse_r[0, r : r + SLAB, :], part)
                level = level_mixed(value) * wide(scale_r[0, r : r + SLAB, :], part)
                row_levels[slot, r : r + SLAB, spot] = level.astype(bf16)
            for ref, base in weights:
                for f in range(0, hidden, SLAB):
                    value = ref[0, f : f + SLAB, cols].astype(f32) * smooth_c
                    value = value * wide(inverse_w[0, base + f : base + f + SLAB, :], part)
                    levels[slot, base + f : base + f + SLAB, spot] = level_bf16(value)

    def multiply(slot):
        acc[...] += dot_t(levels[slot], row_levels[slot])

    quantize(0, 0)

    def pair(i, carry):
        multiply(0)
        quantize(2 * i + 1, 1)
        multiply(1)
        quantize(2 * i + 2, 0)
        return carry

    lax.fori_loop(0, chunks // 2 - 1, pair, 0)
    multiply(0)
    quantize(chunks - 1, 1)
    multiply(1)

    hidden_ref[0] = silu_product(acc[...] * scale_w[0][:, :1])


def quant_hidden(rows, smooth, gate, up, scales, shards, first, amount, space, at, into=None):
    count = rows[0].shape[1]
    hidden, depth = gate.shape[1:]
    chunk = depth // shards
    operands = (gate, up, *scales, *rows, *smooth)
    extra = () if into is None else (into,)

    def spec(*tail):
        return pl.BlockSpec((1,) + tail, lambda e: (first + e,) + (0,) * len(tail))

    return pl.pallas_call(
        quant_kernel,
        grid=(amount,),
        out_shape=jax.ShapeDtypeStruct((space, count, hidden), bf16),
        in_specs=[spec(*a.shape[1:]) for a in operands]
        + [pl.BlockSpec(memory_space=pl.ANY)] * len(extra),
        out_specs=pl.BlockSpec((1, count, hidden), lambda e: (at + e, 0, 0)),
        input_output_aliases={len(operands): 0} if extra else {},
        scratch_shapes=[
            pltpu.VMEM((SLAB, depth), f32),
            pltpu.VMEM((SLAB, depth), f32),
            pltpu.VMEM((2 * hidden, count), f32),
            pltpu.VMEM((2, 2 * hidden, chunk), bf16),
            pltpu.VMEM((2, count, chunk), bf16),
        ],
        compiler_params=params(),
        cost_estimate=BRIEF,
        name="quant_hidden",
    )(*operands, *extra)


def combine_kernel(quantized, skip, last, *refs):
    share_ref, hidden_ref, down_ref, scale_ref = refs[:4]
    e = pl.program_id(0)
    shards, _, count, part = hidden_ref.shape
    unit_rows = UNIT * CAP
    wide_s = refs[-1]
    for r in range(0, count, SLAB):
        spot = slice(r, r + SLAB)
        if not quantized:
            for s in range(shards):
                wide_s[spot, s * part : (s + 1) * part] = hidden_ref[s, 0, spot, :]
            continue
        top = None
        for s in range(shards):
            value = fold_max(jnp.abs(hidden_ref[s, 0, spot, :]).astype(f32))
            top = value if top is None else jnp.maximum(top, value)
        top = jnp.max(top, axis=1, keepdims=True) + EPS
        inverse, scale = LEVELS / top, top / LEVELS
        for s in range(shards):
            value = level_mixed(hidden_ref[s, 0, spot, :].astype(f32) * inverse) * scale
            wide_s[spot, s * part : (s + 1) * part] = value.astype(bf16)

    out = jnp.dot(wide_s[...], down_ref[0], preferred_element_type=f32) * scale_ref[0] * share_ref[0]
    out = out.astype(bf16)
    units = count // unit_rows
    if not last:
        for u in range(units):
            refs[-2][u] = out[u * unit_rows : (u + 1) * unit_rows]
        return
    hot_ref, out_ref, keep_s = refs[4], refs[-3], refs[-2]
    if skip:

        @pl.when(e == 0)
        def _():
            keep_s[:, : skip * unit_rows, :] = refs[5][...]

    at = pl.ds(pl.multiple_of((skip + e) * unit_rows, SLAB), unit_rows)
    for u in range(units):
        keep_s[u, at, :] = out[u * unit_rows : (u + 1) * unit_rows]

    @pl.when(e == pl.num_programs(0) - 1)
    def _():
        tokens = hot_ref.shape[1]
        for u in range(units):
            out_ref[u * tokens : (u + 1) * tokens, :] = jnp.dot(
                hot_ref[u], keep_s[u], preferred_element_type=f32
            ).astype(bf16)


def combine(hot_t, share, hidden, down, scale, quantized, first=0, at=0, pieces=1, last=True, earlier=None):
    units, unit_tokens, hot_rows = hot_t.shape
    shards, amount, count, part = hidden.shape
    units_hidden, width = down.shape[1:]
    block = width // pieces
    unit_rows = UNIT * CAP
    in_specs = [
        pl.BlockSpec((1, count, 1), lambda e: (first + e, 0, 0)),
        pl.BlockSpec((shards, 1, count, part), lambda e: (0, e, 0, 0)),
        pl.BlockSpec((1, units_hidden, block), lambda e: (first + e, 0, at)),
        pl.BlockSpec((1, 1, block), lambda e: (first + e, 0, at)),
    ]
    operands = [share, hidden, down, scale]
    scratch = [pltpu.VMEM((count, units_hidden), bf16)]
    if last:
        operands.append(hot_t)
        in_specs.append(pl.BlockSpec(hot_t.shape, lambda e: (0, 0, 0)))
        scratch = [pltpu.VMEM((units, hot_rows, block), bf16)] + scratch
        out_shape = jax.ShapeDtypeStruct((units * unit_tokens, block), bf16)
        out_spec = pl.BlockSpec((units * unit_tokens, block), lambda e: (0, 0))
        if first:
            operands.append(earlier)
            in_specs.append(pl.BlockSpec((units, first * unit_rows, block), lambda e: (0, 0, at)))
    else:
        out_shape = jax.ShapeDtypeStruct((units, amount * unit_rows, block), bf16)
        out_spec = pl.BlockSpec((units, unit_rows, block), lambda e: (0, e, 0))
    return pl.pallas_call(
        functools.partial(combine_kernel, quantized, first, last),
        grid=(amount,),
        out_shape=out_shape,
        in_specs=in_specs,
        out_specs=out_spec,
        scratch_shapes=scratch,
        compiler_params=params(),
        cost_estimate=BRIEF,
        name="combine_quant" if quantized else "combine_float",
    )(*operands)


def to_pairs(part, groups):
    width = part.shape[1]
    low = lax.axis_index("dp") & 1
    part = part.reshape(groups // 2, 2, -1, width)
    kept = lax.dynamic_index_in_dim(part, low, 1, keepdims=False)
    sent = lax.dynamic_index_in_dim(part, 1 - low, 1, keepdims=False)
    came = lax.ppermute(sent, "dp", [(i, i ^ 1) for i in range(groups)])
    return (kept.astype(f32) + came.astype(f32)).astype(bf16)


def to_tokens(both, groups):
    pairs = groups // 2
    high = lax.axis_index("dp") >> 1
    total = lax.dynamic_index_in_dim(both, high, 0, keepdims=False).astype(f32)
    for k in range(1, pairs):
        block = lax.dynamic_index_in_dim(both, lax.rem(high + k, pairs), 0, keepdims=False)
        came = lax.ppermute(block, "dp", [(i, (i + 2 * k) % groups) for i in range(groups)])
        total = total + came.astype(f32)
    return total


def from_all(x, axis):
    copies = jnp.broadcast_to(x, (lax.axis_size(axis),) + x.shape)
    return lax.all_to_all(copies, axis, split_axis=0, concat_axis=0)


def on_device(tokens, expert_ids, route_weights, gate_weight, up_weight, down_weight):
    groups = lax.axis_size("dp")
    experts = gate_weight.shape[0]
    choices = expert_ids.shape[1]

    payload = jnp.concatenate([expert_ids.T.astype(f32), route_weights.T], axis=0)
    route = from_all(payload, "dp").reshape(-1, payload.shape[1])
    share_width = tokens.shape[1] // HALVES
    all_tokens = []
    for h in range(HALVES):
        half = tokens[:, h * share_width : (h + 1) * share_width]
        half = lax.all_gather(half, ("dp", "expert"), axis=0)
        all_tokens.append(half.reshape((groups, -1) + half.shape[1:]))
    shards = all_tokens[0].shape[1]

    local_peak = channel_peak(gate_weight, up_weight)
    weight_peak = from_all(local_peak.reshape(experts, -1).astype(bf16), "expert")
    weight_peak = jnp.max(weight_peak, axis=0).astype(f32)
    first = (lax.axis_index("dp") * experts).astype(jnp.int32).reshape(1)
    hot, share = prep(first, route, experts, groups, choices)
    hot_t = jnp.swapaxes(hot, 1, 2)
    rows, smooth, carried = [None] * HALVES, [None] * HALVES, ()
    levels = None
    for h in range(HALVES):
        rows[h], smooth[h] = expert_rows(hot, all_tokens[h], weight_peak, experts, groups, h)
        carried = float_hidden(rows[h], gate_weight, up_weight, smooth[h], shards, h, carried)
        if levels is None:
            down_weight, carried = lax.optimization_barrier((down_weight, carried))
            levels, level_scale = down_quant(down_weight)
            hot, levels = lax.optimization_barrier((hot, levels))
    hf, *scales = carried
    wide_f = lax.all_gather(hf, "expert", axis=0)

    half = experts // 2
    more = experts - half
    some = (3 * more) // 4
    operands = (smooth, gate_weight, up_weight, scales, shards)
    hq = quant_hidden(rows, *operands, 0, half, half, 0)
    wide_q = [lax.all_gather(hq, "expert", axis=0)]
    wide_f, hq = lax.optimization_barrier((wide_f, hq))
    part_f = combine(hot_t, share, wide_f, down_weight, jnp.ones_like(level_scale), False)
    both_f = to_pairs(part_f, groups)
    rows, part_f = lax.optimization_barrier((rows, part_f))
    hq = quant_hidden(rows, *operands, half, some, more, 0) if some else None
    rows, both_f = lax.optimization_barrier((rows, both_f))
    out_f = to_tokens(both_f, groups)
    hq = quant_hidden(rows, *operands, half + some, more - some, more, some, hq)
    wide_q.append(lax.all_gather(hq, "expert", axis=0))
    share, hq = lax.optimization_barrier((share, hq))
    earlier = combine(hot_t, share, wide_q[0], levels, level_scale, True, last=False)
    earlier, out_f = lax.optimization_barrier((earlier, out_f))
    out_q = []
    for at in range(2):
        part_q = combine(
            hot_t, share, wide_q[1], levels, level_scale, True, half, at, 2, earlier=earlier
        )
        out_q.append(to_tokens(to_pairs(part_q, groups), groups).astype(bf16))
        earlier, part_q = lax.optimization_barrier((earlier, part_q))
    return jnp.concatenate(out_q, axis=1), out_f


def solution(mesh):
    in_specs = (
        P("dp", "expert"),
        P("dp", None),
        P("dp", None),
        P("dp", "expert", None),
        P("dp", "expert", None),
        P("dp", None, "expert"),
    )
    out_specs = (P("dp", "expert"), P("dp", "expert"))
    return jax.shard_map(
        on_device, mesh=mesh, in_specs=in_specs, out_specs=out_specs, check_vma=False
    )
```

```python
import functools

import jax
import jax.numpy as jnp
from jax import lax
from jax.experimental import pallas as pl
from jax.experimental.pallas import tpu as pltpu
from jax.sharding import PartitionSpec as P

CAP = 20
UNIT = 4
LEVELS = 7.0
EPS = 1e-06
VMEM = 56 * 1024 * 1024
LANES = 128
SLAB = 16
SPACING_ONE = 192.0
CHUNK = 1024
BRIEF = pl.CostEstimate(flops=1, bytes_accessed=1, transcendentals=0)

FRACTION_BF16 = (6.55787162, -12.52307356, 9.17209913)

bf16 = jnp.bfloat16
f32 = jnp.float32


def fraction(r, coefficients):
    dtype = r.dtype
    square = r * r
    total = jnp.asarray(coefficients[-1], dtype)
    for c in coefficients[-2::-1]:
        total = total * square + jnp.asarray(c, dtype)
    return (r * square) * total


def level_bf16(v):
    v = v.astype(bf16)
    offset = jnp.asarray(SPACING_ONE, bf16)
    n = (v + offset) - offset
    return n + fraction(v - n, FRACTION_BF16)


def level_mixed(v):
    n = jnp.round(v)
    return n + fraction((v - n).astype(bf16), FRACTION_BF16).astype(f32)


def fold_max(x):
    if x.shape[1] % LANES:
        return jnp.max(x, axis=1, keepdims=True)
    out = x[:, :LANES]
    for c in range(LANES, x.shape[1], LANES):
        out = jnp.maximum(out, x[:, c : c + LANES])
    return out


def wide(x, width):
    return jnp.concatenate([x] * (width // LANES), axis=1)


def dot_t(a, b):
    return lax.dot_general(a, b, (((1,), (1,)), ((), ())), preferred_element_type=f32)


def flipped(x):
    high, broad = -x.shape[0] % LANES, -x.shape[1] % LANES
    return jnp.pad(x, ((0, high), (0, broad))).T[: x.shape[1], : x.shape[0]]


def params():
    return pltpu.CompilerParams(vmem_limit_bytes=VMEM)


def prep_kernel(local_experts, groups, choices, first_ref, route_ref, hot_ref, share_ref):
    units = groups // UNIT
    group_tokens = route_ref.shape[1]
    unit_rows, unit_tokens = UNIT * CAP, UNIT * group_tokens
    first = first_ref[0].astype(f32)
    before = lax.broadcasted_iota(jnp.int32, (group_tokens, group_tokens), 0) < lax.broadcasted_iota(
        jnp.int32, (group_tokens, group_tokens), 1
    )
    before = jnp.where(before, 1.0, 0.0).astype(bf16)
    codes, weights = [], []
    for g in range(groups):
        base = 2 * choices * g
        ids = route_ref[base : base + choices, :]
        route = route_ref[base + choices : base + 2 * choices, :]
        shares = route / jnp.sum(route, axis=0, keepdims=True)
        hits, mine = [], []
        for e in range(local_experts):
            hit = ids == first + float(e)
            hits.append(jnp.max(jnp.where(hit, 1.0, 0.0), axis=0, keepdims=True))
            mine.append(jnp.sum(jnp.where(hit, shares, 0.0), axis=0, keepdims=True))
        part = jnp.concatenate(hits, axis=0)
        weights.append(jnp.concatenate(mine, axis=0))
        slot = jnp.dot(part.astype(bf16), before, preferred_element_type=f32)
        codes.append(jnp.where(part > 0.5, slot + float((g % UNIT) * CAP), -1.0))
    row = lax.broadcasted_iota(jnp.int32, (unit_rows, unit_tokens), 0).astype(f32)
    for u in range(units):
        code = jnp.concatenate(codes[u * UNIT : (u + 1) * UNIT], axis=1)
        weight = jnp.concatenate(weights[u * UNIT : (u + 1) * UNIT], axis=1)
        for e in range(local_experts):
            hot = row == code[e : e + 1, :]
            hot_ref[u, e * unit_rows : (e + 1) * unit_rows, :] = jnp.where(hot, 1.0, 0.0).astype(bf16)
            share_ref[e, u * unit_rows : (u + 1) * unit_rows, :] = jnp.sum(
                jnp.where(hot, weight[e : e + 1, :], 0.0), axis=1, keepdims=True
            )


def prep(first, route, local_experts, groups, choices):
    units = groups // UNIT
    return pl.pallas_call(
        functools.partial(prep_kernel, local_experts, groups, choices),
        out_shape=(
            jax.ShapeDtypeStruct((units, local_experts * UNIT * CAP, UNIT * route.shape[1]), bf16),
            jax.ShapeDtypeStruct((local_experts, groups * CAP, 1), f32),
        ),
        in_specs=[
            pl.BlockSpec(memory_space=pltpu.SMEM),
            pl.BlockSpec(memory_space=pltpu.VMEM),
        ],
        out_specs=(pl.BlockSpec(memory_space=pltpu.VMEM), pl.BlockSpec(memory_space=pltpu.VMEM)),
        compiler_params=params(),
        name="routing_tables",
    )(first, route)


def channel_peak_kernel(gate_ref, up_ref, peak_ref):
    hidden, depth = gate_ref.shape[1:]

    def one(i, carry):
        cols = pl.ds(pl.multiple_of(i * CHUNK, CHUNK), CHUNK)
        top = None
        for ref in (gate_ref, up_ref):
            for f in range(0, hidden, SLAB):
                value = jnp.abs(ref[0, f : f + SLAB, cols])
                top = value if top is None else jnp.maximum(top, value)
        peak_ref[0, :, cols] = jnp.max(top.astype(f32), axis=0, keepdims=True)
        return carry

    lax.fori_loop(0, depth // CHUNK, one, 0)


def channel_peak(gate, up):
    experts, hidden, depth = gate.shape
    spec = pl.BlockSpec((1, hidden, depth), lambda e: (e, 0, 0))
    return pl.pallas_call(
        channel_peak_kernel,
        grid=(experts,),
        out_shape=jax.ShapeDtypeStruct((experts, 1, depth), f32),
        in_specs=[spec, spec],
        out_specs=pl.BlockSpec((1, 1, depth), lambda e: (e, 0, 0)),
        compiler_params=params(),
        cost_estimate=BRIEF,
        name="channel_peak",
    )(gate, up)


def down_quant_kernel(rows, width, down_ref, level_ref, scale_ref):
    step = 32 * SLAB

    def peak(i, carry):
        base = pl.multiple_of(i * step, step)
        for j in range(0, step, SLAB):
            carry = jnp.maximum(carry, jnp.abs(down_ref[0, pl.ds(base + j, SLAB), :]))
        return carry

    top = lax.fori_loop(0, rows // step, peak, jnp.zeros((SLAB, width), bf16))
    top = jnp.max(top.astype(f32), axis=0, keepdims=True) + EPS
    scale_ref[0] = top / LEVELS
    inverse = jnp.broadcast_to(LEVELS / top, (SLAB, width))

    def quantize(i, carry):
        base = pl.multiple_of(i * step, step)
        for j in range(0, step, SLAB):
            value = down_ref[0, pl.ds(base + j, SLAB), :].astype(f32) * inverse
            level_ref[0, pl.ds(base + j, SLAB), :] = level_bf16(value)
        return carry

    lax.fori_loop(0, rows // step, quantize, 0)


def down_quant(down):
    experts, hidden, width = down.shape
    block = 512
    return pl.pallas_call(
        functools.partial(down_quant_kernel, hidden, block),
        grid=(experts, width // block),
        out_shape=(
            jax.ShapeDtypeStruct(down.shape, bf16),
            jax.ShapeDtypeStruct((experts, 1, width), f32),
        ),
        in_specs=[pl.BlockSpec((1, hidden, block), lambda e, c: (e, 0, c))],
        out_specs=(
            pl.BlockSpec((1, hidden, block), lambda e, c: (e, 0, c)),
            pl.BlockSpec((1, 1, block), lambda e, c: (e, 0, c)),
        ),
        compiler_params=params(),
        cost_estimate=BRIEF,
        name="down_levels",
    )(down)


def rows_kernel(local_experts, units, hot_ref, tokens_ref, peak_ref, rows_ref, smooth_ref):
    unit_rows = UNIT * CAP
    group_tokens, width = tokens_ref.shape[2], tokens_ref.shape[3]
    top = [None] * local_experts
    for u in range(units):
        tokens = tokens_ref[u * UNIT : (u + 1) * UNIT, 0].reshape(UNIT * group_tokens, width)
        picked = jnp.dot(hot_ref[u], tokens, preferred_element_type=f32)
        for e in range(local_experts):
            part = picked[e * unit_rows : (e + 1) * unit_rows]
            rows_ref[e, u * unit_rows : (u + 1) * unit_rows, :] = part.astype(bf16)
            most = jnp.max(jnp.abs(part), axis=0, keepdims=True)
            top[e] = most if top[e] is None else jnp.maximum(top[e], most)
    for e in range(local_experts):
        smooth_ref[e] = jnp.sqrt(jnp.maximum(top[e], 1.0) / (peak_ref[e : e + 1, :] + EPS))


def expert_rows(hot, tokens, weight_peak, local_experts, groups):
    shards, group_tokens, share = tokens.shape[1:]
    units = groups // UNIT
    block = 512
    per = share // block
    return pl.pallas_call(
        functools.partial(rows_kernel, local_experts, units),
        grid=(shards * per,),
        out_shape=(
            jax.ShapeDtypeStruct((local_experts, groups * CAP, shards * share), bf16),
            jax.ShapeDtypeStruct((local_experts, 1, shards * share), f32),
        ),
        in_specs=[
            pl.BlockSpec(hot.shape, lambda c: (0, 0, 0)),
            pl.BlockSpec((groups, 1, group_tokens, block), lambda c: (0, c // per, 0, c % per)),
            pl.BlockSpec((local_experts, block), lambda c: (0, c)),
        ],
        out_specs=(
            pl.BlockSpec((local_experts, groups * CAP, block), lambda c: (0, 0, c)),
            pl.BlockSpec((local_experts, 1, block), lambda c: (0, 0, c)),
        ),
        compiler_params=params(),
        name="expert_rows",
    )(hot, tokens, weight_peak)


def silu_product(both):
    half = both.shape[0] // 2
    gate, up = both[:half], both[half:]
    return flipped(gate / (1.0 + jnp.exp(-gate)) * up).astype(bf16)


def float_kernel(
    rows_ref, gate_ref, up_ref, smooth_ref,
    hidden_ref, inverse_w, scale_w, inverse_r, scale_r,
    smooth_s, unsmooth_s, top_s, top_r, acc,
):
    count = rows_ref.shape[1]
    hidden = gate_ref.shape[1]
    chunks = gate_ref.shape[2] // CHUNK
    weights = ((gate_ref, 0), (up_ref, hidden))

    smooth = smooth_ref[0]
    smooth_s[...] = jnp.broadcast_to(smooth, smooth_s.shape).astype(bf16)
    unsmooth_s[...] = jnp.broadcast_to(1.0 / smooth, unsmooth_s.shape)
    top_s[...] = jnp.zeros_like(top_s)
    top_r[...] = jnp.zeros_like(top_r)
    acc[...] = jnp.zeros_like(acc)

    def peaks(i, carry):
        cols = pl.ds(pl.multiple_of(i * CHUNK, CHUNK), CHUNK)
        smooth_c = smooth_s[:, cols]
        unsmooth_c = unsmooth_s[:, cols]
        rows = rows_ref[0, :, cols]
        for ref, base in weights:
            acc[base : base + hidden, :] += dot_t(ref[0, :, cols], rows)
            for f in range(0, hidden, SLAB):
                value = jnp.abs(ref[0, f : f + SLAB, cols]) * smooth_c
                spot = slice(base + f, base + f + SLAB)
                top_s[spot, :] = jnp.maximum(top_s[spot, :], fold_max(value))
        for r in range(0, count, SLAB):
            value = jnp.abs(rows_ref[0, r : r + SLAB, cols]).astype(f32) * unsmooth_c
            top_r[r : r + SLAB, :] = jnp.maximum(top_r[r : r + SLAB, :], fold_max(value))
        return carry

    lax.fori_loop(0, chunks, peaks, 0)
    hidden_ref[0] = silu_product(acc[...])

    for r in range(0, count, SLAB):
        top = jnp.max(top_r[r : r + SLAB, :], axis=1, keepdims=True) + EPS
        inverse_r[0, r : r + SLAB, :] = jnp.broadcast_to(LEVELS / top, (SLAB, LANES))
        scale_r[0, r : r + SLAB, :] = jnp.broadcast_to(top / LEVELS, (SLAB, LANES))
    for f in range(0, 2 * hidden, LANES):
        top = jnp.max(top_s[f : f + LANES, :].astype(f32), axis=1, keepdims=True) + EPS
        inverse_w[0, f : f + LANES, :] = jnp.broadcast_to(LEVELS / top, (LANES, LANES))
        scale_w[0, f : f + LANES, :] = jnp.broadcast_to(top / LEVELS, (LANES, LANES))


def float_hidden(rows, gate, up, smooth):
    experts, count, depth = rows.shape
    hidden = gate.shape[1]

    def spec(*tail):
        return pl.BlockSpec((1,) + tail, lambda e: (e,) + (0,) * len(tail))

    tails = ((count, hidden), (2 * hidden, LANES), (2 * hidden, LANES), (count, LANES), (count, LANES))
    kinds = (bf16, f32, f32, f32, f32)
    return pl.pallas_call(
        float_kernel,
        grid=(experts,),
        out_shape=tuple(jax.ShapeDtypeStruct((experts,) + s, k) for s, k in zip(tails, kinds)),
        in_specs=[spec(count, depth), spec(hidden, depth), spec(hidden, depth), spec(1, depth)],
        out_specs=tuple(spec(*s) for s in tails),
        scratch_shapes=[
            pltpu.VMEM((SLAB, depth), bf16),
            pltpu.VMEM((SLAB, depth), f32),
            pltpu.VMEM((2 * hidden, LANES), bf16),
            pltpu.VMEM((count, LANES), f32),
            pltpu.VMEM((2 * hidden, count), f32),
        ],
        compiler_params=params(),
        cost_estimate=BRIEF,
        name="float_hidden",
    )(rows, gate, up, smooth)


def quant_kernel(
    rows_ref, gate_ref, up_ref, smooth_ref, inverse_w, scale_w, inverse_r, scale_r, *refs
):
    hidden_ref, smooth_s, unsmooth_s, acc, levels, row_levels = refs[-6:]
    count = rows_ref.shape[1]
    hidden = gate_ref.shape[1]
    chunks = gate_ref.shape[2] // CHUNK
    weights = ((gate_ref, 0), (up_ref, hidden))

    smooth = smooth_ref[0]
    smooth_s[...] = jnp.broadcast_to(smooth, smooth_s.shape)
    unsmooth_s[...] = jnp.broadcast_to(1.0 / smooth, unsmooth_s.shape)
    acc[...] = jnp.zeros_like(acc)

    def quantize(i, slot):
        cols = pl.ds(pl.multiple_of(i * CHUNK, CHUNK), CHUNK)
        smooth_c = smooth_s[:, cols]
        unsmooth_c = unsmooth_s[:, cols]
        for r in range(0, count, SLAB):
            value = rows_ref[0, r : r + SLAB, cols].astype(f32) * unsmooth_c
            value = value * wide(inverse_r[0, r : r + SLAB, :], CHUNK)
            level = level_mixed(value) * wide(scale_r[0, r : r + SLAB, :], CHUNK)
            row_levels[slot, r : r + SLAB, :] = level.astype(bf16)
        for ref, base in weights:
            for f in range(0, hidden, SLAB):
                value = ref[0, f : f + SLAB, cols].astype(f32) * smooth_c
                value = value * wide(inverse_w[0, base + f : base + f + SLAB, :], CHUNK)
                levels[slot, base + f : base + f + SLAB, :] = level_bf16(value)

    def multiply(slot):
        acc[...] += dot_t(levels[slot], row_levels[slot])

    quantize(0, 0)

    def pair(i, carry):
        multiply(0)
        quantize(2 * i + 1, 1)
        multiply(1)
        quantize(2 * i + 2, 0)
        return carry

    lax.fori_loop(0, chunks // 2 - 1, pair, 0)
    multiply(0)
    quantize(chunks - 1, 1)
    multiply(1)

    hidden_ref[0] = silu_product(acc[...] * scale_w[0][:, :1])


def quant_hidden(rows, gate, up, smooth, scales, first, amount, space, at, into=None):
    count, depth = rows.shape[1:]
    hidden = gate.shape[1]
    extra = [] if into is None else [into]

    def spec(*tail):
        return pl.BlockSpec((1,) + tail, lambda e: (first + e,) + (0,) * len(tail))

    return pl.pallas_call(
        quant_kernel,
        grid=(amount,),
        out_shape=jax.ShapeDtypeStruct((space, count, hidden), bf16),
        in_specs=[spec(*a.shape[1:]) for a in (rows, gate, up, smooth) + scales]
        + [pl.BlockSpec(memory_space=pl.ANY)] * len(extra),
        out_specs=pl.BlockSpec((1, count, hidden), lambda e: (at + e, 0, 0)),
        input_output_aliases={8: 0} if extra else {},
        scratch_shapes=[
            pltpu.VMEM((SLAB, depth), f32),
            pltpu.VMEM((SLAB, depth), f32),
            pltpu.VMEM((2 * hidden, count), f32),
            pltpu.VMEM((2, 2 * hidden, CHUNK), bf16),
            pltpu.VMEM((2, count, CHUNK), bf16),
        ],
        compiler_params=params(),
        cost_estimate=BRIEF,
        name="quant_hidden",
    )(rows, gate, up, smooth, *scales, *extra)


def combine_kernel(quantized, skip, last, *refs):
    share_ref, hidden_ref, down_ref, scale_ref = refs[:4]
    e = pl.program_id(0)
    shards, _, count, part = hidden_ref.shape
    unit_rows = UNIT * CAP
    wide_s = refs[-1]
    for r in range(0, count, SLAB):
        spot = slice(r, r + SLAB)
        if not quantized:
            for s in range(shards):
                wide_s[spot, s * part : (s + 1) * part] = hidden_ref[s, 0, spot, :]
            continue
        top = None
        for s in range(shards):
            value = fold_max(jnp.abs(hidden_ref[s, 0, spot, :]).astype(f32))
            top = value if top is None else jnp.maximum(top, value)
        top = jnp.max(top, axis=1, keepdims=True) + EPS
        inverse, scale = LEVELS / top, top / LEVELS
        for s in range(shards):
            value = level_mixed(hidden_ref[s, 0, spot, :].astype(f32) * inverse) * scale
            wide_s[spot, s * part : (s + 1) * part] = value.astype(bf16)

    out = jnp.dot(wide_s[...], down_ref[0], preferred_element_type=f32) * scale_ref[0] * share_ref[0]
    out = out.astype(bf16)
    units = count // unit_rows
    if not last:
        for u in range(units):
            refs[-2][u] = out[u * unit_rows : (u + 1) * unit_rows]
        return
    hot_ref, out_ref, keep_s = refs[4], refs[-3], refs[-2]
    if skip:

        @pl.when(e == 0)
        def _():
            keep_s[:, : skip * unit_rows, :] = refs[5][...]

    at = pl.ds(pl.multiple_of((skip + e) * unit_rows, SLAB), unit_rows)
    for u in range(units):
        keep_s[u, at, :] = out[u * unit_rows : (u + 1) * unit_rows]

    @pl.when(e == pl.num_programs(0) - 1)
    def _():
        tokens = hot_ref.shape[1]
        for u in range(units):
            out_ref[u * tokens : (u + 1) * tokens, :] = jnp.dot(
                hot_ref[u], keep_s[u], preferred_element_type=f32
            ).astype(bf16)


def combine(hot_t, share, hidden, down, scale, quantized, first=0, at=0, pieces=1, last=True, earlier=None):
    units, unit_tokens, hot_rows = hot_t.shape
    shards, amount, count, part = hidden.shape
    units_hidden, width = down.shape[1:]
    block = width // pieces
    unit_rows = UNIT * CAP
    in_specs = [
        pl.BlockSpec((1, count, 1), lambda e: (first + e, 0, 0)),
        pl.BlockSpec((shards, 1, count, part), lambda e: (0, e, 0, 0)),
        pl.BlockSpec((1, units_hidden, block), lambda e: (first + e, 0, at)),
        pl.BlockSpec((1, 1, block), lambda e: (first + e, 0, at)),
    ]
    operands = [share, hidden, down, scale]
    scratch = [pltpu.VMEM((count, units_hidden), bf16)]
    if last:
        operands.append(hot_t)
        in_specs.append(pl.BlockSpec(hot_t.shape, lambda e: (0, 0, 0)))
        scratch = [pltpu.VMEM((units, hot_rows, block), bf16)] + scratch
        out_shape = jax.ShapeDtypeStruct((units * unit_tokens, block), bf16)
        out_spec = pl.BlockSpec((units * unit_tokens, block), lambda e: (0, 0))
        if first:
            operands.append(earlier)
            in_specs.append(pl.BlockSpec((units, first * unit_rows, block), lambda e: (0, 0, at)))
    else:
        out_shape = jax.ShapeDtypeStruct((units, amount * unit_rows, block), bf16)
        out_spec = pl.BlockSpec((units, unit_rows, block), lambda e: (0, e, 0))
    return pl.pallas_call(
        functools.partial(combine_kernel, quantized, first, last),
        grid=(amount,),
        out_shape=out_shape,
        in_specs=in_specs,
        out_specs=out_spec,
        scratch_shapes=scratch,
        compiler_params=params(),
        cost_estimate=BRIEF,
        name="combine_quant" if quantized else "combine_float",
    )(*operands)


def to_pairs(part, groups):
    width = part.shape[1]
    low = lax.axis_index("dp") & 1
    part = part.reshape(groups // 2, 2, -1, width)
    kept = lax.dynamic_index_in_dim(part, low, 1, keepdims=False)
    sent = lax.dynamic_index_in_dim(part, 1 - low, 1, keepdims=False)
    came = lax.ppermute(sent, "dp", [(i, i ^ 1) for i in range(groups)])
    return (kept.astype(f32) + came.astype(f32)).astype(bf16)


def to_tokens(both, groups):
    pairs = groups // 2
    high = lax.axis_index("dp") >> 1
    total = lax.dynamic_index_in_dim(both, high, 0, keepdims=False).astype(f32)
    for k in range(1, pairs):
        block = lax.dynamic_index_in_dim(both, lax.rem(high + k, pairs), 0, keepdims=False)
        came = lax.ppermute(block, "dp", [(i, (i + 2 * k) % groups) for i in range(groups)])
        total = total + came.astype(f32)
    return total


def from_all(x, axis):
    copies = jnp.broadcast_to(x, (lax.axis_size(axis),) + x.shape)
    return lax.all_to_all(copies, axis, split_axis=0, concat_axis=0)


def on_device(tokens, expert_ids, route_weights, gate_weight, up_weight, down_weight):
    groups = lax.axis_size("dp")
    experts = gate_weight.shape[0]
    choices = expert_ids.shape[1]

    payload = jnp.concatenate([expert_ids.T.astype(f32), route_weights.T], axis=0)
    route = from_all(payload, "dp").reshape(-1, payload.shape[1])
    all_tokens = lax.all_gather(tokens, ("dp", "expert"), axis=0)
    all_tokens = all_tokens.reshape((groups, -1) + tokens.shape)

    local_peak = channel_peak(gate_weight, up_weight)
    weight_peak = from_all(local_peak.reshape(experts, -1).astype(bf16), "expert")
    weight_peak = jnp.max(weight_peak, axis=0).astype(f32)
    down_weight, local_peak = lax.optimization_barrier((down_weight, local_peak))
    levels, level_scale = down_quant(down_weight)

    first = (lax.axis_index("dp") * experts).astype(jnp.int32).reshape(1)
    hot, share = prep(first, route, experts, groups, choices)
    hot_t = jnp.swapaxes(hot, 1, 2)
    hot, levels = lax.optimization_barrier((hot, levels))
    rows, smooth = expert_rows(hot, all_tokens, weight_peak, experts, groups)

    hf, *scales = float_hidden(rows, gate_weight, up_weight, smooth)
    scales = tuple(scales)
    wide_f = lax.all_gather(hf, "expert", axis=0)

    half = experts // 2
    more = experts - half
    some = (3 * more) // 4
    operands = (gate_weight, up_weight, smooth, scales)
    hq = quant_hidden(rows, *operands, 0, half, half, 0)
    wide_q = [lax.all_gather(hq, "expert", axis=0)]
    wide_f, hq = lax.optimization_barrier((wide_f, hq))
    part_f = combine(hot_t, share, wide_f, down_weight, jnp.ones_like(level_scale), False)
    both_f = to_pairs(part_f, groups)
    rows, part_f = lax.optimization_barrier((rows, part_f))
    hq = quant_hidden(rows, *operands, half, some, more, 0) if some else None
    rows, both_f = lax.optimization_barrier((rows, both_f))
    out_f = to_tokens(both_f, groups)
    hq = quant_hidden(rows, *operands, half + some, more - some, more, some, hq)
    wide_q.append(lax.all_gather(hq, "expert", axis=0))
    share, hq = lax.optimization_barrier((share, hq))
    earlier = combine(hot_t, share, wide_q[0], levels, level_scale, True, last=False)
    earlier, out_f = lax.optimization_barrier((earlier, out_f))
    out_q = []
    for at in range(2):
        part_q = combine(
            hot_t, share, wide_q[1], levels, level_scale, True, half, at, 2, earlier=earlier
        )
        out_q.append(to_tokens(to_pairs(part_q, groups), groups).astype(bf16))
        earlier, part_q = lax.optimization_barrier((earlier, part_q))
    return jnp.concatenate(out_q, axis=1), out_f


def solution(mesh):
    in_specs = (
        P("dp", "expert"),
        P("dp", None),
        P("dp", None),
        P("dp", "expert", None),
        P("dp", "expert", None),
        P("dp", None, "expert"),
    )
    out_specs = (P("dp", "expert"), P("dp", "expert"))
    return jax.shard_map(
        on_device, mesh=mesh, in_specs=in_specs, out_specs=out_specs, check_vma=False
    )
```

```python
import functools

import jax
import jax.numpy as jnp
from jax import lax
from jax.experimental import pallas as pl
from jax.experimental.pallas import tpu as pltpu
from jax.sharding import PartitionSpec as P

CAP = 20
UNIT = 4
LEVELS = 7.0
EPS = 1e-06
VMEM = 56 * 1024 * 1024
LANES = 128
SLAB = 16
SPACING_ONE = 192.0
CHUNK = 1024
BRIEF = pl.CostEstimate(flops=1, bytes_accessed=1, transcendentals=0)

FRACTION_BF16 = (6.55787162, -12.52307356, 9.17209913)

bf16 = jnp.bfloat16
f32 = jnp.float32


def fraction(r, coefficients):
    dtype = r.dtype
    square = r * r
    total = jnp.asarray(coefficients[-1], dtype)
    for c in coefficients[-2::-1]:
        total = total * square + jnp.asarray(c, dtype)
    return (r * square) * total


def level_bf16(v):
    v = v.astype(bf16)
    offset = jnp.asarray(SPACING_ONE, bf16)
    n = (v + offset) - offset
    return n + fraction(v - n, FRACTION_BF16)


def level_mixed(v):
    n = jnp.round(v)
    return n + fraction((v - n).astype(bf16), FRACTION_BF16).astype(f32)


def fold_max(x):
    if x.shape[1] % LANES:
        return jnp.max(x, axis=1, keepdims=True)
    out = x[:, :LANES]
    for c in range(LANES, x.shape[1], LANES):
        out = jnp.maximum(out, x[:, c : c + LANES])
    return out


def wide(x, width):
    return jnp.concatenate([x] * (width // LANES), axis=1)


def dot_t(a, b):
    return lax.dot_general(a, b, (((1,), (1,)), ((), ())), preferred_element_type=f32)


def flipped(x):
    high, broad = -x.shape[0] % LANES, -x.shape[1] % LANES
    return jnp.pad(x, ((0, high), (0, broad))).T[: x.shape[1], : x.shape[0]]


def params():
    return pltpu.CompilerParams(vmem_limit_bytes=VMEM)


def prep_kernel(local_experts, groups, choices, first_ref, route_ref, hot_ref, share_ref):
    units = groups // UNIT
    group_tokens = route_ref.shape[1]
    unit_rows, unit_tokens = UNIT * CAP, UNIT * group_tokens
    first = first_ref[0].astype(f32)
    before = lax.broadcasted_iota(jnp.int32, (group_tokens, group_tokens), 0) < lax.broadcasted_iota(
        jnp.int32, (group_tokens, group_tokens), 1
    )
    before = jnp.where(before, 1.0, 0.0).astype(bf16)
    codes, weights = [], []
    for g in range(groups):
        base = 2 * choices * g
        ids = route_ref[base : base + choices, :]
        route = route_ref[base + choices : base + 2 * choices, :]
        shares = route / jnp.sum(route, axis=0, keepdims=True)
        hits, mine = [], []
        for e in range(local_experts):
            hit = ids == first + float(e)
            hits.append(jnp.max(jnp.where(hit, 1.0, 0.0), axis=0, keepdims=True))
            mine.append(jnp.sum(jnp.where(hit, shares, 0.0), axis=0, keepdims=True))
        part = jnp.concatenate(hits, axis=0)
        weights.append(jnp.concatenate(mine, axis=0))
        slot = jnp.dot(part.astype(bf16), before, preferred_element_type=f32)
        codes.append(jnp.where(part > 0.5, slot + float((g % UNIT) * CAP), -1.0))
    row = lax.broadcasted_iota(jnp.int32, (unit_rows, unit_tokens), 0).astype(f32)
    for u in range(units):
        code = jnp.concatenate(codes[u * UNIT : (u + 1) * UNIT], axis=1)
        weight = jnp.concatenate(weights[u * UNIT : (u + 1) * UNIT], axis=1)
        for e in range(local_experts):
            hot = row == code[e : e + 1, :]
            hot_ref[u, e * unit_rows : (e + 1) * unit_rows, :] = jnp.where(hot, 1.0, 0.0).astype(bf16)
            share_ref[e, u * unit_rows : (u + 1) * unit_rows, :] = jnp.sum(
                jnp.where(hot, weight[e : e + 1, :], 0.0), axis=1, keepdims=True
            )


def prep(first, route, local_experts, groups, choices):
    units = groups // UNIT
    return pl.pallas_call(
        functools.partial(prep_kernel, local_experts, groups, choices),
        out_shape=(
            jax.ShapeDtypeStruct((units, local_experts * UNIT * CAP, UNIT * route.shape[1]), bf16),
            jax.ShapeDtypeStruct((local_experts, groups * CAP, 1), f32),
        ),
        in_specs=[
            pl.BlockSpec(memory_space=pltpu.SMEM),
            pl.BlockSpec(memory_space=pltpu.VMEM),
        ],
        out_specs=(pl.BlockSpec(memory_space=pltpu.VMEM), pl.BlockSpec(memory_space=pltpu.VMEM)),
        compiler_params=params(),
        name="routing_tables",
    )(first, route)


def channel_peak_kernel(gate_ref, up_ref, peak_ref):
    hidden, depth = gate_ref.shape[1:]

    def one(i, carry):
        cols = pl.ds(pl.multiple_of(i * CHUNK, CHUNK), CHUNK)
        top = None
        for ref in (gate_ref, up_ref):
            for f in range(0, hidden, SLAB):
                value = jnp.abs(ref[0, f : f + SLAB, cols])
                top = value if top is None else jnp.maximum(top, value)
        peak_ref[0, :, cols] = jnp.max(top.astype(f32), axis=0, keepdims=True)
        return carry

    lax.fori_loop(0, depth // CHUNK, one, 0)


def channel_peak(gate, up):
    experts, hidden, depth = gate.shape
    spec = pl.BlockSpec((1, hidden, depth), lambda e: (e, 0, 0))
    return pl.pallas_call(
        channel_peak_kernel,
        grid=(experts,),
        out_shape=jax.ShapeDtypeStruct((experts, 1, depth), f32),
        in_specs=[spec, spec],
        out_specs=pl.BlockSpec((1, 1, depth), lambda e: (e, 0, 0)),
        compiler_params=params(),
        cost_estimate=BRIEF,
        name="channel_peak",
    )(gate, up)


def down_quant_kernel(rows, width, down_ref, level_ref, scale_ref):
    step = 32 * SLAB

    def peak(i, carry):
        base = pl.multiple_of(i * step, step)
        for j in range(0, step, SLAB):
            carry = jnp.maximum(carry, jnp.abs(down_ref[0, pl.ds(base + j, SLAB), :]))
        return carry

    top = lax.fori_loop(0, rows // step, peak, jnp.zeros((SLAB, width), bf16))
    top = jnp.max(top.astype(f32), axis=0, keepdims=True) + EPS
    scale_ref[0] = top / LEVELS
    inverse = jnp.broadcast_to(LEVELS / top, (SLAB, width))

    def quantize(i, carry):
        base = pl.multiple_of(i * step, step)
        for j in range(0, step, SLAB):
            value = down_ref[0, pl.ds(base + j, SLAB), :].astype(f32) * inverse
            level_ref[0, pl.ds(base + j, SLAB), :] = level_bf16(value)
        return carry

    lax.fori_loop(0, rows // step, quantize, 0)


def down_quant(down):
    experts, hidden, width = down.shape
    block = 512
    return pl.pallas_call(
        functools.partial(down_quant_kernel, hidden, block),
        grid=(experts, width // block),
        out_shape=(
            jax.ShapeDtypeStruct(down.shape, bf16),
            jax.ShapeDtypeStruct((experts, 1, width), f32),
        ),
        in_specs=[pl.BlockSpec((1, hidden, block), lambda e, c: (e, 0, c))],
        out_specs=(
            pl.BlockSpec((1, hidden, block), lambda e, c: (e, 0, c)),
            pl.BlockSpec((1, 1, block), lambda e, c: (e, 0, c)),
        ),
        compiler_params=params(),
        cost_estimate=BRIEF,
        name="down_levels",
    )(down)


def rows_kernel(local_experts, units, core_ref, hot_ref, tokens_ref, peak_ref, *refs):
    rows_ref, smooth_ref = refs[-2:]
    unit_rows = UNIT * CAP
    group_tokens, width = tokens_ref.shape[2], tokens_ref.shape[3]
    top = [None] * local_experts
    for u in range(units):
        tokens = tokens_ref[u * UNIT : (u + 1) * UNIT, 0].reshape(UNIT * group_tokens, width)
        picked = jnp.dot(hot_ref[u], tokens, preferred_element_type=f32)
        for e in range(local_experts):
            part = picked[e * unit_rows : (e + 1) * unit_rows]
            rows_ref[e, u * unit_rows : (u + 1) * unit_rows, :] = part.astype(bf16)
            most = jnp.max(jnp.abs(part), axis=0, keepdims=True)
            top[e] = most if top[e] is None else jnp.maximum(top[e], most)
    for e in range(local_experts):
        smooth_ref[e] = jnp.sqrt(jnp.maximum(top[e], 1.0) / (peak_ref[e : e + 1, :] + EPS))


def expert_rows(core, hot, tokens, weight_peak, local_experts, groups, into=()):
    chips, group_tokens, share = tokens.shape[1:]
    units = groups // UNIT
    block = min(512, share)
    per = share // block

    def column(c, core):
        return ((c // per) * 2 + core[0]) * per + c % per

    width = 2 * chips * share
    return pl.pallas_call(
        functools.partial(rows_kernel, local_experts, units),
        grid_spec=pltpu.PrefetchScalarGridSpec(
            num_scalar_prefetch=1,
            grid=(chips * per,),
            in_specs=[
                pl.BlockSpec(hot.shape, lambda c, core: (0, 0, 0)),
                pl.BlockSpec((groups, 1, group_tokens, block), lambda c, core: (0, c // per, 0, c % per)),
                pl.BlockSpec((local_experts, block), lambda c, core: (0, column(c, core))),
            ]
            + [pl.BlockSpec(memory_space=pl.ANY)] * len(into),
            out_specs=[
                pl.BlockSpec((local_experts, groups * CAP, block), lambda c, core: (0, 0, column(c, core))),
                pl.BlockSpec((local_experts, 1, block), lambda c, core: (0, 0, column(c, core))),
            ],
        ),
        out_shape=[
            jax.ShapeDtypeStruct((local_experts, groups * CAP, width), bf16),
            jax.ShapeDtypeStruct((local_experts, 1, width), f32),
        ],
        input_output_aliases={4: 0, 5: 1} if into else {},
        compiler_params=params(),
        cost_estimate=BRIEF,
        name="expert_rows",
    )(core, hot, tokens, weight_peak, *into)


def silu_product(both):
    half = both.shape[0] // 2
    gate, up = both[:half], both[half:]
    return flipped(gate / (1.0 + jnp.exp(-gate)) * up).astype(bf16)


def float_kernel(
    rows_ref, gate_ref, up_ref, smooth_ref,
    hidden_ref, inverse_w, scale_w, inverse_r, scale_r,
    smooth_s, unsmooth_s, top_s, top_r, acc,
):
    count = rows_ref.shape[1]
    hidden = gate_ref.shape[1]
    chunks = gate_ref.shape[2] // CHUNK
    weights = ((gate_ref, 0), (up_ref, hidden))

    smooth = smooth_ref[0]
    smooth_s[...] = jnp.broadcast_to(smooth, smooth_s.shape).astype(bf16)
    unsmooth_s[...] = jnp.broadcast_to(1.0 / smooth, unsmooth_s.shape)
    top_s[...] = jnp.zeros_like(top_s)
    top_r[...] = jnp.zeros_like(top_r)
    acc[...] = jnp.zeros_like(acc)

    def peaks(i, carry):
        cols = pl.ds(pl.multiple_of(i * CHUNK, CHUNK), CHUNK)
        smooth_c = smooth_s[:, cols]
        unsmooth_c = unsmooth_s[:, cols]
        rows = rows_ref[0, :, cols]
        for ref, base in weights:
            acc[base : base + hidden, :] += dot_t(ref[0, :, cols], rows)
            for f in range(0, hidden, SLAB):
                value = jnp.abs(ref[0, f : f + SLAB, cols]) * smooth_c
                spot = slice(base + f, base + f + SLAB)
                top_s[spot, :] = jnp.maximum(top_s[spot, :], fold_max(value))
        for r in range(0, count, SLAB):
            value = jnp.abs(rows_ref[0, r : r + SLAB, cols]).astype(f32) * unsmooth_c
            top_r[r : r + SLAB, :] = jnp.maximum(top_r[r : r + SLAB, :], fold_max(value))
        return carry

    lax.fori_loop(0, chunks, peaks, 0)
    hidden_ref[0] = silu_product(acc[...])

    for r in range(0, count, SLAB):
        top = jnp.max(top_r[r : r + SLAB, :], axis=1, keepdims=True) + EPS
        inverse_r[0, r : r + SLAB, :] = jnp.broadcast_to(LEVELS / top, (SLAB, LANES))
        scale_r[0, r : r + SLAB, :] = jnp.broadcast_to(top / LEVELS, (SLAB, LANES))
    for f in range(0, 2 * hidden, LANES):
        top = jnp.max(top_s[f : f + LANES, :].astype(f32), axis=1, keepdims=True) + EPS
        inverse_w[0, f : f + LANES, :] = jnp.broadcast_to(LEVELS / top, (LANES, LANES))
        scale_w[0, f : f + LANES, :] = jnp.broadcast_to(top / LEVELS, (LANES, LANES))


def float_hidden(rows, gate, up, smooth):
    experts, count, depth = rows.shape
    hidden = gate.shape[1]

    def spec(*tail):
        return pl.BlockSpec((1,) + tail, lambda e: (e,) + (0,) * len(tail))

    tails = ((count, hidden), (2 * hidden, LANES), (2 * hidden, LANES), (count, LANES), (count, LANES))
    kinds = (bf16, f32, f32, f32, f32)
    return pl.pallas_call(
        float_kernel,
        grid=(experts,),
        out_shape=tuple(jax.ShapeDtypeStruct((experts,) + s, k) for s, k in zip(tails, kinds)),
        in_specs=[spec(count, depth), spec(hidden, depth), spec(hidden, depth), spec(1, depth)],
        out_specs=tuple(spec(*s) for s in tails),
        scratch_shapes=[
            pltpu.VMEM((SLAB, depth), bf16),
            pltpu.VMEM((SLAB, depth), f32),
            pltpu.VMEM((2 * hidden, LANES), bf16),
            pltpu.VMEM((count, LANES), f32),
            pltpu.VMEM((2 * hidden, count), f32),
        ],
        compiler_params=params(),
        cost_estimate=BRIEF,
        name="float_hidden",
    )(rows, gate, up, smooth)


def quant_kernel(
    rows_ref, gate_ref, up_ref, smooth_ref, inverse_w, scale_w, inverse_r, scale_r, *refs
):
    hidden_ref, smooth_s, unsmooth_s, acc, levels, row_levels = refs[-6:]
    count = rows_ref.shape[1]
    hidden = gate_ref.shape[1]
    chunks = gate_ref.shape[2] // CHUNK
    weights = ((gate_ref, 0), (up_ref, hidden))

    smooth = smooth_ref[0]
    smooth_s[...] = jnp.broadcast_to(smooth, smooth_s.shape)
    unsmooth_s[...] = jnp.broadcast_to(1.0 / smooth, unsmooth_s.shape)
    acc[...] = jnp.zeros_like(acc)

    def quantize(i, slot):
        cols = pl.ds(pl.multiple_of(i * CHUNK, CHUNK), CHUNK)
        smooth_c = smooth_s[:, cols]
        unsmooth_c = unsmooth_s[:, cols]
        for r in range(0, count, SLAB):
            value = rows_ref[0, r : r + SLAB, cols].astype(f32) * unsmooth_c
            value = value * wide(inverse_r[0, r : r + SLAB, :], CHUNK)
            level = level_mixed(value) * wide(scale_r[0, r : r + SLAB, :], CHUNK)
            row_levels[slot, r : r + SLAB, :] = level.astype(bf16)
        for ref, base in weights:
            for f in range(0, hidden, SLAB):
                value = ref[0, f : f + SLAB, cols].astype(f32) * smooth_c
                value = value * wide(inverse_w[0, base + f : base + f + SLAB, :], CHUNK)
                levels[slot, base + f : base + f + SLAB, :] = level_bf16(value)

    def multiply(slot):
        acc[...] += dot_t(levels[slot], row_levels[slot])

    quantize(0, 0)

    def pair(i, carry):
        multiply(0)
        quantize(2 * i + 1, 1)
        multiply(1)
        quantize(2 * i + 2, 0)
        return carry

    lax.fori_loop(0, chunks // 2 - 1, pair, 0)
    multiply(0)
    quantize(chunks - 1, 1)
    multiply(1)

    hidden_ref[0] = silu_product(acc[...] * scale_w[0][:, :1])


def quant_hidden(rows, gate, up, smooth, scales, first, amount, space, at, into=None):
    count, depth = rows.shape[1:]
    hidden = gate.shape[1]
    extra = [] if into is None else [into]

    def spec(*tail):
        return pl.BlockSpec((1,) + tail, lambda e: (first + e,) + (0,) * len(tail))

    return pl.pallas_call(
        quant_kernel,
        grid=(amount,),
        out_shape=jax.ShapeDtypeStruct((space, count, hidden), bf16),
        in_specs=[spec(*a.shape[1:]) for a in (rows, gate, up, smooth) + scales]
        + [pl.BlockSpec(memory_space=pl.ANY)] * len(extra),
        out_specs=pl.BlockSpec((1, count, hidden), lambda e: (at + e, 0, 0)),
        input_output_aliases={8: 0} if extra else {},
        scratch_shapes=[
            pltpu.VMEM((SLAB, depth), f32),
            pltpu.VMEM((SLAB, depth), f32),
            pltpu.VMEM((2 * hidden, count), f32),
            pltpu.VMEM((2, 2 * hidden, CHUNK), bf16),
            pltpu.VMEM((2, count, CHUNK), bf16),
        ],
        compiler_params=params(),
        cost_estimate=BRIEF,
        name="quant_hidden",
    )(rows, gate, up, smooth, *scales, *extra)


def combine_kernel(quantized, skip, last, *refs):
    share_ref, hidden_ref, down_ref, scale_ref = refs[:4]
    e = pl.program_id(0)
    shards, _, count, part = hidden_ref.shape
    unit_rows = UNIT * CAP
    wide_s = refs[-1]
    for r in range(0, count, SLAB):
        spot = slice(r, r + SLAB)
        if not quantized:
            for s in range(shards):
                wide_s[spot, s * part : (s + 1) * part] = hidden_ref[s, 0, spot, :]
            continue
        top = None
        for s in range(shards):
            value = fold_max(jnp.abs(hidden_ref[s, 0, spot, :]).astype(f32))
            top = value if top is None else jnp.maximum(top, value)
        top = jnp.max(top, axis=1, keepdims=True) + EPS
        inverse, scale = LEVELS / top, top / LEVELS
        for s in range(shards):
            value = level_mixed(hidden_ref[s, 0, spot, :].astype(f32) * inverse) * scale
            wide_s[spot, s * part : (s + 1) * part] = value.astype(bf16)

    out = jnp.dot(wide_s[...], down_ref[0], preferred_element_type=f32) * scale_ref[0] * share_ref[0]
    out = out.astype(bf16)
    units = count // unit_rows
    if not last:
        for u in range(units):
            refs[-2][u] = out[u * unit_rows : (u + 1) * unit_rows]
        return
    hot_ref, out_ref, keep_s = refs[4], refs[-3], refs[-2]
    if skip:

        @pl.when(e == 0)
        def _():
            keep_s[:, : skip * unit_rows, :] = refs[5][...]

    at = pl.ds(pl.multiple_of((skip + e) * unit_rows, SLAB), unit_rows)
    for u in range(units):
        keep_s[u, at, :] = out[u * unit_rows : (u + 1) * unit_rows]

    @pl.when(e == pl.num_programs(0) - 1)
    def _():
        tokens = hot_ref.shape[1]
        for u in range(units):
            out_ref[u * tokens : (u + 1) * tokens, :] = jnp.dot(
                hot_ref[u], keep_s[u], preferred_element_type=f32
            ).astype(bf16)


def combine(hot_t, share, hidden, down, scale, quantized, first=0, at=0, pieces=1, last=True, earlier=None):
    units, unit_tokens, hot_rows = hot_t.shape
    shards, amount, count, part = hidden.shape
    units_hidden, width = down.shape[1:]
    block = width // pieces
    unit_rows = UNIT * CAP
    in_specs = [
        pl.BlockSpec((1, count, 1), lambda e: (first + e, 0, 0)),
        pl.BlockSpec((shards, 1, count, part), lambda e: (0, e, 0, 0)),
        pl.BlockSpec((1, units_hidden, block), lambda e: (first + e, 0, at)),
        pl.BlockSpec((1, 1, block), lambda e: (first + e, 0, at)),
    ]
    operands = [share, hidden, down, scale]
    scratch = [pltpu.VMEM((count, units_hidden), bf16)]
    if last:
        operands.append(hot_t)
        in_specs.append(pl.BlockSpec(hot_t.shape, lambda e: (0, 0, 0)))
        scratch = [pltpu.VMEM((units, hot_rows, block), bf16)] + scratch
        out_shape = jax.ShapeDtypeStruct((units * unit_tokens, block), bf16)
        out_spec = pl.BlockSpec((units * unit_tokens, block), lambda e: (0, 0))
        if first:
            operands.append(earlier)
            in_specs.append(pl.BlockSpec((units, first * unit_rows, block), lambda e: (0, 0, at)))
    else:
        out_shape = jax.ShapeDtypeStruct((units, amount * unit_rows, block), bf16)
        out_spec = pl.BlockSpec((units, unit_rows, block), lambda e: (0, e, 0))
    return pl.pallas_call(
        functools.partial(combine_kernel, quantized, first, last),
        grid=(amount,),
        out_shape=out_shape,
        in_specs=in_specs,
        out_specs=out_spec,
        scratch_shapes=scratch,
        compiler_params=params(),
        cost_estimate=BRIEF,
        name="combine_quant" if quantized else "combine_float",
    )(*operands)


def to_pairs(part, groups):
    width = part.shape[1]
    low = lax.axis_index("dp") & 1
    part = part.reshape(groups // 2, 2, -1, width)
    kept = lax.dynamic_index_in_dim(part, low, 1, keepdims=False)
    sent = lax.dynamic_index_in_dim(part, 1 - low, 1, keepdims=False)
    came = lax.ppermute(sent, "dp", [(i, i ^ 1) for i in range(groups)])
    return (kept.astype(f32) + came.astype(f32)).astype(bf16)


def to_tokens(both, groups):
    pairs = groups // 2
    high = lax.axis_index("dp") >> 1
    total = lax.dynamic_index_in_dim(both, high, 0, keepdims=False).astype(f32)
    for k in range(1, pairs):
        block = lax.dynamic_index_in_dim(both, lax.rem(high + k, pairs), 0, keepdims=False)
        came = lax.ppermute(block, "dp", [(i, (i + 2 * k) % groups) for i in range(groups)])
        total = total + came.astype(f32)
    return total


def from_all(x, axis):
    copies = jnp.broadcast_to(x, (lax.axis_size(axis),) + x.shape)
    return lax.all_to_all(copies, axis, split_axis=0, concat_axis=0)


def on_device(tokens, expert_ids, route_weights, gate_weight, up_weight, down_weight):
    groups = lax.axis_size("dp")
    experts = gate_weight.shape[0]
    choices = expert_ids.shape[1]

    payload = jnp.concatenate([expert_ids.T.astype(f32), route_weights.T], axis=0)
    route = from_all(payload, "dp").reshape(-1, payload.shape[1])
    shards = lax.axis_size("expert")
    same_core = [list(range(c, groups * shards, 2)) for c in range(2)]
    mine = lax.all_gather(tokens, ("dp", "expert"), axis=0, axis_index_groups=same_core)
    mine = mine.reshape((groups, shards // 2) + tokens.shape)
    core = (lax.axis_index("expert") & 1).astype(jnp.int32).reshape(1)

    local_peak = channel_peak(gate_weight, up_weight)
    weight_peak = from_all(local_peak.reshape(experts, -1).astype(bf16), "expert")
    weight_peak = jnp.max(weight_peak, axis=0).astype(f32)
    down_weight, local_peak = lax.optimization_barrier((down_weight, local_peak))
    levels, level_scale = down_quant(down_weight)

    first = (lax.axis_index("dp") * experts).astype(jnp.int32).reshape(1)
    hot, share = prep(first, route, experts, groups, choices)
    hot_t = jnp.swapaxes(hot, 1, 2)
    hot, levels, mine, weight_peak = lax.optimization_barrier((hot, levels, mine, weight_peak))
    other = lax.ppermute(mine, "expert", [(i, i ^ 1) for i in range(shards)])
    done = expert_rows(core, hot, mine, weight_peak, experts, groups)
    rows, smooth = expert_rows(1 - core, hot, other, weight_peak, experts, groups, done)

    hf, *scales = float_hidden(rows, gate_weight, up_weight, smooth)
    scales = tuple(scales)
    wide_f = lax.all_gather(hf, "expert", axis=0)

    half = experts // 2
    more = experts - half
    some = (3 * more) // 4
    operands = (gate_weight, up_weight, smooth, scales)
    hq = quant_hidden(rows, *operands, 0, half, half, 0)
    wide_q = [lax.all_gather(hq, "expert", axis=0)]
    wide_f, hq = lax.optimization_barrier((wide_f, hq))
    part_f = combine(hot_t, share, wide_f, down_weight, jnp.ones_like(level_scale), False)
    both_f = to_pairs(part_f, groups)
    rows, part_f = lax.optimization_barrier((rows, part_f))
    hq = quant_hidden(rows, *operands, half, some, more, 0) if some else None
    rows, both_f = lax.optimization_barrier((rows, both_f))
    out_f = to_tokens(both_f, groups)
    hq = quant_hidden(rows, *operands, half + some, more - some, more, some, hq)
    wide_q.append(lax.all_gather(hq, "expert", axis=0))
    share, hq = lax.optimization_barrier((share, hq))
    earlier = combine(hot_t, share, wide_q[0], levels, level_scale, True, last=False)
    earlier, out_f = lax.optimization_barrier((earlier, out_f))
    out_q = []
    for at in range(2):
        part_q = combine(
            hot_t, share, wide_q[1], levels, level_scale, True, half, at, 2, earlier=earlier
        )
        out_q.append(to_tokens(to_pairs(part_q, groups), groups).astype(bf16))
        earlier, part_q = lax.optimization_barrier((earlier, part_q))
    return jnp.concatenate(out_q, axis=1), out_f


def solution(mesh):
    in_specs = (
        P("dp", "expert"),
        P("dp", None),
        P("dp", None),
        P("dp", "expert", None),
        P("dp", "expert", None),
        P("dp", None, "expert"),
    )
    out_specs = (P("dp", "expert"), P("dp", "expert"))
    return jax.shard_map(
        on_device, mesh=mesh, in_specs=in_specs, out_specs=out_specs, check_vma=False
    )
```

```python
import functools

import jax
import jax.numpy as jnp
from jax import lax
from jax.experimental import pallas as pl
from jax.experimental.pallas import tpu as pltpu
from jax.sharding import PartitionSpec as P

CAP = 20
PAIR = 2
UNIT = 4
LEVELS = 7.0
EPS = 1e-06
VMEM = 56 * 1024 * 1024
LANES = 128
SLAB = 16
SPACING_ONE = 192.0
CHUNK = 1024
BRIEF = pl.CostEstimate(flops=1, bytes_accessed=1, transcendentals=0)

FRACTION_BF16 = (6.55787162, -12.52307356, 9.17209913)

bf16 = jnp.bfloat16
f32 = jnp.float32


def fraction(r, coefficients):
    dtype = r.dtype
    square = r * r
    total = jnp.asarray(coefficients[-1], dtype)
    for c in coefficients[-2::-1]:
        total = total * square + jnp.asarray(c, dtype)
    return (r * square) * total


def level_bf16(v):
    v = v.astype(bf16)
    offset = jnp.asarray(SPACING_ONE, bf16)
    n = (v + offset) - offset
    return n + fraction(v - n, FRACTION_BF16)


def level_mixed(v):
    n = jnp.round(v)
    return n + fraction((v - n).astype(bf16), FRACTION_BF16).astype(f32)


def fold_max(x):
    if x.shape[1] % LANES:
        return jnp.max(x, axis=1, keepdims=True)
    out = x[:, :LANES]
    for c in range(LANES, x.shape[1], LANES):
        out = jnp.maximum(out, x[:, c : c + LANES])
    return out


def wide(x, width):
    return jnp.concatenate([x] * (width // LANES), axis=1)


def dot_t(a, b):
    return lax.dot_general(a, b, (((1,), (1,)), ((), ())), preferred_element_type=f32)


def flipped(x):
    high, broad = -x.shape[0] % LANES, -x.shape[1] % LANES
    return jnp.pad(x, ((0, high), (0, broad))).T[: x.shape[1], : x.shape[0]]


def params():
    return pltpu.CompilerParams(vmem_limit_bytes=VMEM)


def prep_kernel(local_experts, groups, choices, first_ref, route_ref, hot_ref, pick_ref, share_ref):
    units = groups // UNIT
    group_tokens = route_ref.shape[1]
    unit_rows, unit_tokens = UNIT * CAP, UNIT * group_tokens
    first = first_ref[0].astype(f32)
    before = lax.broadcasted_iota(jnp.int32, (group_tokens, group_tokens), 0) < lax.broadcasted_iota(
        jnp.int32, (group_tokens, group_tokens), 1
    )
    before = jnp.where(before, 1.0, 0.0).astype(bf16)
    codes, weights = [], []
    for g in range(groups):
        base = 2 * choices * g
        ids = route_ref[base : base + choices, :]
        route = route_ref[base + choices : base + 2 * choices, :]
        shares = route / jnp.sum(route, axis=0, keepdims=True)
        hits, mine = [], []
        for e in range(local_experts):
            hit = ids == first + float(e)
            hits.append(jnp.max(jnp.where(hit, 1.0, 0.0), axis=0, keepdims=True))
            mine.append(jnp.sum(jnp.where(hit, shares, 0.0), axis=0, keepdims=True))
        part = jnp.concatenate(hits, axis=0)
        weights.append(jnp.concatenate(mine, axis=0))
        slot = jnp.dot(part.astype(bf16), before, preferred_element_type=f32)
        codes.append(jnp.where(part > 0.5, slot + float((g % UNIT) * CAP), -1.0))
    pair_rows, pair_tokens = PAIR * CAP, PAIR * group_tokens
    row = lax.broadcasted_iota(jnp.int32, (pair_rows, pair_tokens), 0).astype(f32)
    for v in range(groups // PAIR):
        code = jnp.concatenate(codes[v * PAIR : (v + 1) * PAIR], axis=1)
        base = row + float((v * PAIR) % UNIT * CAP)
        hot = [jnp.where(base == code[e : e + 1, :], 1.0, 0.0) for e in range(local_experts)]
        pick_ref[v] = jnp.concatenate(hot, axis=0).astype(bf16)
    row = lax.broadcasted_iota(jnp.int32, (unit_rows, unit_tokens), 0).astype(f32)
    for u in range(units):
        code = jnp.concatenate(codes[u * UNIT : (u + 1) * UNIT], axis=1)
        weight = jnp.concatenate(weights[u * UNIT : (u + 1) * UNIT], axis=1)
        for e in range(local_experts):
            hot = row == code[e : e + 1, :]
            hot_ref[u, e * unit_rows : (e + 1) * unit_rows, :] = jnp.where(hot, 1.0, 0.0).astype(bf16)
            share_ref[e, u * unit_rows : (u + 1) * unit_rows, :] = jnp.sum(
                jnp.where(hot, weight[e : e + 1, :], 0.0), axis=1, keepdims=True
            )


def prep(first, route, local_experts, groups, choices):
    units = groups // UNIT
    return pl.pallas_call(
        functools.partial(prep_kernel, local_experts, groups, choices),
        out_shape=(
            jax.ShapeDtypeStruct((units, local_experts * UNIT * CAP, UNIT * route.shape[1]), bf16),
            jax.ShapeDtypeStruct((groups // PAIR, local_experts * PAIR * CAP, PAIR * route.shape[1]), bf16),
            jax.ShapeDtypeStruct((local_experts, groups * CAP, 1), f32),
        ),
        in_specs=[
            pl.BlockSpec(memory_space=pltpu.SMEM),
            pl.BlockSpec(memory_space=pltpu.VMEM),
        ],
        out_specs=(pl.BlockSpec(memory_space=pltpu.VMEM),) * 3,
        compiler_params=params(),
        name="routing_tables",
    )(first, route)


def channel_peak_kernel(gate_ref, up_ref, peak_ref):
    hidden, depth = gate_ref.shape[1:]

    def one(i, carry):
        cols = pl.ds(pl.multiple_of(i * CHUNK, CHUNK), CHUNK)
        top = None
        for ref in (gate_ref, up_ref):
            for f in range(0, hidden, SLAB):
                value = jnp.abs(ref[0, f : f + SLAB, cols])
                top = value if top is None else jnp.maximum(top, value)
        peak_ref[0, :, cols] = jnp.max(top.astype(f32), axis=0, keepdims=True)
        return carry

    lax.fori_loop(0, depth // CHUNK, one, 0)


def channel_peak(gate, up):
    experts, hidden, depth = gate.shape
    spec = pl.BlockSpec((1, hidden, depth), lambda e: (e, 0, 0))
    return pl.pallas_call(
        channel_peak_kernel,
        grid=(experts,),
        out_shape=jax.ShapeDtypeStruct((experts, 1, depth), f32),
        in_specs=[spec, spec],
        out_specs=pl.BlockSpec((1, 1, depth), lambda e: (e, 0, 0)),
        compiler_params=params(),
        cost_estimate=BRIEF,
        name="channel_peak",
    )(gate, up)


def down_quant_kernel(rows, width, down_ref, level_ref, scale_ref):
    step = 32 * SLAB

    def peak(i, carry):
        base = pl.multiple_of(i * step, step)
        for j in range(0, step, SLAB):
            carry = jnp.maximum(carry, jnp.abs(down_ref[0, pl.ds(base + j, SLAB), :]))
        return carry

    top = lax.fori_loop(0, rows // step, peak, jnp.zeros((SLAB, width), bf16))
    top = jnp.max(top.astype(f32), axis=0, keepdims=True) + EPS
    scale_ref[0] = top / LEVELS
    inverse = jnp.broadcast_to(LEVELS / top, (SLAB, width))

    def quantize(i, carry):
        base = pl.multiple_of(i * step, step)
        for j in range(0, step, SLAB):
            value = down_ref[0, pl.ds(base + j, SLAB), :].astype(f32) * inverse
            level_ref[0, pl.ds(base + j, SLAB), :] = level_bf16(value)
        return carry

    lax.fori_loop(0, rows // step, quantize, 0)


def down_quant(down):
    experts, hidden, width = down.shape
    block = 512
    return pl.pallas_call(
        functools.partial(down_quant_kernel, hidden, block),
        grid=(experts, width // block),
        out_shape=(
            jax.ShapeDtypeStruct(down.shape, bf16),
            jax.ShapeDtypeStruct((experts, 1, width), f32),
        ),
        in_specs=[pl.BlockSpec((1, hidden, block), lambda e, c: (e, 0, c))],
        out_specs=(
            pl.BlockSpec((1, hidden, block), lambda e, c: (e, 0, c)),
            pl.BlockSpec((1, 1, block), lambda e, c: (e, 0, c)),
        ),
        compiler_params=params(),
        cost_estimate=BRIEF,
        name="down_levels",
    )(down)


def rows_kernel(local_experts, units, pick_ref, tokens_ref, peak_ref, rows_ref, smooth_ref):
    unit_rows, pair_rows = UNIT * CAP, PAIR * CAP
    group_tokens, width = tokens_ref.shape[2], tokens_ref.shape[3]
    top = [None] * local_experts
    for u in range(units):
        picked = []
        for v in range(u * UNIT // PAIR, (u + 1) * UNIT // PAIR):
            tokens = tokens_ref[v * PAIR : (v + 1) * PAIR, 0].reshape(PAIR * group_tokens, width)
            picked.append(jnp.dot(pick_ref[v], tokens, preferred_element_type=f32))
        for e in range(local_experts):
            part = jnp.concatenate([p[e * pair_rows : (e + 1) * pair_rows] for p in picked], axis=0)
            rows_ref[e, u * unit_rows : (u + 1) * unit_rows, :] = part.astype(bf16)
            most = jnp.max(jnp.abs(part), axis=0, keepdims=True)
            top[e] = most if top[e] is None else jnp.maximum(top[e], most)
    for e in range(local_experts):
        smooth_ref[e] = jnp.sqrt(jnp.maximum(top[e], 1.0) / (peak_ref[e : e + 1, :] + EPS))


def expert_rows(pick, tokens, weight_peak, local_experts, groups):
    shards, group_tokens, share = tokens.shape[1:]
    units = groups // UNIT
    block = 512
    per = share // block
    return pl.pallas_call(
        functools.partial(rows_kernel, local_experts, units),
        grid=(shards * per,),
        out_shape=(
            jax.ShapeDtypeStruct((local_experts, groups * CAP, shards * share), bf16),
            jax.ShapeDtypeStruct((local_experts, 1, shards * share), f32),
        ),
        in_specs=[
            pl.BlockSpec(pick.shape, lambda c: (0, 0, 0)),
            pl.BlockSpec((groups, 1, group_tokens, block), lambda c: (0, c // per, 0, c % per)),
            pl.BlockSpec((local_experts, block), lambda c: (0, c)),
        ],
        out_specs=(
            pl.BlockSpec((local_experts, groups * CAP, block), lambda c: (0, 0, c)),
            pl.BlockSpec((local_experts, 1, block), lambda c: (0, 0, c)),
        ),
        compiler_params=params(),
        name="expert_rows",
    )(pick, tokens, weight_peak)


def silu_product(both):
    half = both.shape[0] // 2
    gate, up = both[:half], both[half:]
    return flipped(gate / (1.0 + jnp.exp(-gate)) * up).astype(bf16)


def float_kernel(
    rows_ref, gate_ref, up_ref, smooth_ref,
    hidden_ref, inverse_w, scale_w, inverse_r, scale_r,
    smooth_s, unsmooth_s, top_s, top_r, acc,
):
    count = rows_ref.shape[1]
    hidden = gate_ref.shape[1]
    chunks = gate_ref.shape[2] // CHUNK
    weights = ((gate_ref, 0), (up_ref, hidden))

    smooth = smooth_ref[0]
    smooth_s[...] = jnp.broadcast_to(smooth, smooth_s.shape).astype(bf16)
    unsmooth_s[...] = jnp.broadcast_to(1.0 / smooth, unsmooth_s.shape)
    top_s[...] = jnp.zeros_like(top_s)
    top_r[...] = jnp.zeros_like(top_r)
    acc[...] = jnp.zeros_like(acc)

    def peaks(i, carry):
        cols = pl.ds(pl.multiple_of(i * CHUNK, CHUNK), CHUNK)
        smooth_c = smooth_s[:, cols]
        unsmooth_c = unsmooth_s[:, cols]
        rows = rows_ref[0, :, cols]
        for ref, base in weights:
            acc[base : base + hidden, :] += dot_t(ref[0, :, cols], rows)
            for f in range(0, hidden, SLAB):
                value = jnp.abs(ref[0, f : f + SLAB, cols]) * smooth_c
                spot = slice(base + f, base + f + SLAB)
                top_s[spot, :] = jnp.maximum(top_s[spot, :], fold_max(value))
        for r in range(0, count, SLAB):
            value = jnp.abs(rows_ref[0, r : r + SLAB, cols]).astype(f32) * unsmooth_c
            top_r[r : r + SLAB, :] = jnp.maximum(top_r[r : r + SLAB, :], fold_max(value))
        return carry

    lax.fori_loop(0, chunks, peaks, 0)
    hidden_ref[0] = silu_product(acc[...])

    for r in range(0, count, SLAB):
        top = jnp.max(top_r[r : r + SLAB, :], axis=1, keepdims=True) + EPS
        inverse_r[0, r : r + SLAB, :] = jnp.broadcast_to(LEVELS / top, (SLAB, LANES))
        scale_r[0, r : r + SLAB, :] = jnp.broadcast_to(top / LEVELS, (SLAB, LANES))
    for f in range(0, 2 * hidden, LANES):
        top = jnp.max(top_s[f : f + LANES, :].astype(f32), axis=1, keepdims=True) + EPS
        inverse_w[0, f : f + LANES, :] = jnp.broadcast_to(LEVELS / top, (LANES, LANES))
        scale_w[0, f : f + LANES, :] = jnp.broadcast_to(top / LEVELS, (LANES, LANES))


def float_hidden(rows, gate, up, smooth):
    experts, count, depth = rows.shape
    hidden = gate.shape[1]

    def spec(*tail):
        return pl.BlockSpec((1,) + tail, lambda e: (e,) + (0,) * len(tail))

    tails = ((count, hidden), (2 * hidden, LANES), (2 * hidden, LANES), (count, LANES), (count, LANES))
    kinds = (bf16, f32, f32, f32, f32)
    return pl.pallas_call(
        float_kernel,
        grid=(experts,),
        out_shape=tuple(jax.ShapeDtypeStruct((experts,) + s, k) for s, k in zip(tails, kinds)),
        in_specs=[spec(count, depth), spec(hidden, depth), spec(hidden, depth), spec(1, depth)],
        out_specs=tuple(spec(*s) for s in tails),
        scratch_shapes=[
            pltpu.VMEM((SLAB, depth), bf16),
            pltpu.VMEM((SLAB, depth), f32),
            pltpu.VMEM((2 * hidden, LANES), bf16),
            pltpu.VMEM((count, LANES), f32),
            pltpu.VMEM((2 * hidden, count), f32),
        ],
        compiler_params=params(),
        cost_estimate=BRIEF,
        name="float_hidden",
    )(rows, gate, up, smooth)


def quant_kernel(
    rows_ref, gate_ref, up_ref, smooth_ref, inverse_w, scale_w, inverse_r, scale_r, *refs
):
    hidden_ref, smooth_s, unsmooth_s, acc, levels, row_levels = refs[-6:]
    count = rows_ref.shape[1]
    hidden = gate_ref.shape[1]
    chunks = gate_ref.shape[2] // CHUNK
    weights = ((gate_ref, 0), (up_ref, hidden))

    smooth = smooth_ref[0]
    smooth_s[...] = jnp.broadcast_to(smooth, smooth_s.shape)
    unsmooth_s[...] = jnp.broadcast_to(1.0 / smooth, unsmooth_s.shape)
    acc[...] = jnp.zeros_like(acc)

    def quantize(i, slot):
        cols = pl.ds(pl.multiple_of(i * CHUNK, CHUNK), CHUNK)
        smooth_c = smooth_s[:, cols]
        unsmooth_c = unsmooth_s[:, cols]
        for r in range(0, count, SLAB):
            value = rows_ref[0, r : r + SLAB, cols].astype(f32) * unsmooth_c
            value = value * wide(inverse_r[0, r : r + SLAB, :], CHUNK)
            level = level_mixed(value) * wide(scale_r[0, r : r + SLAB, :], CHUNK)
            row_levels[slot, r : r + SLAB, :] = level.astype(bf16)
        for ref, base in weights:
            for f in range(0, hidden, SLAB):
                value = ref[0, f : f + SLAB, cols].astype(f32) * smooth_c
                value = value * wide(inverse_w[0, base + f : base + f + SLAB, :], CHUNK)
                levels[slot, base + f : base + f + SLAB, :] = level_bf16(value)

    def multiply(slot):
        acc[...] += dot_t(levels[slot], row_levels[slot])

    quantize(0, 0)

    def pair(i, carry):
        multiply(0)
        quantize(2 * i + 1, 1)
        multiply(1)
        quantize(2 * i + 2, 0)
        return carry

    lax.fori_loop(0, chunks // 2 - 1, pair, 0)
    multiply(0)
    quantize(chunks - 1, 1)
    multiply(1)

    hidden_ref[0] = silu_product(acc[...] * scale_w[0][:, :1])


def quant_hidden(rows, gate, up, smooth, scales, first, amount, space, at, into=None):
    count, depth = rows.shape[1:]
    hidden = gate.shape[1]
    extra = [] if into is None else [into]

    def spec(*tail):
        return pl.BlockSpec((1,) + tail, lambda e: (first + e,) + (0,) * len(tail))

    return pl.pallas_call(
        quant_kernel,
        grid=(amount,),
        out_shape=jax.ShapeDtypeStruct((space, count, hidden), bf16),
        in_specs=[spec(*a.shape[1:]) for a in (rows, gate, up, smooth) + scales]
        + [pl.BlockSpec(memory_space=pl.ANY)] * len(extra),
        out_specs=pl.BlockSpec((1, count, hidden), lambda e: (at + e, 0, 0)),
        input_output_aliases={8: 0} if extra else {},
        scratch_shapes=[
            pltpu.VMEM((SLAB, depth), f32),
            pltpu.VMEM((SLAB, depth), f32),
            pltpu.VMEM((2 * hidden, count), f32),
            pltpu.VMEM((2, 2 * hidden, CHUNK), bf16),
            pltpu.VMEM((2, count, CHUNK), bf16),
        ],
        compiler_params=params(),
        cost_estimate=BRIEF,
        name="quant_hidden",
    )(rows, gate, up, smooth, *scales, *extra)


def combine_kernel(quantized, skip, last, *refs):
    share_ref, hidden_ref, down_ref, scale_ref = refs[:4]
    e = pl.program_id(0)
    shards, _, count, part = hidden_ref.shape
    unit_rows = UNIT * CAP
    wide_s = refs[-1]
    for r in range(0, count, SLAB):
        spot = slice(r, r + SLAB)
        if not quantized:
            for s in range(shards):
                wide_s[spot, s * part : (s + 1) * part] = hidden_ref[s, 0, spot, :]
            continue
        top = None
        for s in range(shards):
            value = fold_max(jnp.abs(hidden_ref[s, 0, spot, :]).astype(f32))
            top = value if top is None else jnp.maximum(top, value)
        top = jnp.max(top, axis=1, keepdims=True) + EPS
        inverse, scale = LEVELS / top, top / LEVELS
        for s in range(shards):
            value = level_mixed(hidden_ref[s, 0, spot, :].astype(f32) * inverse) * scale
            wide_s[spot, s * part : (s + 1) * part] = value.astype(bf16)

    out = jnp.dot(wide_s[...], down_ref[0], preferred_element_type=f32) * scale_ref[0] * share_ref[0]
    out = out.astype(bf16)
    units = count // unit_rows
    if not last:
        for u in range(units):
            refs[-2][u] = out[u * unit_rows : (u + 1) * unit_rows]
        return
    hot_ref, out_ref, keep_s = refs[4], refs[-3], refs[-2]
    if skip:

        @pl.when(e == 0)
        def _():
            keep_s[:, : skip * unit_rows, :] = refs[5][...]

    at = pl.ds(pl.multiple_of((skip + e) * unit_rows, SLAB), unit_rows)
    for u in range(units):
        keep_s[u, at, :] = out[u * unit_rows : (u + 1) * unit_rows]

    @pl.when(e == pl.num_programs(0) - 1)
    def _():
        tokens = hot_ref.shape[1]
        for u in range(units):
            out_ref[u * tokens : (u + 1) * tokens, :] = jnp.dot(
                hot_ref[u], keep_s[u], preferred_element_type=f32
            ).astype(bf16)


def combine(hot_t, share, hidden, down, scale, quantized, first=0, at=0, pieces=1, last=True, earlier=None):
    units, unit_tokens, hot_rows = hot_t.shape
    shards, amount, count, part = hidden.shape
    units_hidden, width = down.shape[1:]
    block = width // pieces
    unit_rows = UNIT * CAP
    in_specs = [
        pl.BlockSpec((1, count, 1), lambda e: (first + e, 0, 0)),
        pl.BlockSpec((shards, 1, count, part), lambda e: (0, e, 0, 0)),
        pl.BlockSpec((1, units_hidden, block), lambda e: (first + e, 0, at)),
        pl.BlockSpec((1, 1, block), lambda e: (first + e, 0, at)),
    ]
    operands = [share, hidden, down, scale]
    scratch = [pltpu.VMEM((count, units_hidden), bf16)]
    if last:
        operands.append(hot_t)
        in_specs.append(pl.BlockSpec(hot_t.shape, lambda e: (0, 0, 0)))
        scratch = [pltpu.VMEM((units, hot_rows, block), bf16)] + scratch
        out_shape = jax.ShapeDtypeStruct((units * unit_tokens, block), bf16)
        out_spec = pl.BlockSpec((units * unit_tokens, block), lambda e: (0, 0))
        if first:
            operands.append(earlier)
            in_specs.append(pl.BlockSpec((units, first * unit_rows, block), lambda e: (0, 0, at)))
    else:
        out_shape = jax.ShapeDtypeStruct((units, amount * unit_rows, block), bf16)
        out_spec = pl.BlockSpec((units, unit_rows, block), lambda e: (0, e, 0))
    return pl.pallas_call(
        functools.partial(combine_kernel, quantized, first, last),
        grid=(amount,),
        out_shape=out_shape,
        in_specs=in_specs,
        out_specs=out_spec,
        scratch_shapes=scratch,
        compiler_params=params(),
        cost_estimate=BRIEF,
        name="combine_quant" if quantized else "combine_float",
    )(*operands)


def to_pairs(part, groups):
    width = part.shape[1]
    low = lax.axis_index("dp") & 1
    part = part.reshape(groups // 2, 2, -1, width)
    kept = lax.dynamic_index_in_dim(part, low, 1, keepdims=False)
    sent = lax.dynamic_index_in_dim(part, 1 - low, 1, keepdims=False)
    came = lax.ppermute(sent, "dp", [(i, i ^ 1) for i in range(groups)])
    return (kept.astype(f32) + came.astype(f32)).astype(bf16)


def to_tokens(both, groups):
    pairs = groups // 2
    high = lax.axis_index("dp") >> 1
    total = lax.dynamic_index_in_dim(both, high, 0, keepdims=False).astype(f32)
    for k in range(1, pairs):
        block = lax.dynamic_index_in_dim(both, lax.rem(high + k, pairs), 0, keepdims=False)
        came = lax.ppermute(block, "dp", [(i, (i + 2 * k) % groups) for i in range(groups)])
        total = total + came.astype(f32)
    return total


def from_all(x, axis):
    copies = jnp.broadcast_to(x, (lax.axis_size(axis),) + x.shape)
    return lax.all_to_all(copies, axis, split_axis=0, concat_axis=0)


def on_device(tokens, expert_ids, route_weights, gate_weight, up_weight, down_weight):
    groups = lax.axis_size("dp")
    experts = gate_weight.shape[0]
    choices = expert_ids.shape[1]

    payload = jnp.concatenate([expert_ids.T.astype(f32), route_weights.T], axis=0)
    route = from_all(payload, "dp").reshape(-1, payload.shape[1])
    all_tokens = lax.all_gather(tokens, ("dp", "expert"), axis=0)
    all_tokens = all_tokens.reshape((groups, -1) + tokens.shape)

    local_peak = channel_peak(gate_weight, up_weight)
    weight_peak = from_all(local_peak.reshape(experts, -1).astype(bf16), "expert")
    weight_peak = jnp.max(weight_peak, axis=0).astype(f32)
    down_weight, local_peak = lax.optimization_barrier((down_weight, local_peak))
    levels, level_scale = down_quant(down_weight)

    first = (lax.axis_index("dp") * experts).astype(jnp.int32).reshape(1)
    hot, pick, share = prep(first, route, experts, groups, choices)
    hot_t = jnp.swapaxes(hot, 1, 2)
    pick, levels = lax.optimization_barrier((pick, levels))
    rows, smooth = expert_rows(pick, all_tokens, weight_peak, experts, groups)

    hf, *scales = float_hidden(rows, gate_weight, up_weight, smooth)
    scales = tuple(scales)
    wide_f = lax.all_gather(hf, "expert", axis=0)

    half = experts // 2
    more = experts - half
    some = (3 * more) // 4
    operands = (gate_weight, up_weight, smooth, scales)
    hq = quant_hidden(rows, *operands, 0, half, half, 0)
    wide_q = [lax.all_gather(hq, "expert", axis=0)]
    wide_f, hq = lax.optimization_barrier((wide_f, hq))
    part_f = combine(hot_t, share, wide_f, down_weight, jnp.ones_like(level_scale), False)
    both_f = to_pairs(part_f, groups)
    rows, part_f = lax.optimization_barrier((rows, part_f))
    hq = quant_hidden(rows, *operands, half, some, more, 0) if some else None
    rows, both_f = lax.optimization_barrier((rows, both_f))
    out_f = to_tokens(both_f, groups)
    hq = quant_hidden(rows, *operands, half + some, more - some, more, some, hq)
    wide_q.append(lax.all_gather(hq, "expert", axis=0))
    share, hq = lax.optimization_barrier((share, hq))
    earlier = combine(hot_t, share, wide_q[0], levels, level_scale, True, last=False)
    out_q = []
    for at in range(2):
        part_q = combine(
            hot_t, share, wide_q[1], levels, level_scale, True, half, at, 2, earlier=earlier
        )
        out_q.append(to_tokens(to_pairs(part_q, groups), groups).astype(bf16))
        earlier, part_q, out_f = lax.optimization_barrier((earlier, part_q, out_f))
    return jnp.concatenate(out_q, axis=1), out_f


def solution(mesh):
    in_specs = (
        P("dp", "expert"),
        P("dp", None),
        P("dp", None),
        P("dp", "expert", None),
        P("dp", "expert", None),
        P("dp", None, "expert"),
    )
    out_specs = (P("dp", "expert"), P("dp", "expert"))
    return jax.shard_map(
        on_device, mesh=mesh, in_specs=in_specs, out_specs=out_specs, check_vma=False
    )
```

```python
import functools

import jax
import jax.numpy as jnp
from jax import lax
from jax.experimental import pallas as pl
from jax.experimental.pallas import tpu as pltpu
from jax.sharding import PartitionSpec as P

CAP = 20
PAIR = 2
UNIT = 4
LEVELS = 7.0
EPS = 1e-06
VMEM = 56 * 1024 * 1024
LANES = 128
SLAB = 16
SPACING_ONE = 192.0
CHUNK = 1024
BRIEF = pl.CostEstimate(flops=1, bytes_accessed=1, transcendentals=0)

FRACTION_BF16 = (6.55787162, -12.52307356, 9.17209913)

bf16 = jnp.bfloat16
f32 = jnp.float32


def fraction(r, coefficients):
    dtype = r.dtype
    square = r * r
    total = jnp.asarray(coefficients[-1], dtype)
    for c in coefficients[-2::-1]:
        total = total * square + jnp.asarray(c, dtype)
    return (r * square) * total


def level_bf16(v):
    v = v.astype(bf16)
    offset = jnp.asarray(SPACING_ONE, bf16)
    n = (v + offset) - offset
    return n + fraction(v - n, FRACTION_BF16)


def level_mixed(v):
    n = jnp.round(v)
    return n + fraction((v - n).astype(bf16), FRACTION_BF16).astype(f32)


def fold_max(x):
    if x.shape[1] % LANES:
        return jnp.max(x, axis=1, keepdims=True)
    out = x[:, :LANES]
    for c in range(LANES, x.shape[1], LANES):
        out = jnp.maximum(out, x[:, c : c + LANES])
    return out


def wide(x, width):
    return jnp.concatenate([x] * (width // LANES), axis=1)


def dot_t(a, b):
    return lax.dot_general(a, b, (((1,), (1,)), ((), ())), preferred_element_type=f32)


def flipped(x):
    high, broad = -x.shape[0] % LANES, -x.shape[1] % LANES
    return jnp.pad(x, ((0, high), (0, broad))).T[: x.shape[1], : x.shape[0]]


def params():
    return pltpu.CompilerParams(vmem_limit_bytes=VMEM)


def prep_kernel(local_experts, groups, choices, first_ref, route_ref, hot_ref, pick_ref, share_ref):
    units = groups // UNIT
    group_tokens = route_ref.shape[1]
    unit_rows, unit_tokens = UNIT * CAP, UNIT * group_tokens
    first = first_ref[0].astype(f32)
    before = lax.broadcasted_iota(jnp.int32, (group_tokens, group_tokens), 0) < lax.broadcasted_iota(
        jnp.int32, (group_tokens, group_tokens), 1
    )
    before = jnp.where(before, 1.0, 0.0).astype(bf16)
    codes, weights = [], []
    for g in range(groups):
        base = 2 * choices * g
        ids = route_ref[base : base + choices, :]
        route = route_ref[base + choices : base + 2 * choices, :]
        shares = route / jnp.sum(route, axis=0, keepdims=True)
        hits, mine = [], []
        for e in range(local_experts):
            hit = ids == first + float(e)
            hits.append(jnp.max(jnp.where(hit, 1.0, 0.0), axis=0, keepdims=True))
            mine.append(jnp.sum(jnp.where(hit, shares, 0.0), axis=0, keepdims=True))
        part = jnp.concatenate(hits, axis=0)
        weights.append(jnp.concatenate(mine, axis=0))
        slot = jnp.dot(part.astype(bf16), before, preferred_element_type=f32)
        codes.append(jnp.where(part > 0.5, slot + float((g % UNIT) * CAP), -1.0))
    pair_rows, pair_tokens = PAIR * CAP, PAIR * group_tokens
    row = lax.broadcasted_iota(jnp.int32, (pair_rows, pair_tokens), 0).astype(f32)
    for v in range(groups // PAIR):
        code = jnp.concatenate(codes[v * PAIR : (v + 1) * PAIR], axis=1)
        base = row + float((v * PAIR) % UNIT * CAP)
        hot = [jnp.where(base == code[e : e + 1, :], 1.0, 0.0) for e in range(local_experts)]
        pick_ref[v] = jnp.concatenate(hot, axis=0).astype(bf16)
    row = lax.broadcasted_iota(jnp.int32, (unit_rows, unit_tokens), 0).astype(f32)
    for u in range(units):
        code = jnp.concatenate(codes[u * UNIT : (u + 1) * UNIT], axis=1)
        weight = jnp.concatenate(weights[u * UNIT : (u + 1) * UNIT], axis=1)
        for e in range(local_experts):
            hot = row == code[e : e + 1, :]
            hot_ref[u, e * unit_rows : (e + 1) * unit_rows, :] = jnp.where(hot, 1.0, 0.0).astype(bf16)
            share_ref[e, u * unit_rows : (u + 1) * unit_rows, :] = jnp.sum(
                jnp.where(hot, weight[e : e + 1, :], 0.0), axis=1, keepdims=True
            )


def prep(first, route, local_experts, groups, choices):
    units = groups // UNIT
    return pl.pallas_call(
        functools.partial(prep_kernel, local_experts, groups, choices),
        out_shape=(
            jax.ShapeDtypeStruct((units, local_experts * UNIT * CAP, UNIT * route.shape[1]), bf16),
            jax.ShapeDtypeStruct((groups // PAIR, local_experts * PAIR * CAP, PAIR * route.shape[1]), bf16),
            jax.ShapeDtypeStruct((local_experts, groups * CAP, 1), f32),
        ),
        in_specs=[
            pl.BlockSpec(memory_space=pltpu.SMEM),
            pl.BlockSpec(memory_space=pltpu.VMEM),
        ],
        out_specs=(pl.BlockSpec(memory_space=pltpu.VMEM),) * 3,
        compiler_params=params(),
        name="routing_tables",
    )(first, route)


def channel_peak_kernel(gate_ref, up_ref, peak_ref):
    hidden, depth = gate_ref.shape[1:]

    def one(i, carry):
        cols = pl.ds(pl.multiple_of(i * CHUNK, CHUNK), CHUNK)
        top = None
        for ref in (gate_ref, up_ref):
            for f in range(0, hidden, SLAB):
                value = jnp.abs(ref[0, f : f + SLAB, cols])
                top = value if top is None else jnp.maximum(top, value)
        peak_ref[0, :, cols] = jnp.max(top.astype(f32), axis=0, keepdims=True)
        return carry

    lax.fori_loop(0, depth // CHUNK, one, 0)


def channel_peak(gate, up):
    experts, hidden, depth = gate.shape
    spec = pl.BlockSpec((1, hidden, depth), lambda e: (e, 0, 0))
    return pl.pallas_call(
        channel_peak_kernel,
        grid=(experts,),
        out_shape=jax.ShapeDtypeStruct((experts, 1, depth), f32),
        in_specs=[spec, spec],
        out_specs=pl.BlockSpec((1, 1, depth), lambda e: (e, 0, 0)),
        compiler_params=params(),
        cost_estimate=BRIEF,
        name="channel_peak",
    )(gate, up)


def down_quant_kernel(rows, width, down_ref, level_ref, scale_ref):
    step = 32 * SLAB

    def peak(i, carry):
        base = pl.multiple_of(i * step, step)
        for j in range(0, step, SLAB):
            carry = jnp.maximum(carry, jnp.abs(down_ref[0, pl.ds(base + j, SLAB), :]))
        return carry

    top = lax.fori_loop(0, rows // step, peak, jnp.zeros((SLAB, width), bf16))
    top = jnp.max(top.astype(f32), axis=0, keepdims=True) + EPS
    scale_ref[0] = top / LEVELS
    inverse = jnp.broadcast_to(LEVELS / top, (SLAB, width))

    def quantize(i, carry):
        base = pl.multiple_of(i * step, step)
        for j in range(0, step, SLAB):
            value = down_ref[0, pl.ds(base + j, SLAB), :].astype(f32) * inverse
            level_ref[0, pl.ds(base + j, SLAB), :] = level_bf16(value)
        return carry

    lax.fori_loop(0, rows // step, quantize, 0)


def down_quant(down):
    experts, hidden, width = down.shape
    block = 512
    return pl.pallas_call(
        functools.partial(down_quant_kernel, hidden, block),
        grid=(experts, width // block),
        out_shape=(
            jax.ShapeDtypeStruct(down.shape, bf16),
            jax.ShapeDtypeStruct((experts, 1, width), f32),
        ),
        in_specs=[pl.BlockSpec((1, hidden, block), lambda e, c: (e, 0, c))],
        out_specs=(
            pl.BlockSpec((1, hidden, block), lambda e, c: (e, 0, c)),
            pl.BlockSpec((1, 1, block), lambda e, c: (e, 0, c)),
        ),
        compiler_params=params(),
        cost_estimate=BRIEF,
        name="down_levels",
    )(down)


def rows_kernel(local_experts, units, pick_ref, tokens_ref, peak_ref, rows_ref, smooth_ref):
    unit_rows, pair_rows = UNIT * CAP, PAIR * CAP
    group_tokens, width = tokens_ref.shape[2], tokens_ref.shape[3]
    top = [None] * local_experts
    for u in range(units):
        picked = []
        for v in range(u * UNIT // PAIR, (u + 1) * UNIT // PAIR):
            tokens = tokens_ref[v * PAIR : (v + 1) * PAIR, 0].reshape(PAIR * group_tokens, width)
            picked.append(jnp.dot(pick_ref[v], tokens, preferred_element_type=f32))
        for e in range(local_experts):
            part = jnp.concatenate([p[e * pair_rows : (e + 1) * pair_rows] for p in picked], axis=0)
            rows_ref[e, u * unit_rows : (u + 1) * unit_rows, :] = part.astype(bf16)
            most = jnp.max(jnp.abs(part), axis=0, keepdims=True)
            top[e] = most if top[e] is None else jnp.maximum(top[e], most)
    for e in range(local_experts):
        smooth_ref[e] = jnp.sqrt(jnp.maximum(top[e], 1.0) / (peak_ref[e : e + 1, :] + EPS))


def expert_rows(pick, tokens, weight_peak, local_experts, groups):
    shards, group_tokens, share = tokens.shape[1:]
    units = groups // UNIT
    block = 512
    per = share // block
    return pl.pallas_call(
        functools.partial(rows_kernel, local_experts, units),
        grid=(shards * per,),
        out_shape=(
            jax.ShapeDtypeStruct((local_experts, groups * CAP, shards * share), bf16),
            jax.ShapeDtypeStruct((local_experts, 1, shards * share), f32),
        ),
        in_specs=[
            pl.BlockSpec(pick.shape, lambda c: (0, 0, 0)),
            pl.BlockSpec((groups, 1, group_tokens, block), lambda c: (0, c // per, 0, c % per)),
            pl.BlockSpec((local_experts, block), lambda c: (0, c)),
        ],
        out_specs=(
            pl.BlockSpec((local_experts, groups * CAP, block), lambda c: (0, 0, c)),
            pl.BlockSpec((local_experts, 1, block), lambda c: (0, 0, c)),
        ),
        compiler_params=params(),
        name="expert_rows",
    )(pick, tokens, weight_peak)


def silu_product(both):
    half = both.shape[0] // 2
    gate, up = both[:half], both[half:]
    return flipped(gate / (1.0 + jnp.exp(-gate)) * up).astype(bf16)


def float_kernel(
    rows_ref, gate_ref, up_ref, smooth_ref,
    hidden_ref, inverse_w, scale_w, inverse_r, scale_r,
    smooth_s, unsmooth_s, top_s, top_r, acc,
):
    count = rows_ref.shape[1]
    hidden = gate_ref.shape[1]
    chunks = gate_ref.shape[2] // CHUNK
    weights = ((gate_ref, 0), (up_ref, hidden))

    smooth = smooth_ref[0]
    smooth_s[...] = jnp.broadcast_to(smooth, smooth_s.shape).astype(bf16)
    unsmooth_s[...] = jnp.broadcast_to(1.0 / smooth, unsmooth_s.shape)
    top_s[...] = jnp.zeros_like(top_s)
    top_r[...] = jnp.zeros_like(top_r)
    acc[...] = jnp.zeros_like(acc)

    def peaks(i, carry):
        cols = pl.ds(pl.multiple_of(i * CHUNK, CHUNK), CHUNK)
        smooth_c = smooth_s[:, cols]
        unsmooth_c = unsmooth_s[:, cols]
        rows = rows_ref[0, :, cols]
        for ref, base in weights:
            acc[base : base + hidden, :] += dot_t(ref[0, :, cols], rows)
            for f in range(0, hidden, SLAB):
                value = jnp.abs(ref[0, f : f + SLAB, cols]) * smooth_c
                spot = slice(base + f, base + f + SLAB)
                top_s[spot, :] = jnp.maximum(top_s[spot, :], fold_max(value))
        for r in range(0, count, SLAB):
            value = jnp.abs(rows_ref[0, r : r + SLAB, cols]).astype(f32) * unsmooth_c
            top_r[r : r + SLAB, :] = jnp.maximum(top_r[r : r + SLAB, :], fold_max(value))
        return carry

    lax.fori_loop(0, chunks, peaks, 0)
    hidden_ref[0] = silu_product(acc[...])

    for r in range(0, count, SLAB):
        top = jnp.max(top_r[r : r + SLAB, :], axis=1, keepdims=True) + EPS
        inverse_r[0, r : r + SLAB, :] = jnp.broadcast_to(LEVELS / top, (SLAB, LANES))
        scale_r[0, r : r + SLAB, :] = jnp.broadcast_to(top / LEVELS, (SLAB, LANES))
    for f in range(0, 2 * hidden, LANES):
        top = jnp.max(top_s[f : f + LANES, :].astype(f32), axis=1, keepdims=True) + EPS
        inverse_w[0, f : f + LANES, :] = jnp.broadcast_to(LEVELS / top, (LANES, LANES))
        scale_w[0, f : f + LANES, :] = jnp.broadcast_to(top / LEVELS, (LANES, LANES))


def float_hidden(rows, gate, up, smooth):
    experts, count, depth = rows.shape
    hidden = gate.shape[1]

    def spec(*tail):
        return pl.BlockSpec((1,) + tail, lambda e: (e,) + (0,) * len(tail))

    tails = ((count, hidden), (2 * hidden, LANES), (2 * hidden, LANES), (count, LANES), (count, LANES))
    kinds = (bf16, f32, f32, f32, f32)
    return pl.pallas_call(
        float_kernel,
        grid=(experts,),
        out_shape=tuple(jax.ShapeDtypeStruct((experts,) + s, k) for s, k in zip(tails, kinds)),
        in_specs=[spec(count, depth), spec(hidden, depth), spec(hidden, depth), spec(1, depth)],
        out_specs=tuple(spec(*s) for s in tails),
        scratch_shapes=[
            pltpu.VMEM((SLAB, depth), bf16),
            pltpu.VMEM((SLAB, depth), f32),
            pltpu.VMEM((2 * hidden, LANES), bf16),
            pltpu.VMEM((count, LANES), f32),
            pltpu.VMEM((2 * hidden, count), f32),
        ],
        compiler_params=params(),
        cost_estimate=BRIEF,
        name="float_hidden",
    )(rows, gate, up, smooth)


def quant_kernel(
    rows_ref, gate_ref, up_ref, smooth_ref, inverse_w, scale_w, inverse_r, scale_r, *refs
):
    hidden_ref, smooth_s, unsmooth_s, acc, levels, row_levels = refs[-6:]
    count = rows_ref.shape[1]
    hidden = gate_ref.shape[1]
    chunks = gate_ref.shape[2] // CHUNK
    weights = ((gate_ref, 0), (up_ref, hidden))

    smooth = smooth_ref[0]
    smooth_s[...] = jnp.broadcast_to(smooth, smooth_s.shape)
    unsmooth_s[...] = jnp.broadcast_to(1.0 / smooth, unsmooth_s.shape)
    acc[...] = jnp.zeros_like(acc)

    def quantize(i, slot):
        cols = pl.ds(pl.multiple_of(i * CHUNK, CHUNK), CHUNK)
        smooth_c = smooth_s[:, cols]
        unsmooth_c = unsmooth_s[:, cols]
        for r in range(0, count, SLAB):
            value = rows_ref[0, r : r + SLAB, cols].astype(f32) * unsmooth_c
            value = value * wide(inverse_r[0, r : r + SLAB, :], CHUNK)
            level = level_mixed(value) * wide(scale_r[0, r : r + SLAB, :], CHUNK)
            row_levels[slot, r : r + SLAB, :] = level.astype(bf16)
        for ref, base in weights:
            for f in range(0, hidden, SLAB):
                value = ref[0, f : f + SLAB, cols].astype(f32) * smooth_c
                value = value * wide(inverse_w[0, base + f : base + f + SLAB, :], CHUNK)
                levels[slot, base + f : base + f + SLAB, :] = level_bf16(value)

    def multiply(slot):
        acc[...] += dot_t(levels[slot], row_levels[slot])

    quantize(0, 0)

    def pair(i, carry):
        multiply(0)
        quantize(2 * i + 1, 1)
        multiply(1)
        quantize(2 * i + 2, 0)
        return carry

    lax.fori_loop(0, chunks // 2 - 1, pair, 0)
    multiply(0)
    quantize(chunks - 1, 1)
    multiply(1)

    hidden_ref[0] = silu_product(acc[...] * scale_w[0][:, :1])


def quant_hidden(rows, gate, up, smooth, scales, first, amount, space, at, into=None):
    count, depth = rows.shape[1:]
    hidden = gate.shape[1]
    extra = [] if into is None else [into]

    def spec(*tail):
        return pl.BlockSpec((1,) + tail, lambda e: (first + e,) + (0,) * len(tail))

    return pl.pallas_call(
        quant_kernel,
        grid=(amount,),
        out_shape=jax.ShapeDtypeStruct((space, count, hidden), bf16),
        in_specs=[spec(*a.shape[1:]) for a in (rows, gate, up, smooth) + scales]
        + [pl.BlockSpec(memory_space=pl.ANY)] * len(extra),
        out_specs=pl.BlockSpec((1, count, hidden), lambda e: (at + e, 0, 0)),
        input_output_aliases={8: 0} if extra else {},
        scratch_shapes=[
            pltpu.VMEM((SLAB, depth), f32),
            pltpu.VMEM((SLAB, depth), f32),
            pltpu.VMEM((2 * hidden, count), f32),
            pltpu.VMEM((2, 2 * hidden, CHUNK), bf16),
            pltpu.VMEM((2, count, CHUNK), bf16),
        ],
        compiler_params=params(),
        cost_estimate=BRIEF,
        name="quant_hidden",
    )(rows, gate, up, smooth, *scales, *extra)


def combine_kernel(quantized, skip, last, *refs):
    share_ref, hidden_ref, down_ref, scale_ref = refs[:4]
    e = pl.program_id(0)
    shards, _, count, part = hidden_ref.shape
    unit_rows = UNIT * CAP
    wide_s = refs[-1]
    for r in range(0, count, SLAB):
        spot = slice(r, r + SLAB)
        if not quantized:
            for s in range(shards):
                wide_s[spot, s * part : (s + 1) * part] = hidden_ref[s, 0, spot, :]
            continue
        top = None
        for s in range(shards):
            value = fold_max(jnp.abs(hidden_ref[s, 0, spot, :]).astype(f32))
            top = value if top is None else jnp.maximum(top, value)
        top = jnp.max(top, axis=1, keepdims=True) + EPS
        inverse, scale = LEVELS / top, top / LEVELS
        for s in range(shards):
            value = level_mixed(hidden_ref[s, 0, spot, :].astype(f32) * inverse) * scale
            wide_s[spot, s * part : (s + 1) * part] = value.astype(bf16)

    out = jnp.dot(wide_s[...], down_ref[0], preferred_element_type=f32) * scale_ref[0] * share_ref[0]
    out = out.astype(bf16)
    units = count // unit_rows
    if not last:
        for u in range(units):
            refs[-2][u] = out[u * unit_rows : (u + 1) * unit_rows]
        return
    hot_ref, out_ref, keep_s = refs[4], refs[-3], refs[-2]
    if skip:

        @pl.when(e == 0)
        def _():
            keep_s[:, : skip * unit_rows, :] = refs[5][...]

    at = pl.ds(pl.multiple_of((skip + e) * unit_rows, SLAB), unit_rows)
    for u in range(units):
        keep_s[u, at, :] = out[u * unit_rows : (u + 1) * unit_rows]

    @pl.when(e == pl.num_programs(0) - 1)
    def _():
        tokens = hot_ref.shape[1]
        for u in range(units):
            out_ref[u * tokens : (u + 1) * tokens, :] = jnp.dot(
                hot_ref[u], keep_s[u], preferred_element_type=f32
            ).astype(bf16)


def combine(hot_t, share, hidden, down, scale, quantized, first=0, at=0, pieces=1, last=True, earlier=None):
    units, unit_tokens, hot_rows = hot_t.shape
    shards, amount, count, part = hidden.shape
    units_hidden, width = down.shape[1:]
    block = width // pieces
    unit_rows = UNIT * CAP
    in_specs = [
        pl.BlockSpec((1, count, 1), lambda e: (first + e, 0, 0)),
        pl.BlockSpec((shards, 1, count, part), lambda e: (0, e, 0, 0)),
        pl.BlockSpec((1, units_hidden, block), lambda e: (first + e, 0, at)),
        pl.BlockSpec((1, 1, block), lambda e: (first + e, 0, at)),
    ]
    operands = [share, hidden, down, scale]
    scratch = [pltpu.VMEM((count, units_hidden), bf16)]
    if last:
        operands.append(hot_t)
        in_specs.append(pl.BlockSpec(hot_t.shape, lambda e: (0, 0, 0)))
        scratch = [pltpu.VMEM((units, hot_rows, block), bf16)] + scratch
        out_shape = jax.ShapeDtypeStruct((units * unit_tokens, block), bf16)
        out_spec = pl.BlockSpec((units * unit_tokens, block), lambda e: (0, 0))
        if first:
            operands.append(earlier)
            in_specs.append(pl.BlockSpec((units, first * unit_rows, block), lambda e: (0, 0, at)))
    else:
        out_shape = jax.ShapeDtypeStruct((units, amount * unit_rows, block), bf16)
        out_spec = pl.BlockSpec((units, unit_rows, block), lambda e: (0, e, 0))
    return pl.pallas_call(
        functools.partial(combine_kernel, quantized, first, last),
        grid=(amount,),
        out_shape=out_shape,
        in_specs=in_specs,
        out_specs=out_spec,
        scratch_shapes=scratch,
        compiler_params=params(),
        cost_estimate=BRIEF,
        name="combine_quant" if quantized else "combine_float",
    )(*operands)


def to_pairs(part, groups):
    width = part.shape[1]
    low = lax.axis_index("dp") & 1
    part = part.reshape(groups // 2, 2, -1, width)
    kept = lax.dynamic_index_in_dim(part, low, 1, keepdims=False)
    sent = lax.dynamic_index_in_dim(part, 1 - low, 1, keepdims=False)
    came = lax.ppermute(sent, "dp", [(i, i ^ 1) for i in range(groups)])
    return (kept.astype(f32) + came.astype(f32)).astype(bf16)


def to_tokens(both, groups):
    pairs = groups // 2
    high = lax.axis_index("dp") >> 1
    total = lax.dynamic_index_in_dim(both, high, 0, keepdims=False).astype(f32)
    for k in range(1, pairs):
        block = lax.dynamic_index_in_dim(both, lax.rem(high + k, pairs), 0, keepdims=False)
        came = lax.ppermute(block, "dp", [(i, (i + 2 * k) % groups) for i in range(groups)])
        total = total + came.astype(f32)
    return total


def from_all(x, axis):
    copies = jnp.broadcast_to(x, (lax.axis_size(axis),) + x.shape)
    return lax.all_to_all(copies, axis, split_axis=0, concat_axis=0)


def on_device(tokens, expert_ids, route_weights, gate_weight, up_weight, down_weight):
    groups = lax.axis_size("dp")
    experts = gate_weight.shape[0]
    choices = expert_ids.shape[1]

    payload = jnp.concatenate([expert_ids.T.astype(f32), route_weights.T], axis=0)
    route = from_all(payload, "dp").reshape(-1, payload.shape[1])
    all_tokens = lax.all_gather(tokens, ("dp", "expert"), axis=0)
    all_tokens = all_tokens.reshape((groups, -1) + tokens.shape)

    local_peak = channel_peak(gate_weight, up_weight)
    weight_peak = from_all(local_peak.reshape(experts, -1).astype(bf16), "expert")
    weight_peak = jnp.max(weight_peak, axis=0).astype(f32)
    down_weight, local_peak = lax.optimization_barrier((down_weight, local_peak))
    levels, level_scale = down_quant(down_weight)

    first = (lax.axis_index("dp") * experts).astype(jnp.int32).reshape(1)
    hot, pick, share = prep(first, route, experts, groups, choices)
    hot_t = jnp.swapaxes(hot, 1, 2)
    pick, levels = lax.optimization_barrier((pick, levels))
    rows, smooth = expert_rows(pick, all_tokens, weight_peak, experts, groups)

    hf, *scales = float_hidden(rows, gate_weight, up_weight, smooth)
    scales = tuple(scales)
    wide_f = lax.all_gather(hf, "expert", axis=0)

    half = max(1, 5 * experts // 8)
    more = experts - half
    some = (3 * more) // 4
    operands = (gate_weight, up_weight, smooth, scales)
    hq = quant_hidden(rows, *operands, 0, half, half, 0)
    wide_q = [lax.all_gather(hq, "expert", axis=0)]
    wide_f, hq = lax.optimization_barrier((wide_f, hq))
    part_f = combine(hot_t, share, wide_f, down_weight, jnp.ones_like(level_scale), False)
    both_f = to_pairs(part_f, groups)
    rows, part_f = lax.optimization_barrier((rows, part_f))
    hq = quant_hidden(rows, *operands, half, some, more, 0) if some else None
    rows, both_f = lax.optimization_barrier((rows, both_f))
    out_f = to_tokens(both_f, groups)
    hq = quant_hidden(rows, *operands, half + some, more - some, more, some, hq)
    wide_q.append(lax.all_gather(hq, "expert", axis=0))
    share, hq = lax.optimization_barrier((share, hq))
    earlier = combine(hot_t, share, wide_q[0], levels, level_scale, True, last=False)
    out_q = []
    for at in range(2):
        part_q = combine(
            hot_t, share, wide_q[1], levels, level_scale, True, half, at, 2, earlier=earlier
        )
        out_q.append(to_tokens(to_pairs(part_q, groups), groups).astype(bf16))
        earlier, part_q, out_f = lax.optimization_barrier((earlier, part_q, out_f))
    return jnp.concatenate(out_q, axis=1), out_f


def solution(mesh):
    in_specs = (
        P("dp", "expert"),
        P("dp", None),
        P("dp", None),
        P("dp", "expert", None),
        P("dp", "expert", None),
        P("dp", None, "expert"),
    )
    out_specs = (P("dp", "expert"), P("dp", "expert"))
    return jax.shard_map(
        on_device, mesh=mesh, in_specs=in_specs, out_specs=out_specs, check_vma=False
    )
```
